32 devices in a mesh: ctxa: 4 (over x, core), ctxb: 8 (over z, y).
Axes of the slice: x: 2, y: 2, z: 4, core: 2. Of those that a mesh axis runs over, the one named last changes fastest.
Arguments:
- tokens: bfloat16 [16384, 2048], P(('ctxa', 'ctxb')), may hold values from -6 to 6
- cotangent: bfloat16 [16384, 2048], P(('ctxa', 'ctxb')), may hold values from -6 to 6
- w_query: bfloat16 [2048, 1024], replicated, may hold values from -0.125 to 0.125
- w_key: bfloat16 [2048, 1024], replicated, may hold values from -0.125 to 0.125
- w_value: bfloat16 [2048, 1024], replicated, may hold values from -0.125 to 0.125
- w_out: bfloat16 [1024, 2048], replicated, may hold values from -0.125 to 0.125
Outputs:
- grad_tokens: bfloat16 [16384, 2048], P(('ctxa', 'ctxb'))
The draws below stay inside these ranges and needn't reach their ends.
All inputs are finite; a program needn't handle non-finite values.
Results may differ from the reference program's by a relative error of at most 0.012.
Values may be sent and summed in bfloat16 or wider, within the bound.
No kernel may reach another device: no remote copies, remote signals or barrier semaphores. Data moves between devices by JAX's collectives and lax.ppermute only.
A program may use at most 256 MiB of HBM per device.

```python
import math
import jax
import jax.numpy as jnp
from jax import lax

D = 2048
H = 8
DH = 128
TOK_DEV = 512
SEQ = 16384


def steps_of(rng, shape, pieces, low, largest):
    gain, own = 1.0, jax.random.fold_in(rng, 6)
    for axis_at, shards_of in pieces:
        draws = jnp.exp(jax.random.uniform(jax.random.fold_in(own, axis_at), (shards_of,), jnp.float32, low / len(pieces), largest / len(pieces)))
        gain = gain * jnp.repeat(draws, shape[axis_at] // shards_of).reshape([-1 if axis == axis_at else 1 for axis in range(len(shape))])
    return gain


def gaussian(key, dims, deviation, bound, split=(), held_as=jnp.bfloat16):
    values = deviation * jax.random.normal(key, dims, jnp.float32)
    if split:
        values = values * steps_of(key, dims, split, -0.22, 0.18)
    return jnp.clip(values, -bound, bound).astype(held_as)


def setup_inputs(seed: int = 0) -> dict:
    key_list = jax.random.split(jax.random.key(seed), 7)
    return {
        "tokens": gaussian(key_list[0], (SEQ, D), 1.0, 6.0, ((0, 32),)),
        "cotangent": gaussian(key_list[1], (SEQ, D), 1.0, 6.0, ((0, 32),)),
        "w_query": gaussian(key_list[2], (D, H * DH), D ** -0.5, 0.125),
        "w_key": gaussian(key_list[3], (D, H * DH), D ** -0.5, 0.125),
        "w_value": gaussian(key_list[4], (D, H * DH), D ** -0.5, 0.125),
        "w_out": gaussian(key_list[5], (H * DH, D), D ** -0.5, 0.125),
    }


def reference(tokens, cotangent, w_query, w_key, w_value, w_out):
    factor = 1.0 / math.sqrt(DH * SEQ)
    blocks = SEQ // TOK_DEV
    query = jnp.dot(tokens, w_query, preferred_element_type=jnp.float32).astype(jnp.bfloat16)
    keys = jnp.dot(tokens, w_key, preferred_element_type=jnp.float32).astype(jnp.bfloat16)
    values = jnp.dot(tokens, w_value, preferred_element_type=jnp.float32).astype(jnp.bfloat16)
    grad_out = jnp.dot(cotangent, w_out.T, preferred_element_type=jnp.float32).astype(jnp.bfloat16)
    query4 = query.reshape(blocks, TOK_DEV, H, DH)
    keys4 = keys.reshape(blocks, TOK_DEV, H, DH)
    values4 = values.reshape(blocks, TOK_DEV, H, DH)
    grad4 = grad_out.reshape(blocks, TOK_DEV, H, DH)
    key_state = jnp.einsum('crhi,crhj->chij', keys4.astype(jnp.float32), values4.astype(jnp.float32))
    grad_state = jnp.einsum('crhi,crhj->chij', query4.astype(jnp.float32), grad4.astype(jnp.float32))
    zero_state = jnp.zeros((1, H, DH, DH), jnp.float32)
    prefix = jnp.concatenate([zero_state, jnp.cumsum(key_state, axis=0)[:-1]], axis=0)
    suffix = jnp.concatenate([jnp.cumsum(grad_state[::-1], axis=0)[:-1][::-1], zero_state], axis=0)
    prefix_bf = prefix.astype(jnp.bfloat16)
    suffix_bf = suffix.astype(jnp.bfloat16)
    index = jnp.arange(TOK_DEV)
    causal = (index[:, None] >= index[None, :])[None]

    def rounded(array):
        return lax.optimization_barrier(array.astype(jnp.bfloat16)).astype(jnp.float32)

    def one_block(items):
        q_block, k_block, v_block, o_block, before, after = items
        q_f = q_block.astype(jnp.float32)
        k_f = k_block.astype(jnp.float32)
        v_f = v_block.astype(jnp.float32)
        o_f = o_block.astype(jnp.float32)
        b_f = before.astype(jnp.float32)
        a_f = after.astype(jnp.float32)
        attend = rounded(jnp.where(causal, jnp.einsum('thi,shi->hts', q_f, k_f), 0.0))
        probe = rounded(jnp.where(causal, jnp.einsum('thj,shj->hts', o_f, v_f), 0.0))
        grad_query = jnp.einsum('hts,shi->thi', probe, k_f) + jnp.einsum('thj,hij->thi', o_f, b_f)
        grad_key = jnp.einsum('hts,thi->shi', probe, q_f) + jnp.einsum('shj,hij->shi', v_f, a_f)
        grad_value = jnp.einsum('hts,thj->shj', attend, o_f) + jnp.einsum('shi,hij->shj', k_f, a_f)
        return ((factor * grad_query).astype(jnp.bfloat16).reshape(TOK_DEV, H * DH), (factor * grad_key).astype(jnp.bfloat16).reshape(TOK_DEV, H * DH), (factor * grad_value).astype(jnp.bfloat16).reshape(TOK_DEV, H * DH))
    grad_query, grad_key, grad_value = lax.map(one_block, (query4, keys4, values4, grad4, prefix_bf, suffix_bf))
    grad_query = grad_query.reshape(SEQ, H * DH)
    grad_key = grad_key.reshape(SEQ, H * DH)
    grad_value = grad_value.reshape(SEQ, H * DH)
    total = jnp.dot(grad_query, w_query.T, preferred_element_type=jnp.float32)
    total = total + jnp.dot(grad_key, w_key.T, preferred_element_type=jnp.float32)
    total = total + jnp.dot(grad_value, w_value.T, preferred_element_type=jnp.float32)
    return total.astype(jnp.bfloat16)
```

```python
import math

import jax
import jax.numpy as jnp
from jax import lax
from jax.sharding import PartitionSpec as P

DH = 128
AXES = ("ctxa", "ctxb")


def exclusive_scan(state, backward):
    heads, wide, _ = state.shape
    count = lax.axis_size(AXES)
    slices = state.astype(jnp.bfloat16).reshape(count, heads * wide // count, wide)
    slices = lax.all_to_all(slices, AXES, 0, 0, tiled=True)
    total = jnp.zeros(slices.shape[1:], jnp.float32)
    sums = [None] * count
    for lap in range(count):
        place = count - 1 - lap if backward else lap
        sums[place] = total.astype(jnp.bfloat16)
        total = total + slices[place].astype(jnp.float32)
    sums = lax.all_to_all(jnp.stack(sums), AXES, 0, 0, tiled=True)
    return sums.reshape(heads, wide, wide)


def project(left, weight):
    return jnp.dot(left, weight, preferred_element_type=jnp.float32).astype(jnp.bfloat16)


def shards(tokens, cotangent, w_query, w_key, w_value, w_out):
    rows = tokens.shape[0]
    heads = w_query.shape[1] // DH
    factor = 1.0 / math.sqrt(DH * rows * lax.axis_size(AXES))
    query = project(tokens, w_query).reshape(rows, heads, DH)
    grad_out = lax.dot_general(
        cotangent, w_out, (((1,), (1,)), ((), ())), preferred_element_type=jnp.float32
    )
    grad_out = grad_out.astype(jnp.bfloat16).reshape(rows, heads, DH)
    grad_state = jnp.einsum("rhi,rhj->hij", query, grad_out, preferred_element_type=jnp.float32)
    later = exclusive_scan(grad_state, True)
    keys = project(tokens, w_key).reshape(rows, heads, DH)
    values = project(tokens, w_value).reshape(rows, heads, DH)
    key_state = jnp.einsum("rhi,rhj->hij", keys, values, preferred_element_type=jnp.float32)
    prior = exclusive_scan(key_state, False)
    index = jnp.arange(rows)
    causal = (index[:, None] >= index[None, :])[None]
    attend = jnp.where(
        causal, jnp.einsum("thi,shi->hts", query, keys, preferred_element_type=jnp.float32), 0.0
    ).astype(jnp.bfloat16)
    probe = jnp.where(
        causal,
        jnp.einsum("thj,shj->hts", grad_out, values, preferred_element_type=jnp.float32),
        0.0,
    ).astype(jnp.bfloat16)
    grad_query = jnp.einsum("hts,shi->thi", probe, keys, preferred_element_type=jnp.float32)
    grad_query = grad_query + jnp.einsum(
        "thj,hij->thi", grad_out, prior, preferred_element_type=jnp.float32
    )
    grad_key = jnp.einsum("hts,thi->shi", probe, query, preferred_element_type=jnp.float32)
    grad_key = grad_key + jnp.einsum(
        "shj,hij->shi", values, later, preferred_element_type=jnp.float32
    )
    grad_value = jnp.einsum("hts,thj->shj", attend, grad_out, preferred_element_type=jnp.float32)
    grad_value = grad_value + jnp.einsum(
        "shi,hij->shj", keys, later, preferred_element_type=jnp.float32
    )

    def finish(partial_grad):
        return (factor * partial_grad).astype(jnp.bfloat16).reshape(rows, heads * DH)

    total = jnp.dot(finish(grad_key), w_key.T, preferred_element_type=jnp.float32)
    total = total + jnp.dot(finish(grad_value), w_value.T, preferred_element_type=jnp.float32)
    total = total + jnp.dot(finish(grad_query), w_query.T, preferred_element_type=jnp.float32)
    return total.astype(jnp.bfloat16)


def solution(mesh):
    placed = (P(AXES, None), P(AXES, None), P(), P(), P(), P())
    return jax.shard_map(
        shards, mesh=mesh, in_specs=placed, out_specs=P(AXES, None), check_vma=False
    )
```

```python
import functools
import math

import jax
import jax.numpy as jnp
from jax import lax
from jax.experimental import pallas as pl
from jax.experimental.pallas import tpu as pltpu
from jax.sharding import PartitionSpec as P

DH = 128
AXES = ("ctxa", "ctxb")


def scan_kernel(backward, slices_ref, sums_ref):
    count = slices_ref.shape[0]

    def one(lap, total):
        place = count - 1 - lap if backward else lap
        sums_ref[place] = total.astype(jnp.bfloat16)
        return total + slices_ref[place].astype(jnp.float32)

    lax.fori_loop(0, count, one, jnp.zeros(slices_ref.shape[1:], jnp.float32), unroll=4)


def exclusive_scan(state, backward):
    heads, wide, _ = state.shape
    count = lax.axis_size(AXES)
    slices = state.astype(jnp.bfloat16).reshape(count, heads * wide // count, wide)
    slices = lax.all_to_all(slices, AXES, 0, 0, tiled=True)
    sums = pl.pallas_call(
        functools.partial(scan_kernel, backward),
        out_shape=jax.ShapeDtypeStruct(slices.shape, jnp.bfloat16),
        name="scan_later" if backward else "scan_earlier",
    )(slices)
    sums = lax.all_to_all(sums, AXES, 0, 0, tiled=True)
    return sums.reshape(heads, wide, wide)


def project(left, weight):
    return jnp.dot(left, weight, preferred_element_type=jnp.float32).astype(jnp.bfloat16)


def shards(tokens, cotangent, w_query, w_key, w_value, w_out):
    rows = tokens.shape[0]
    heads = w_query.shape[1] // DH
    factor = 1.0 / math.sqrt(DH * rows * lax.axis_size(AXES))
    query = project(tokens, w_query).reshape(rows, heads, DH)
    grad_out = lax.dot_general(
        cotangent, w_out, (((1,), (1,)), ((), ())), preferred_element_type=jnp.float32
    )
    grad_out = grad_out.astype(jnp.bfloat16).reshape(rows, heads, DH)
    grad_state = jnp.einsum("rhi,rhj->hij", query, grad_out, preferred_element_type=jnp.float32)
    later = exclusive_scan(grad_state, True)
    keys = project(tokens, w_key).reshape(rows, heads, DH)
    values = project(tokens, w_value).reshape(rows, heads, DH)
    key_state = jnp.einsum("rhi,rhj->hij", keys, values, preferred_element_type=jnp.float32)
    prior = exclusive_scan(key_state, False)
    index = jnp.arange(rows)
    causal = (index[:, None] >= index[None, :])[None]
    attend = jnp.where(
        causal, jnp.einsum("thi,shi->hts", query, keys, preferred_element_type=jnp.float32), 0.0
    ).astype(jnp.bfloat16)
    probe = jnp.where(
        causal,
        jnp.einsum("thj,shj->hts", grad_out, values, preferred_element_type=jnp.float32),
        0.0,
    ).astype(jnp.bfloat16)
    grad_query = jnp.einsum("hts,shi->thi", probe, keys, preferred_element_type=jnp.float32)
    grad_query = grad_query + jnp.einsum(
        "thj,hij->thi", grad_out, prior, preferred_element_type=jnp.float32
    )
    grad_key = jnp.einsum("hts,thi->shi", probe, query, preferred_element_type=jnp.float32)
    grad_key = grad_key + jnp.einsum(
        "shj,hij->shi", values, later, preferred_element_type=jnp.float32
    )
    grad_value = jnp.einsum("hts,thj->shj", attend, grad_out, preferred_element_type=jnp.float32)
    grad_value = grad_value + jnp.einsum(
        "shi,hij->shj", keys, later, preferred_element_type=jnp.float32
    )

    def finish(partial_grad):
        return (factor * partial_grad).astype(jnp.bfloat16).reshape(rows, heads * DH)

    total = jnp.dot(finish(grad_key), w_key.T, preferred_element_type=jnp.float32)
    total = total + jnp.dot(finish(grad_value), w_value.T, preferred_element_type=jnp.float32)
    total = total + jnp.dot(finish(grad_query), w_query.T, preferred_element_type=jnp.float32)
    return total.astype(jnp.bfloat16)


def solution(mesh):
    placed = (P(AXES, None), P(AXES, None), P(), P(), P(), P())
    return jax.shard_map(
        shards, mesh=mesh, in_specs=placed, out_specs=P(AXES, None), check_vma=False
    )
```

```python
import functools
import math

import jax
import jax.numpy as jnp
from jax import lax
from jax.experimental import pallas as pl
from jax.experimental.pallas import tpu as pltpu
from jax.sharding import PartitionSpec as P

DH = 128
PAIR = 2 * DH
AXES = ("ctxa", "ctxb")
ROWS_ROWS = (((0,), (0,)), ((), ()))
LAST_LAST = (((1,), (1,)), ((), ()))
PLAIN = (((1,), (0,)), ((), ()))


def mul(left, right, dims=PLAIN):
    return lax.dot_general(left, right, dims, preferred_element_type=jnp.float32)


def params(mebibytes):
    return pltpu.CompilerParams(vmem_limit_bytes=mebibytes << 20)


def scan_kernel(backward, slices_ref, sums_ref):
    count = slices_ref.shape[0]

    def one(lap, total):
        place = count - 1 - lap if backward else lap
        sums_ref[place] = total.astype(jnp.bfloat16)
        return total + slices_ref[place].astype(jnp.float32)

    lax.fori_loop(0, count, one, jnp.zeros(slices_ref.shape[1:], jnp.float32), unroll=4)


def exclusive_scan(state, backward):
    heads, wide, _ = state.shape
    count = lax.axis_size(AXES)
    slices = state.reshape(count, heads * wide // count, wide)
    slices = lax.all_to_all(slices, AXES, 0, 0, tiled=True)
    sums = pl.pallas_call(
        functools.partial(scan_kernel, backward),
        out_shape=jax.ShapeDtypeStruct(slices.shape, jnp.bfloat16),
        name="scan_later" if backward else "scan_earlier",
    )(slices)
    sums = lax.all_to_all(sums, AXES, 0, 0, tiled=True)
    return sums.reshape(heads, wide, wide)


def state_of(first, second, state_ref):
    both = mul(first, second, ROWS_ROWS).astype(jnp.bfloat16)
    state_ref[0] = both[:DH, :DH]
    state_ref[1] = both[DH:, DH:]


def query_kernel(tokens_ref, w_query_ref, cotangent_ref, w_out_ref, query_ref, grad_out_ref, state_ref):
    query = mul(tokens_ref[...], w_query_ref[...]).astype(jnp.bfloat16)
    query_ref[...] = query
    grad_out = mul(cotangent_ref[...], w_out_ref[...], LAST_LAST).astype(jnp.bfloat16)
    grad_out_ref[...] = grad_out
    state_of(query, grad_out, state_ref)


def key_kernel(tokens_ref, w_key_ref, w_value_ref, keys_ref, values_ref, state_ref):
    keys = mul(tokens_ref[...], w_key_ref[...]).astype(jnp.bfloat16)
    keys_ref[...] = keys
    values = mul(tokens_ref[...], w_value_ref[...]).astype(jnp.bfloat16)
    values_ref[...] = values
    state_of(keys, values, state_ref)


def intra_kernel(query_ref, keys_ref, values_ref, grad_out_ref, grad_query_ref, grad_key_ref, grad_value_ref):
    rows = query_ref.shape[0]
    step = min(rows, 256)
    down = lax.broadcasted_iota(jnp.int32, (step, step), 0)
    across = lax.broadcasted_iota(jnp.int32, (step, step), 1)

    def product(left, right, masked):
        found = mul(left, right, LAST_LAST)
        return (found if masked is None else jnp.where(masked, found, 0.0)).astype(jnp.bfloat16)

    for head in range(query_ref.shape[1] // DH):
        lanes = pl.ds(head * DH, DH)
        for block in range(rows // step):
            mine = pl.ds(block * step, step)
            total = None
            for other in range(block + 1):
                theirs = pl.ds(other * step, step)
                probe = product(
                    grad_out_ref[mine, lanes], values_ref[theirs, lanes], down >= across if other == block else None
                )
                term = mul(probe, keys_ref[theirs, lanes])
                total = term if total is None else total + term
            grad_query_ref[mine, lanes] = total.astype(jnp.bfloat16)
            total_key, total_value = None, None
            for other in range(block, rows // step):
                theirs = pl.ds(other * step, step)
                masked = across >= down if other == block else None
                probe = product(values_ref[mine, lanes], grad_out_ref[theirs, lanes], masked)
                attend = product(keys_ref[mine, lanes], query_ref[theirs, lanes], masked)
                term_key = mul(probe, query_ref[theirs, lanes])
                term_value = mul(attend, grad_out_ref[theirs, lanes])
                total_key = term_key if total_key is None else total_key + term_key
                total_value = term_value if total_value is None else total_value + term_value
            grad_key_ref[mine, lanes] = total_key.astype(jnp.bfloat16)
            grad_value_ref[mine, lanes] = total_value.astype(jnp.bfloat16)


def finish_kernel(
    factor, pairs,
    intra_query_ref, intra_key_ref, intra_value_ref, keys_ref, values_ref, grad_out_ref, prior_ref, later_ref,
    w_query_ref, w_key_ref, w_value_ref, out_ref, grads_ref,
):
    at = pl.program_id(0)

    @pl.when(at < pairs)
    def _():
        for head in range(2):
            lanes = pl.ds(head * DH, DH)
            prior, later = prior_ref[head], later_ref[head]
            grad_query = mul(grad_out_ref[:, lanes], prior, LAST_LAST)
            grad_key = mul(values_ref[:, lanes], later, LAST_LAST)
            grad_value = mul(keys_ref[:, lanes], later)
            for kind, (inter, intra_ref) in enumerate(
                ((grad_query, intra_query_ref), (grad_key, intra_key_ref), (grad_value, intra_value_ref))
            ):
                total = factor * (inter + intra_ref[:, lanes].astype(jnp.float32))
                grads_ref[kind, at, :, lanes] = total.astype(jnp.bfloat16)

    @pl.when(at >= pairs)
    def _():
        total = None
        for kind, weight_ref in enumerate((w_query_ref, w_key_ref, w_value_ref)):
            for pair in range(pairs):
                term = mul(grads_ref[kind, pair], weight_ref[:, pl.ds(pair * PAIR, PAIR)], LAST_LAST)
                total = term if total is None else total + term
        out_ref[...] = total.astype(jnp.bfloat16)


def shards(tokens, cotangent, w_query, w_key, w_value, w_out):
    rows, wide = tokens.shape
    columns = w_query.shape[1]
    heads = columns // DH
    pairs = heads // 2
    factor = 1.0 / math.sqrt(DH * rows * lax.axis_size(AXES))
    whole = pl.BlockSpec((rows, wide), lambda i: (0, 0))
    into = pl.BlockSpec((wide, PAIR), lambda i: (0, i))
    outof = pl.BlockSpec((PAIR, wide), lambda i: (i, 0))
    part = pl.BlockSpec((rows, PAIR), lambda i: (0, i))
    states = pl.BlockSpec((2, DH, DH), lambda i: (i, 0, 0))
    columns_shape = jax.ShapeDtypeStruct((rows, columns), jnp.bfloat16)
    state_shape = jax.ShapeDtypeStruct((heads, DH, DH), jnp.bfloat16)

    def cost(flops, bytes_accessed):
        return pl.CostEstimate(flops=flops, bytes_accessed=bytes_accessed, transcendentals=0)

    project_flops = 4 * rows * wide * columns + 2 * rows * columns * PAIR
    query, grad_out, grad_state = pl.pallas_call(
        query_kernel,
        grid=(pairs,),
        in_specs=[whole, into, whole, outof],
        out_specs=[part, part, states],
        out_shape=[columns_shape, columns_shape, state_shape],
        compiler_params=params(24),
        cost_estimate=cost(project_flops, 4 * (rows + columns) * wide + 4 * rows * columns),
        name="query_grad_out",
    )(tokens, w_query, cotangent, w_out)
    later = exclusive_scan(grad_state, True)
    keys, values, key_state = pl.pallas_call(
        key_kernel,
        grid=(pairs,),
        in_specs=[whole, into, into],
        out_specs=[part, part, states],
        out_shape=[columns_shape, columns_shape, state_shape],
        compiler_params=params(24),
        cost_estimate=cost(project_flops, 2 * (rows + 2 * columns) * wide + 4 * rows * columns),
        name="keys_values",
    )(tokens, w_key, w_value)
    prior = exclusive_scan(key_state, False)
    intra_query, intra_key, intra_value = pl.pallas_call(
        intra_kernel,
        grid=(pairs,),
        in_specs=[part] * 4,
        out_specs=[part] * 3,
        out_shape=[columns_shape] * 3,
        compiler_params=params(24),
        cost_estimate=cost(12 * rows * rows * columns, 14 * rows * columns),
        name="intra",
    )(query, keys, values, grad_out)

    held = pl.BlockSpec((rows, PAIR), lambda i: (0, jnp.minimum(i, pairs - 1)))
    held_states = pl.BlockSpec((2, DH, DH), lambda i: (jnp.minimum(i, pairs - 1), 0, 0))
    block = min(256, wide)
    back = pl.BlockSpec((block, columns), lambda i: (jnp.maximum(i - pairs, 0), 0))
    return pl.pallas_call(
        functools.partial(finish_kernel, factor, pairs),
        grid=(pairs + wide // block,),
        in_specs=[held] * 6 + [held_states] * 2 + [back] * 3,
        out_specs=pl.BlockSpec((rows, block), lambda i: (0, jnp.maximum(i - pairs, 0))),
        out_shape=jax.ShapeDtypeStruct((rows, wide), jnp.bfloat16),
        scratch_shapes=[pltpu.VMEM((3, pairs, rows, PAIR), jnp.bfloat16)],
        compiler_params=params(24),
        cost_estimate=cost(6 * rows * columns * (wide + DH), 2 * (6 * rows * columns + 3 * wide * columns)),
        name="finish",
    )(intra_query, intra_key, intra_value, keys, values, grad_out, prior, later, w_query, w_key, w_value)


def solution(mesh):
    placed = (P(AXES, None), P(AXES, None), P(), P(), P(), P())
    return jax.shard_map(
        shards, mesh=mesh, in_specs=placed, out_specs=P(AXES, None), check_vma=False
    )
```

```python
import functools
import math

import jax
import jax.numpy as jnp
from jax import lax
from jax.experimental import pallas as pl
from jax.experimental.pallas import tpu as pltpu
from jax.sharding import PartitionSpec as P

DH = 128
PAIR = 2 * DH
AXES = ("ctxa", "ctxb")
ROWS_ROWS = (((0,), (0,)), ((), ()))
LAST_LAST = (((1,), (1,)), ((), ()))
PLAIN = (((1,), (0,)), ((), ()))


def mul(left, right, dims=PLAIN):
    return lax.dot_general(left, right, dims, preferred_element_type=jnp.float32)


def params(mebibytes):
    return pltpu.CompilerParams(vmem_limit_bytes=mebibytes << 20)


def group_kernel(slices_ref, sum_ref):
    total = jnp.sum(slices_ref[...].astype(jnp.float32), axis=0).astype(jnp.bfloat16)
    for group in range(sum_ref.shape[0]):
        sum_ref[group] = total


def scan_kernel(backward, groups_ref, slices_ref, sums_ref):
    count = slices_ref.shape[0]
    mine = lax.axis_index("ctxa")
    total = jnp.zeros(slices_ref.shape[1:], jnp.float32)
    for group in range(groups_ref.shape[0]):
        ahead = group > mine if backward else group < mine
        total = total + jnp.where(ahead, groups_ref[group].astype(jnp.float32), 0.0)
    for lap in range(count):
        place = count - 1 - lap if backward else lap
        sums_ref[place] = total.astype(jnp.bfloat16)
        if lap < count - 1:
            total = total + slices_ref[place].astype(jnp.float32)


def exclusive_scan(state, backward):
    heads, wide, _ = state.shape
    groups, count = lax.axis_size("ctxa"), lax.axis_size("ctxb")
    kind = "later" if backward else "earlier"
    slices = state.reshape(count, heads * wide // count, wide)
    slices = lax.all_to_all(slices, "ctxb", 0, 0, tiled=True)
    totals = pl.pallas_call(
        group_kernel,
        out_shape=jax.ShapeDtypeStruct((groups,) + slices.shape[1:], jnp.bfloat16),
        compiler_params=params(60),
        name="group_" + kind,
    )(slices)
    totals = lax.all_to_all(totals, "ctxa", 0, 0, tiled=True)
    sums = pl.pallas_call(
        functools.partial(scan_kernel, backward),
        out_shape=jax.ShapeDtypeStruct(slices.shape, jnp.bfloat16),
        compiler_params=params(60),
        name="scan_" + kind,
    )(totals, slices)
    sums = lax.all_to_all(sums, "ctxb", 0, 0, tiled=True)
    return sums.reshape(heads, wide, wide)


def state_of(first, second, state_ref):
    both = mul(first, second, ROWS_ROWS).astype(jnp.bfloat16)
    state_ref[0] = both[:DH, :DH]
    state_ref[1] = both[DH:, DH:]


def query_kernel(tokens_ref, w_query_ref, cotangent_ref, w_out_ref, query_ref, grad_out_ref, state_ref):
    query = mul(tokens_ref[...], w_query_ref[...]).astype(jnp.bfloat16)
    query_ref[...] = query
    grad_out = mul(cotangent_ref[...], w_out_ref[...], LAST_LAST).astype(jnp.bfloat16)
    grad_out_ref[...] = grad_out
    state_of(query, grad_out, state_ref)


def key_kernel(tokens_ref, w_key_ref, w_value_ref, keys_ref, values_ref, state_ref):
    keys = mul(tokens_ref[...], w_key_ref[...]).astype(jnp.bfloat16)
    keys_ref[...] = keys
    values = mul(tokens_ref[...], w_value_ref[...]).astype(jnp.bfloat16)
    values_ref[...] = values
    state_of(keys, values, state_ref)


def intra_kernel(query_ref, keys_ref, values_ref, grad_out_ref, grad_query_ref, grad_key_ref, grad_value_ref):
    rows = query_ref.shape[0]
    step = min(rows, 256)
    down = lax.broadcasted_iota(jnp.int32, (step, step), 0)
    across = lax.broadcasted_iota(jnp.int32, (step, step), 1)

    def product(left, right, masked):
        found = mul(left, right, LAST_LAST)
        return (found if masked is None else jnp.where(masked, found, 0.0)).astype(jnp.bfloat16)

    for head in range(query_ref.shape[1] // DH):
        lanes = pl.ds(head * DH, DH)
        for block in range(rows // step):
            mine = pl.ds(block * step, step)
            total = None
            for other in range(block + 1):
                theirs = pl.ds(other * step, step)
                probe = product(
                    grad_out_ref[mine, lanes], values_ref[theirs, lanes], down >= across if other == block else None
                )
                term = mul(probe, keys_ref[theirs, lanes])
                total = term if total is None else total + term
            grad_query_ref[mine, lanes] = total.astype(jnp.bfloat16)
            total_key, total_value = None, None
            for other in range(block, rows // step):
                theirs = pl.ds(other * step, step)
                masked = across >= down if other == block else None
                probe = product(values_ref[mine, lanes], grad_out_ref[theirs, lanes], masked)
                attend = product(keys_ref[mine, lanes], query_ref[theirs, lanes], masked)
                term_key = mul(probe, query_ref[theirs, lanes])
                term_value = mul(attend, grad_out_ref[theirs, lanes])
                total_key = term_key if total_key is None else total_key + term_key
                total_value = term_value if total_value is None else total_value + term_value
            grad_key_ref[mine, lanes] = total_key.astype(jnp.bfloat16)
            grad_value_ref[mine, lanes] = total_value.astype(jnp.bfloat16)


def finish_kernel(
    factor, pairs,
    intra_query_ref, intra_key_ref, intra_value_ref, keys_ref, values_ref, grad_out_ref, prior_ref, later_ref,
    w_query_ref, w_key_ref, w_value_ref, out_ref, grads_ref,
):
    at = pl.program_id(0)

    @pl.when(at < pairs)
    def _():
        for head in range(2):
            lanes = pl.ds(head * DH, DH)
            prior, later = prior_ref[head], later_ref[head]
            grad_query = mul(grad_out_ref[:, lanes], prior, LAST_LAST)
            grad_key = mul(values_ref[:, lanes], later, LAST_LAST)
            grad_value = mul(keys_ref[:, lanes], later)
            for kind, (inter, intra_ref) in enumerate(
                ((grad_query, intra_query_ref), (grad_key, intra_key_ref), (grad_value, intra_value_ref))
            ):
                total = factor * (inter + intra_ref[:, lanes].astype(jnp.float32))
                grads_ref[kind, at, :, lanes] = total.astype(jnp.bfloat16)

    @pl.when(at >= pairs)
    def _():
        total = None
        for kind, weight_ref in enumerate((w_query_ref, w_key_ref, w_value_ref)):
            for pair in range(pairs):
                term = mul(grads_ref[kind, pair], weight_ref[:, pl.ds(pair * PAIR, PAIR)], LAST_LAST)
                total = term if total is None else total + term
        out_ref[...] = total.astype(jnp.bfloat16)


def shards(tokens, cotangent, w_query, w_key, w_value, w_out):
    rows, wide = tokens.shape
    columns = w_query.shape[1]
    heads = columns // DH
    pairs = heads // 2
    factor = 1.0 / math.sqrt(DH * rows * lax.axis_size(AXES))
    whole = pl.BlockSpec((rows, wide), lambda i: (0, 0))
    into = pl.BlockSpec((wide, PAIR), lambda i: (0, i))
    outof = pl.BlockSpec((PAIR, wide), lambda i: (i, 0))
    part = pl.BlockSpec((rows, PAIR), lambda i: (0, i))
    states = pl.BlockSpec((2, DH, DH), lambda i: (i, 0, 0))
    columns_shape = jax.ShapeDtypeStruct((rows, columns), jnp.bfloat16)
    state_shape = jax.ShapeDtypeStruct((heads, DH, DH), jnp.bfloat16)

    def cost(flops, bytes_accessed):
        return pl.CostEstimate(flops=flops, bytes_accessed=bytes_accessed, transcendentals=0)

    project_flops = 4 * rows * wide * columns + 2 * rows * columns * PAIR
    query, grad_out, grad_state = pl.pallas_call(
        query_kernel,
        grid=(pairs,),
        in_specs=[whole, into, whole, outof],
        out_specs=[part, part, states],
        out_shape=[columns_shape, columns_shape, state_shape],
        compiler_params=params(60),
        cost_estimate=cost(project_flops, 4 * (rows + columns) * wide + 4 * rows * columns),
        name="query_grad_out",
    )(tokens, w_query, cotangent, w_out)
    later = exclusive_scan(grad_state, True)
    keys, values, key_state = pl.pallas_call(
        key_kernel,
        grid=(pairs,),
        in_specs=[whole, into, into],
        out_specs=[part, part, states],
        out_shape=[columns_shape, columns_shape, state_shape],
        compiler_params=params(60),
        cost_estimate=cost(project_flops, 2 * (rows + 2 * columns) * wide + 4 * rows * columns),
        name="keys_values",
    )(tokens, w_key, w_value)
    prior = exclusive_scan(key_state, False)
    intra_query, intra_key, intra_value = pl.pallas_call(
        intra_kernel,
        grid=(pairs,),
        in_specs=[part] * 4,
        out_specs=[part] * 3,
        out_shape=[columns_shape] * 3,
        compiler_params=params(60),
        cost_estimate=cost(12 * rows * rows * columns, 14 * rows * columns),
        name="intra",
    )(query, keys, values, grad_out)

    held = pl.BlockSpec((rows, PAIR), lambda i: (0, jnp.minimum(i, pairs - 1)))
    held_states = pl.BlockSpec((2, DH, DH), lambda i: (jnp.minimum(i, pairs - 1), 0, 0))
    block = min(256, wide)
    back = pl.BlockSpec((block, columns), lambda i: (jnp.maximum(i - pairs, 0), 0))
    return pl.pallas_call(
        functools.partial(finish_kernel, factor, pairs),
        grid=(pairs + wide // block,),
        in_specs=[held] * 6 + [held_states] * 2 + [back] * 3,
        out_specs=pl.BlockSpec((rows, block), lambda i: (0, jnp.maximum(i - pairs, 0))),
        out_shape=jax.ShapeDtypeStruct((rows, wide), jnp.bfloat16),
        scratch_shapes=[pltpu.VMEM((3, pairs, rows, PAIR), jnp.bfloat16)],
        compiler_params=params(60),
        cost_estimate=cost(6 * rows * columns * (wide + DH), 2 * (6 * rows * columns + 3 * wide * columns)),
        name="finish",
    )(intra_query, intra_key, intra_value, keys, values, grad_out, prior, later, w_query, w_key, w_value)


def solution(mesh):
    placed = (P(AXES, None), P(AXES, None), P(), P(), P(), P())
    return jax.shard_map(
        shards, mesh=mesh, in_specs=placed, out_specs=P(AXES, None), check_vma=False
    )
```

```python
import functools
import math

import jax
import jax.numpy as jnp
from jax import lax
from jax.experimental import pallas as pl
from jax.experimental.pallas import tpu as pltpu
from jax.sharding import PartitionSpec as P

DH = 128
PAIR = 2 * DH
AXES = ("ctxa", "ctxb")
ROWS_ROWS = (((0,), (0,)), ((), ()))
LAST_LAST = (((1,), (1,)), ((), ()))
PLAIN = (((1,), (0,)), ((), ()))


def mul(left, right, dims=PLAIN):
    return lax.dot_general(left, right, dims, preferred_element_type=jnp.float32)


def params(mebibytes):
    return pltpu.CompilerParams(vmem_limit_bytes=mebibytes << 20)


def scan_kernel(backward, slices_ref, sums_ref):
    count = slices_ref.shape[0]

    def one(lap, total):
        place = count - 1 - lap if backward else lap
        sums_ref[place] = total.astype(jnp.bfloat16)
        return total + slices_ref[place].astype(jnp.float32)

    lax.fori_loop(0, count, one, jnp.zeros(slices_ref.shape[1:], jnp.float32), unroll=4)


def exclusive_scan(state, backward):
    heads, wide, _ = state.shape
    count = lax.axis_size(AXES)
    slices = state.reshape(count, heads * wide // count, wide)
    slices = lax.all_to_all(slices, AXES, 0, 0, tiled=True)
    sums = pl.pallas_call(
        functools.partial(scan_kernel, backward),
        out_shape=jax.ShapeDtypeStruct(slices.shape, jnp.bfloat16),
        compiler_params=params(60),
        name="scan_later" if backward else "scan_earlier",
    )(slices)
    sums = lax.all_to_all(sums, AXES, 0, 0, tiled=True)
    return sums.reshape(heads, wide, wide)


def arrive(source, target, sem):
    copy = pltpu.make_async_copy(source, target, sem)
    copy.start()
    return copy


def halves(extent):
    return [pl.ds(half * (extent // 2), extent // 2) for half in range(2)]


def project(left_ref, right_ref, copies, wide, transposed):
    total = None
    for lanes, waits in zip(halves(wide), copies):
        for copy in waits:
            copy.wait()
        if transposed:
            term = mul(left_ref[:, lanes], right_ref[:, lanes], LAST_LAST)
        else:
            term = mul(left_ref[:, lanes], right_ref[lanes, :])
        total = term if total is None else total + term
    return total.astype(jnp.bfloat16)


def state_kernel(
    first_hbm, w_first_hbm, second_hbm, w_second_hbm, first_out, second_out, state_ref,
    first_left, first_right, second_left, second_right, first, second, in_sem, out_sem,
    *, transposed, shared,
):
    wide = first_hbm.shape[1]
    parts = halves(wide)
    first_copies, second_copies = [], []
    sem = 0
    for lanes in parts:
        first_copies.append([
            arrive(first_hbm.at[:, lanes], first_left.at[:, lanes], in_sem.at[sem]),
            arrive(
                w_first_hbm.at[:, lanes] if transposed else w_first_hbm.at[lanes],
                first_right.at[:, lanes] if transposed else first_right.at[lanes],
                in_sem.at[sem + 1],
            ),
        ])
        sem += 2
    for lanes in parts:
        here = []
        if not shared:
            here.append(arrive(second_hbm.at[:, lanes], second_left.at[:, lanes], in_sem.at[sem]))
        here.append(arrive(w_second_hbm.at[lanes], second_right.at[lanes], in_sem.at[sem + 1]))
        second_copies.append(here)
        sem += 2
    first[...] = project(first_left, first_right, first_copies, wide, transposed)
    first_done = arrive(first, first_out, out_sem.at[0])
    second[...] = project(first_left if shared else second_left, second_right, second_copies, wide, False)
    second_done = arrive(second, second_out, out_sem.at[1])
    for head in range(state_ref.shape[0]):
        lanes = pl.ds(head * DH, DH)
        left, right = (first, second) if shared else (second, first)
        state_ref[head] = mul(left[:, lanes], right[:, lanes], ROWS_ROWS).astype(jnp.bfloat16)
    first_done.wait()
    second_done.wait()


def states_call(name, first, w_first, second, w_second, transposed, shared):
    rows, wide = first.shape
    columns = w_second.shape[1]
    heads = columns // DH
    left = pltpu.VMEM((rows, wide), jnp.bfloat16)
    out = jax.ShapeDtypeStruct((rows, columns), jnp.bfloat16)
    small = pltpu.VMEM((16, 128), jnp.bfloat16)
    anywhere = pl.BlockSpec(memory_space=pl.ANY)
    return pl.pallas_call(
        functools.partial(state_kernel, transposed=transposed, shared=shared),
        in_specs=[anywhere] * 4,
        out_specs=[anywhere, anywhere, pl.BlockSpec(memory_space=pltpu.VMEM)],
        out_shape=[out, out, jax.ShapeDtypeStruct((heads, DH, DH), jnp.bfloat16)],
        scratch_shapes=[
            left, pltpu.VMEM(w_first.shape, jnp.bfloat16),
            small if shared else left, pltpu.VMEM(w_second.shape, jnp.bfloat16),
            pltpu.VMEM((rows, columns), jnp.bfloat16), pltpu.VMEM((rows, columns), jnp.bfloat16),
            pltpu.SemaphoreType.DMA((8,)), pltpu.SemaphoreType.DMA((2,)),
        ],
        compiler_params=params(60),
        cost_estimate=pl.CostEstimate(
            flops=4 * rows * wide * columns, bytes_accessed=4 * (rows + columns) * wide, transcendentals=0
        ),
        name=name,
    )(first, w_first, second, w_second)


def intra_kernel(query_ref, keys_ref, values_ref, grad_out_ref, grad_query_ref, grad_key_ref, grad_value_ref):
    rows = query_ref.shape[0]
    step = min(rows, 256)
    blocks = [pl.ds(at * step, step) for at in range(rows // step)]
    below = lax.broadcasted_iota(jnp.int32, (step, step), 0) >= lax.broadcasted_iota(jnp.int32, (step, step), 1)

    def score(left, right, masked):
        found = mul(left, right, LAST_LAST)
        return (jnp.where(below, found, 0.0) if masked else found).astype(jnp.bfloat16)

    for head in range(query_ref.shape[1] // DH):
        lanes = pl.ds(head * DH, DH)
        query_t = query_ref[:, lanes].T
        grad_out_t = grad_out_ref[:, lanes].T
        key_sums, value_sums = [None] * len(blocks), [None] * len(blocks)
        for t, mine in enumerate(blocks):
            span = slice(t * step, (t + 1) * step)
            query_sum = None
            for s, theirs in enumerate(blocks[: t + 1]):
                probe = score(grad_out_ref[mine, lanes], values_ref[theirs, lanes], s == t)
                attend = score(query_ref[mine, lanes], keys_ref[theirs, lanes], s == t)
                term = mul(probe, keys_ref[theirs, lanes])
                query_sum = term if query_sum is None else query_sum + term
                term = mul(query_t[:, span], probe)
                key_sums[s] = term if key_sums[s] is None else key_sums[s] + term
                term = mul(grad_out_t[:, span], attend)
                value_sums[s] = term if value_sums[s] is None else value_sums[s] + term
            grad_query_ref[mine, lanes] = query_sum.astype(jnp.bfloat16)
        for s, theirs in enumerate(blocks):
            grad_key_ref[theirs, lanes] = key_sums[s].T.astype(jnp.bfloat16)
            grad_value_ref[theirs, lanes] = value_sums[s].T.astype(jnp.bfloat16)


def finish_kernel(
    factor, keys_hbm, values_hbm, grad_out_hbm, intra_value_hbm, intra_key_hbm, intra_query_hbm, later_hbm, prior_hbm,
    w_value_hbm, w_key_hbm, w_query_hbm, out_hbm,
    lefts, intras, states, weights, grads, total, out, in_sem, out_sem,
):
    wide = w_query_hbm.shape[0]
    heads = later_hbm.shape[0]
    parts = halves(wide)
    later_copy = arrive(later_hbm, states.at[0], in_sem.at[0])
    prior_copy = None
    copies = []
    sem = 2
    for kind, (left_hbm, intra_hbm, weight_hbm) in enumerate((
        (keys_hbm, intra_value_hbm, w_value_hbm),
        (values_hbm, intra_key_hbm, w_key_hbm),
        (grad_out_hbm, intra_query_hbm, w_query_hbm),
    )):
        if kind == 2:
            prior_copy = arrive(prior_hbm, states.at[1], in_sem.at[1])
        here = [arrive(left_hbm, lefts.at[kind], in_sem.at[sem]), arrive(intra_hbm, intras.at[kind], in_sem.at[sem + 1])]
        for half, rows in enumerate(parts):
            here.append(arrive(weight_hbm.at[rows], weights.at[kind, rows], in_sem.at[sem + 2 + half]))
        sem += 4
        copies.append(here)
    sent = []
    for kind in range(3):
        if kind == 0:
            later_copy.wait()
        if kind == 2:
            prior_copy.wait()
        copies[kind][0].wait()
        copies[kind][1].wait()
        for head in range(heads):
            lanes = pl.ds(head * DH, DH)
            state = states[1 if kind == 2 else 0, head]
            inter = mul(lefts[kind, :, lanes], state, PLAIN if kind == 0 else LAST_LAST)
            grads[kind, :, lanes] = (factor * (inter + intras[kind, :, lanes].astype(jnp.float32))).astype(jnp.bfloat16)
        for half, columns in enumerate(parts):
            copies[kind][2 + half].wait()
            term = mul(grads[kind], weights[kind, columns], LAST_LAST)
            if kind == 0:
                total[:, columns] = term
            elif kind == 1:
                total[:, columns] += term
            else:
                out[:, columns] = (total[:, columns] + term).astype(jnp.bfloat16)
                sent.append(arrive(out.at[:, columns], out_hbm.at[:, columns], out_sem.at[half]))
    for copy in sent:
        copy.wait()


def shards(tokens, cotangent, w_query, w_key, w_value, w_out):
    rows, wide = tokens.shape
    columns = w_query.shape[1]
    heads = columns // DH
    factor = 1.0 / math.sqrt(DH * rows * lax.axis_size(AXES))
    part = pl.BlockSpec((rows, PAIR), lambda i: (0, i))
    columns_shape = jax.ShapeDtypeStruct((rows, columns), jnp.bfloat16)

    grad_out, query, grad_state = states_call("grad_out_query", cotangent, w_out, tokens, w_query, True, False)
    later = exclusive_scan(grad_state, True)
    keys, values, key_state = states_call("keys_values", tokens, w_key, tokens, w_value, False, True)
    prior = exclusive_scan(key_state, False)
    intra_query, intra_key, intra_value = pl.pallas_call(
        intra_kernel,
        grid=(heads // 2,),
        in_specs=[part] * 4,
        out_specs=[part] * 3,
        out_shape=[columns_shape] * 3,
        compiler_params=params(60),
        cost_estimate=pl.CostEstimate(
            flops=10 * rows * rows * columns, bytes_accessed=14 * rows * columns, transcendentals=0
        ),
        name="intra",
    )(query, keys, values, grad_out)

    anywhere = pl.BlockSpec(memory_space=pl.ANY)
    three = pltpu.VMEM((3, rows, columns), jnp.bfloat16)
    return pl.pallas_call(
        functools.partial(finish_kernel, factor),
        in_specs=[anywhere] * 11,
        out_specs=anywhere,
        out_shape=jax.ShapeDtypeStruct((rows, wide), jnp.bfloat16),
        scratch_shapes=[
            three, three, pltpu.VMEM((2, heads, DH, DH), jnp.bfloat16), pltpu.VMEM((3, wide, columns), jnp.bfloat16), three,
            pltpu.VMEM((rows, wide), jnp.float32), pltpu.VMEM((rows, wide), jnp.bfloat16),
            pltpu.SemaphoreType.DMA((14,)), pltpu.SemaphoreType.DMA((2,)),
        ],
        compiler_params=params(60),
        cost_estimate=pl.CostEstimate(
            flops=6 * rows * columns * (wide + DH), bytes_accessed=2 * (6 * rows * columns + 3 * wide * columns),
            transcendentals=0,
        ),
        name="finish",
    )(keys, values, grad_out, intra_value, intra_key, intra_query, later, prior, w_value, w_key, w_query)


def solution(mesh):
    placed = (P(AXES, None), P(AXES, None), P(), P(), P(), P())
    return jax.shard_map(
        shards, mesh=mesh, in_specs=placed, out_specs=P(AXES, None), check_vma=False
    )
```

```python
import functools
import math

import jax
import jax.numpy as jnp
from jax import lax
from jax.experimental import pallas as pl
from jax.experimental.pallas import tpu as pltpu
from jax.sharding import PartitionSpec as P

DH = 128
PAIR = 2 * DH
AXES = ("ctxa", "ctxb")
ROWS_ROWS = (((0,), (0,)), ((), ()))
LAST_LAST = (((1,), (1,)), ((), ()))
PLAIN = (((1,), (0,)), ((), ()))


def mul(left, right, dims=PLAIN):
    return lax.dot_general(left, right, dims, preferred_element_type=jnp.float32)


HELD = pl.BlockSpec(memory_space=pltpu.VMEM)
FAR = pl.BlockSpec(memory_space=pl.ANY)


def held(array):
    return pltpu.with_memory_space_constraint(array, pltpu.VMEM)


def far(array):
    return pltpu.with_memory_space_constraint(array, pltpu.HBM)


def params(mebibytes):
    return pltpu.CompilerParams(vmem_limit_bytes=mebibytes << 20)


def scan_kernel(slices_ref, sums_ref):
    count = slices_ref.shape[0]
    zero = jnp.zeros(slices_ref.shape[2:], jnp.float32)

    def one(lap, totals):
        prior, later = totals
        place = count - 1 - lap
        sums_ref[lap, 0] = prior.astype(jnp.bfloat16)
        sums_ref[place, 1] = later.astype(jnp.bfloat16)
        return prior + slices_ref[lap, 0].astype(jnp.float32), later + slices_ref[place, 1].astype(jnp.float32)

    lax.fori_loop(0, count, one, (zero, zero), unroll=8)


def exclusive_scan(slices):
    slices = lax.all_to_all(slices, AXES, 0, 0, tiled=True)
    sums = pl.pallas_call(
        scan_kernel,
        in_specs=[HELD],
        out_specs=HELD,
        out_shape=pltpu.VMEM(slices.shape, jnp.bfloat16),
        compiler_params=params(8),
        name="scan",
    )(held(slices))
    return lax.all_to_all(sums, AXES, 0, 0, tiled=True)


def arrive(source, target, sem):
    copy = pltpu.make_async_copy(source, target, sem)
    copy.start()
    return copy


def halves(extent):
    return [pl.ds(half * (extent // 2), extent // 2) for half in range(2)]


def project(left_ref, right_ref, copies, wide, transposed):
    total = None
    for lanes, waits in zip(halves(wide), copies):
        for copy in waits:
            copy.wait()
        if transposed:
            term = mul(left_ref[:, lanes], right_ref[:, lanes], LAST_LAST)
        else:
            term = mul(left_ref[:, lanes], right_ref[lanes, :])
        total = term if total is None else total + term
    return total.astype(jnp.bfloat16)


def project_kernel(
    cotangent_hbm, w_out_hbm, tokens_hbm, w_query_hbm, w_key_hbm, w_value_hbm,
    grad_out, query, keys, values, slices_ref, w_query, w_key, w_value, cotangent, w_out, tokens, sems,
):
    wide = tokens_hbm.shape[1]
    copies, sem = [], 0
    for left_hbm, left, right_hbm, right, transposed in (
        (cotangent_hbm, cotangent, w_out_hbm, w_out, True),
        (tokens_hbm, tokens, w_query_hbm, w_query, False),
        (None, None, w_key_hbm, w_key, False),
        (None, None, w_value_hbm, w_value, False),
    ):
        here = []
        for lanes in halves(wide):
            waits = []
            if left is not None:
                waits.append(arrive(left_hbm.at[:, lanes], left.at[:, lanes], sems.at[sem]))
                sem += 1
            if transposed:
                waits.append(arrive(right_hbm.at[:, lanes], right.at[:, lanes], sems.at[sem]))
            else:
                waits.append(arrive(right_hbm.at[lanes], right.at[lanes], sems.at[sem]))
            sem += 1
            here.append(waits)
        copies.append(here)
    grad_out[...] = project(cotangent, w_out, copies[0], wide, True)
    query[...] = project(tokens, w_query, copies[1], wide, False)
    keys[...] = project(tokens, w_key, copies[2], wide, False)
    values[...] = project(tokens, w_value, copies[3], wide, False)
    rows = slices_ref.shape[2]
    for kind, (left, right) in enumerate(((keys, values), (query, grad_out))):
        for head in range(left.shape[1] // DH):
            lanes = pl.ds(head * DH, DH)
            state = mul(left[:, lanes], right[:, lanes], ROWS_ROWS).astype(jnp.bfloat16)
            for part in range(DH // rows):
                slices_ref[head * (DH // rows) + part, kind] = state[part * rows : (part + 1) * rows]


def intra_kernel(query_ref, keys_ref, values_ref, grad_out_ref, grad_query_ref, grad_key_ref, grad_value_ref):
    rows = query_ref.shape[0]
    step = min(rows, 256)
    blocks = [pl.ds(at * step, step) for at in range(rows // step)]
    below = lax.broadcasted_iota(jnp.int32, (step, step), 0) >= lax.broadcasted_iota(jnp.int32, (step, step), 1)

    def score(left, right, masked):
        found = mul(left, right, LAST_LAST)
        return (jnp.where(below, found, 0.0) if masked else found).astype(jnp.bfloat16)

    for head in range(query_ref.shape[1] // DH):
        lanes = pl.ds(head * DH, DH)
        query_t = query_ref[:, lanes].T
        grad_out_t = grad_out_ref[:, lanes].T
        key_sums, value_sums = [None] * len(blocks), [None] * len(blocks)
        for t, mine in enumerate(blocks):
            span = slice(t * step, (t + 1) * step)
            query_sum = None
            for s, theirs in enumerate(blocks[: t + 1]):
                probe = score(grad_out_ref[mine, lanes], values_ref[theirs, lanes], s == t)
                attend = score(query_ref[mine, lanes], keys_ref[theirs, lanes], s == t)
                term = mul(probe, keys_ref[theirs, lanes])
                query_sum = term if query_sum is None else query_sum + term
                term = mul(query_t[:, span], probe)
                key_sums[s] = term if key_sums[s] is None else key_sums[s] + term
                term = mul(grad_out_t[:, span], attend)
                value_sums[s] = term if value_sums[s] is None else value_sums[s] + term
            grad_query_ref[mine, lanes] = query_sum.astype(jnp.bfloat16)
        for s, theirs in enumerate(blocks):
            grad_key_ref[theirs, lanes] = key_sums[s].T.astype(jnp.bfloat16)
            grad_value_ref[theirs, lanes] = value_sums[s].T.astype(jnp.bfloat16)


def finish_kernel(
    factor, keys, values, grad_out, intra_value, intra_key, intra_query, sums_ref, w_value, w_key, w_query, out_hbm,
    grads, total, out, sems,
):
    wide = w_query.shape[0]
    heads = keys.shape[1] // DH
    per_head = sums_ref.shape[0] // heads
    parts = halves(wide)
    sent = []
    for kind, (left, intra, weight) in enumerate(
        ((keys, intra_value, w_value), (values, intra_key, w_key), (grad_out, intra_query, w_query))
    ):
        for head in range(heads):
            lanes = pl.ds(head * DH, DH)
            state = sums_ref[pl.ds(head * per_head, per_head), 0 if kind == 2 else 1].reshape(DH, DH)
            inter = mul(left[:, lanes], state, PLAIN if kind == 0 else LAST_LAST)
            grads[:, lanes] = (factor * (inter + intra[:, lanes].astype(jnp.float32))).astype(jnp.bfloat16)
        for half, columns in enumerate(parts):
            term = mul(grads[...], weight[columns], LAST_LAST)
            if kind == 0:
                total[:, columns] = term
            elif kind == 1:
                total[:, columns] += term
            else:
                out[:, columns] = (total[:, columns] + term).astype(jnp.bfloat16)
                sent.append(arrive(out.at[:, columns], out_hbm.at[:, columns], sems.at[half]))
    for copy in sent:
        copy.wait()


def shards(tokens, cotangent, w_query, w_key, w_value, w_out):
    rows, wide = tokens.shape
    columns = w_query.shape[1]
    heads = columns // DH
    count = lax.axis_size(AXES)
    factor = 1.0 / math.sqrt(DH * rows * count)
    activation = pltpu.VMEM((rows, columns), jnp.bfloat16)
    weight = pltpu.VMEM((wide, columns), jnp.bfloat16)
    whole = pltpu.VMEM((rows, wide), jnp.bfloat16)

    grad_out, query, keys, values, slices, w_query, w_key, w_value = pl.pallas_call(
        project_kernel,
        in_specs=[FAR] * 6,
        out_specs=[HELD] * 8,
        out_shape=[activation] * 4 + [pltpu.VMEM((count, 2, columns // count, DH), jnp.bfloat16)] + [weight] * 3,
        scratch_shapes=[whole, pltpu.VMEM((columns, wide), jnp.bfloat16), whole, pltpu.SemaphoreType.DMA((12,))],
        compiler_params=params(24),
        cost_estimate=pl.CostEstimate(
            flops=8 * rows * wide * columns, bytes_accessed=4 * (rows + 2 * columns) * wide, transcendentals=0
        ),
        name="project",
    )(far(cotangent), far(w_out), far(tokens), far(w_query), far(w_key), far(w_value))
    sums = exclusive_scan(slices)
    intra_query, intra_key, intra_value = pl.pallas_call(
        intra_kernel,
        in_specs=[HELD] * 4,
        out_specs=[HELD] * 3,
        out_shape=[activation] * 3,
        compiler_params=params(16),
        cost_estimate=pl.CostEstimate(
            flops=10 * rows * rows * columns, bytes_accessed=14 * rows * columns, transcendentals=0
        ),
        name="intra",
    )(held(query), held(keys), held(values), held(grad_out))
    return pl.pallas_call(
        functools.partial(finish_kernel, factor),
        in_specs=[HELD] * 10,
        out_specs=FAR,
        out_shape=jax.ShapeDtypeStruct((rows, wide), jnp.bfloat16),
        scratch_shapes=[
            pltpu.VMEM((rows, columns), jnp.bfloat16), pltpu.VMEM((rows, wide), jnp.float32), whole,
            pltpu.SemaphoreType.DMA((2,)),
        ],
        compiler_params=params(24),
        cost_estimate=pl.CostEstimate(
            flops=6 * rows * columns * (wide + DH), bytes_accessed=2 * (6 * rows * columns + 3 * wide * columns),
            transcendentals=0,
        ),
        name="finish",
    )(*map(held, (keys, values, grad_out, intra_value, intra_key, intra_query, sums, w_value, w_key, w_query)))


def solution(mesh):
    placed = (P(AXES, None), P(AXES, None), P(), P(), P(), P())
    return jax.shard_map(
        shards, mesh=mesh, in_specs=placed, out_specs=P(AXES, None), check_vma=False
    )
```

```python
import functools
import math

import jax
import jax.numpy as jnp
from jax import lax
from jax.experimental import pallas as pl
from jax.experimental.pallas import tpu as pltpu
from jax.sharding import PartitionSpec as P

DH = 128
PAIR = 2 * DH
AXES = ("ctxa", "half", "rest")
HOMES = ("ctxa", "rest")
ROWS_ROWS = (((0,), (0,)), ((), ()))
LAST_LAST = (((1,), (1,)), ((), ()))
PLAIN = (((1,), (0,)), ((), ()))


def mul(left, right, dims=PLAIN):
    return lax.dot_general(left, right, dims, preferred_element_type=jnp.float32)


HELD = pl.BlockSpec(memory_space=pltpu.VMEM)
FAR = pl.BlockSpec(memory_space=pl.ANY)


def params(mebibytes):
    return pltpu.CompilerParams(vmem_limit_bytes=mebibytes << 20)


def sums_kernel(slices_ref, sums_ref):
    groups = sums_ref.shape[0]
    each = slices_ref.shape[0] // groups
    for group in range(groups):
        total = slices_ref[group * each].astype(jnp.float32)
        for place in range(1, each):
            total = total + slices_ref[group * each + place].astype(jnp.float32)
        sums_ref[group] = total.astype(jnp.bfloat16)


def scan_kernel(slices_ref, others_ref, out_ref):
    groups = others_ref.shape[0]
    each = slices_ref.shape[0] // groups
    upper = lax.axis_index("half") == 1
    for kind in range(2):
        total = jnp.zeros(slices_ref.shape[2:], jnp.float32)
        for lap in range(groups):
            group = groups - 1 - lap if kind else lap
            other = others_ref[group, kind].astype(jnp.float32)
            ahead = jnp.where(upper, 0.0, other) if kind else jnp.where(upper, other, 0.0)
            total = total + ahead
            for step in range(each):
                place = group * each + (each - 1 - step if kind else step)
                out_ref[place, kind] = total.astype(jnp.bfloat16)
                total = total + slices_ref[place, kind].astype(jnp.float32)
            total = total + (other - ahead)


def exclusive_scan(slices):
    groups = lax.axis_size("ctxa")
    slices = lax.all_to_all(slices, HOMES, 0, 0, tiled=True)
    sums = pl.pallas_call(
        sums_kernel,
        out_shape=jax.ShapeDtypeStruct((groups,) + slices.shape[1:], jnp.bfloat16),
        compiler_params=params(60),
        name="sums",
    )(slices)
    others = lax.ppermute(sums, "half", [(0, 1), (1, 0)])
    sums = pl.pallas_call(
        scan_kernel,
        out_shape=jax.ShapeDtypeStruct(slices.shape, jnp.bfloat16),
        compiler_params=params(60),
        name="scan",
    )(slices, others)
    return lax.all_to_all(sums, HOMES, 0, 0, tiled=True)


def arrive(source, target, sem):
    copy = pltpu.make_async_copy(source, target, sem)
    copy.start()
    return copy


def halves(extent):
    return [pl.ds(half * (extent // 2), extent // 2) for half in range(2)]


def project(left, right, copies, wide, transposed):
    if len(copies) == 1:
        for copy in copies[0]:
            copy.wait()
        return mul(left[...], right[...], LAST_LAST if transposed else PLAIN).astype(jnp.bfloat16)
    total = None
    for lanes, waits in zip(halves(wide), copies):
        for copy in waits:
            copy.wait()
        if transposed:
            term = mul(left[:, lanes], right[:, lanes], LAST_LAST)
        else:
            term = mul(left[:, lanes], right[lanes, :])
        total = term if total is None else total + term
    return total.astype(jnp.bfloat16)


def project_kernel(
    cotangent_hbm, w_out_hbm, tokens_hbm, w_query_hbm, w_key_hbm, w_value_hbm,
    grad_out_hbm, query_hbm, keys_hbm, values_hbm, slices_ref,
    cotangent, w_out, tokens, w_query, w_key, w_value, grad_out, query, keys, values, sems, out_sems,
):
    wide = tokens_hbm.shape[1]
    first = []
    for half, lanes in enumerate(halves(wide)):
        first.append([
            arrive(cotangent_hbm.at[:, lanes], cotangent.at[:, lanes], sems.at[2 * half]),
            arrive(w_out_hbm.at[:, lanes], w_out.at[:, lanes], sems.at[2 * half + 1]),
        ])
    second = [[arrive(tokens_hbm, tokens, sems.at[4]), arrive(w_query_hbm, w_query, sems.at[5])]]
    third = [[arrive(w_key_hbm, w_key, sems.at[6])]]
    fourth = [[arrive(w_value_hbm, w_value, sems.at[7])]]
    sent = []
    for at, (left, right, copies, out, out_hbm) in enumerate((
        (cotangent, w_out, first, grad_out, grad_out_hbm),
        (tokens, w_query, second, query, query_hbm),
        (tokens, w_key, third, keys, keys_hbm),
        (tokens, w_value, fourth, values, values_hbm),
    )):
        out[...] = project(left, right, copies, wide, at == 0)
        sent.append(arrive(out, out_hbm, out_sems.at[at]))
    rows = slices_ref.shape[2]
    for kind, (left, right) in enumerate(((keys, values), (query, grad_out))):
        for head in range(left.shape[1] // DH):
            lanes = pl.ds(head * DH, DH)
            state = mul(left[:, lanes], right[:, lanes], ROWS_ROWS).astype(jnp.bfloat16)
            for part in range(DH // rows):
                slices_ref[head * (DH // rows) + part, kind] = state[part * rows : (part + 1) * rows]
    for copy in sent:
        copy.wait()


def intra_kernel(query_ref, keys_ref, values_ref, grad_out_ref, grad_query_ref, grad_key_ref, grad_value_ref):
    rows = query_ref.shape[0]
    step = min(rows, 256)
    blocks = [pl.ds(at * step, step) for at in range(rows // step)]
    below = lax.broadcasted_iota(jnp.int32, (step, step), 0) >= lax.broadcasted_iota(jnp.int32, (step, step), 1)

    def score(left, right, masked):
        found = mul(left, right, LAST_LAST)
        return (jnp.where(below, found, 0.0) if masked else found).astype(jnp.bfloat16)

    for head in range(query_ref.shape[1] // DH):
        lanes = pl.ds(head * DH, DH)
        query_t = query_ref[:, lanes].T
        grad_out_t = grad_out_ref[:, lanes].T
        key_sums, value_sums = [None] * len(blocks), [None] * len(blocks)
        for t, mine in enumerate(blocks):
            span = slice(t * step, (t + 1) * step)
            query_sum = None
            for s, theirs in enumerate(blocks[: t + 1]):
                probe = score(grad_out_ref[mine, lanes], values_ref[theirs, lanes], s == t)
                attend = score(query_ref[mine, lanes], keys_ref[theirs, lanes], s == t)
                term = mul(probe, keys_ref[theirs, lanes])
                query_sum = term if query_sum is None else query_sum + term
                term = mul(query_t[:, span], probe)
                key_sums[s] = term if key_sums[s] is None else key_sums[s] + term
                term = mul(grad_out_t[:, span], attend)
                value_sums[s] = term if value_sums[s] is None else value_sums[s] + term
            grad_query_ref[mine, lanes] = query_sum.astype(jnp.bfloat16)
        for s, theirs in enumerate(blocks):
            grad_key_ref[theirs, lanes] = key_sums[s].T.astype(jnp.bfloat16)
            grad_value_ref[theirs, lanes] = value_sums[s].T.astype(jnp.bfloat16)


def finish_kernel(
    factor, keys_hbm, values_hbm, grad_out_hbm, intra_value_hbm, intra_key_hbm, intra_query_hbm, sums_hbm,
    w_value_hbm, w_key_hbm, w_query_hbm, out_hbm,
    lefts, intras, states, weights, grads, total, out, sems, out_sems,
):
    wide = w_query_hbm.shape[0]
    heads = keys_hbm.shape[1] // DH
    per_head = sums_hbm.shape[0] // heads
    parts = halves(wide)
    states_copy = arrive(sums_hbm, states, sems.at[12])
    copies = []
    for kind, (left_hbm, intra_hbm, weight_hbm) in enumerate((
        (keys_hbm, intra_value_hbm, w_value_hbm),
        (values_hbm, intra_key_hbm, w_key_hbm),
        (grad_out_hbm, intra_query_hbm, w_query_hbm),
    )):
        here = [
            arrive(left_hbm, lefts.at[kind], sems.at[4 * kind]),
            arrive(intra_hbm, intras.at[kind], sems.at[4 * kind + 1]),
        ]
        for half, columns in enumerate(parts):
            here.append(arrive(weight_hbm.at[columns], weights.at[kind, columns], sems.at[4 * kind + 2 + half]))
        copies.append(here)
    states_copy.wait()
    sent = []
    for kind in range(3):
        copies[kind][0].wait()
        copies[kind][1].wait()
        for head in range(heads):
            lanes = pl.ds(head * DH, DH)
            state = states[pl.ds(head * per_head, per_head), 0 if kind == 2 else 1].reshape(DH, DH)
            inter = mul(lefts[kind, :, lanes], state, PLAIN if kind == 0 else LAST_LAST)
            grads[:, lanes] = (factor * (inter + intras[kind, :, lanes].astype(jnp.float32))).astype(jnp.bfloat16)
        for half, columns in enumerate(parts):
            copies[kind][2 + half].wait()
            term = mul(grads[...], weights[kind, columns], LAST_LAST)
            if kind == 0:
                total[:, columns] = term
            elif kind == 1:
                total[:, columns] += term
            else:
                out[:, columns] = (total[:, columns] + term).astype(jnp.bfloat16)
                sent.append(arrive(out.at[:, columns], out_hbm.at[:, columns], out_sems.at[half]))
    for copy in sent:
        copy.wait()


def shards(tokens, cotangent, w_query, w_key, w_value, w_out):
    rows, wide = tokens.shape
    columns = w_query.shape[1]
    heads = columns // DH
    homes = lax.axis_size(HOMES)
    factor = 1.0 / math.sqrt(DH * rows * lax.axis_size(AXES))
    activation = pltpu.VMEM((rows, columns), jnp.bfloat16)
    weight = pltpu.VMEM((wide, columns), jnp.bfloat16)
    whole = pltpu.VMEM((rows, wide), jnp.bfloat16)
    columns_shape = jax.ShapeDtypeStruct((rows, columns), jnp.bfloat16)
    slices_shape = (homes, 2, columns // homes, DH)

    grad_out, query, keys, values, slices = pl.pallas_call(
        project_kernel,
        in_specs=[FAR] * 6,
        out_specs=[FAR] * 4 + [HELD],
        out_shape=[columns_shape] * 4 + [jax.ShapeDtypeStruct(slices_shape, jnp.bfloat16)],
        scratch_shapes=[whole, pltpu.VMEM((columns, wide), jnp.bfloat16), whole] + [weight] * 3 + [activation] * 4
        + [pltpu.SemaphoreType.DMA((8,)), pltpu.SemaphoreType.DMA((4,))],
        compiler_params=params(60),
        cost_estimate=pl.CostEstimate(
            flops=8 * rows * wide * columns, bytes_accessed=4 * (rows + 2 * columns) * wide, transcendentals=0
        ),
        name="project",
    )(cotangent, w_out, tokens, w_query, w_key, w_value)
    sums = exclusive_scan(slices)
    part = pl.BlockSpec((rows, PAIR), lambda i: (0, i))
    intra_query, intra_key, intra_value = pl.pallas_call(
        intra_kernel,
        grid=(heads // 2,),
        in_specs=[part] * 4,
        out_specs=[part] * 3,
        out_shape=[columns_shape] * 3,
        compiler_params=params(60),
        cost_estimate=pl.CostEstimate(
            flops=10 * rows * rows * columns, bytes_accessed=14 * rows * columns, transcendentals=0
        ),
        name="intra",
    )(query, keys, values, grad_out)
    three = pltpu.VMEM((3, rows, columns), jnp.bfloat16)
    return pl.pallas_call(
        functools.partial(finish_kernel, factor),
        in_specs=[FAR] * 10,
        out_specs=FAR,
        out_shape=jax.ShapeDtypeStruct((rows, wide), jnp.bfloat16),
        scratch_shapes=[
            three, three, pltpu.VMEM(slices_shape, jnp.bfloat16), pltpu.VMEM((3, wide, columns), jnp.bfloat16), activation,
            pltpu.VMEM((rows, wide), jnp.float32), whole,
            pltpu.SemaphoreType.DMA((13,)), pltpu.SemaphoreType.DMA((2,)),
        ],
        compiler_params=params(60),
        cost_estimate=pl.CostEstimate(
            flops=6 * rows * columns * (wide + DH), bytes_accessed=2 * (6 * rows * columns + 3 * wide * columns),
            transcendentals=0,
        ),
        name="finish",
    )(keys, values, grad_out, intra_value, intra_key, intra_query, sums, w_value, w_key, w_query)


def solution(mesh):
    groups, places = mesh.devices.shape
    mesh = jax.sharding.Mesh(mesh.devices.reshape(groups, 2, places // 2), AXES)
    placed = (P(AXES, None), P(AXES, None), P(), P(), P(), P())
    return jax.shard_map(
        shards, mesh=mesh, in_specs=placed, out_specs=P(AXES, None), check_vma=False
    )
```

```python
import functools
import math

import jax
import jax.numpy as jnp
from jax import lax
from jax.experimental import pallas as pl
from jax.experimental.pallas import tpu as pltpu
from jax.sharding import PartitionSpec as P

DH = 128
PAIR = 2 * DH
AXES = ("ctxa", "ctxb")
ROWS_ROWS = (((0,), (0,)), ((), ()))
LAST_LAST = (((1,), (1,)), ((), ()))
PLAIN = (((1,), (0,)), ((), ()))


def mul(left, right, dims=PLAIN):
    return lax.dot_general(left, right, dims, preferred_element_type=jnp.float32)


HELD = pl.BlockSpec(memory_space=pltpu.VMEM)
FAR = pl.BlockSpec(memory_space=pl.ANY)


def params(mebibytes):
    return pltpu.CompilerParams(vmem_limit_bytes=mebibytes << 20)


def scan_kernel(slices_ref, sums_ref):
    count = slices_ref.shape[0]
    zero = jnp.zeros(slices_ref.shape[2:], jnp.float32)

    def one(lap, totals):
        prior, later = totals
        place = count - 1 - lap
        sums_ref[lap, 0] = prior.astype(jnp.bfloat16)
        sums_ref[place, 1] = later.astype(jnp.bfloat16)
        return prior + slices_ref[lap, 0].astype(jnp.float32), later + slices_ref[place, 1].astype(jnp.float32)

    lax.fori_loop(0, count, one, (zero, zero), unroll=8)


def exclusive_scan(slices):
    slices = lax.all_to_all(slices, AXES, 0, 0, tiled=True)
    sums = pl.pallas_call(
        scan_kernel,
        out_shape=jax.ShapeDtypeStruct(slices.shape, jnp.bfloat16),
        compiler_params=params(60),
        name="scan",
    )(slices)
    return lax.all_to_all(sums, AXES, 0, 0, tiled=True)


def arrive(source, target, sem):
    copy = pltpu.make_async_copy(source, target, sem)
    copy.start()
    return copy


def chunks(extent, size):
    return [pl.ds(at, size) for at in range(0, extent, size)]


def project_kernel(
    cotangent_hbm, w_out_hbm, tokens_hbm, w_query_hbm, w_key_hbm, w_value_hbm,
    grad_out_hbm, query_hbm, keys_hbm, values_hbm, slices_ref,
    cotangent, w_out, tokens, w_query, w_key, w_value, grad_out, query, keys, values, sems, out_sems,
):
    parts = chunks(grad_out.shape[1], PAIR)
    first = [arrive(cotangent_hbm, cotangent, sems.at[0])]
    w_out_copies = [arrive(w_out_hbm.at[part], w_out.at[part], sems.at[4 + at]) for at, part in enumerate(parts)]
    second = [arrive(tokens_hbm, tokens, sems.at[1]), arrive(w_query_hbm, w_query, sems.at[4 + len(parts)])]
    third = [arrive(w_key_hbm, w_key, sems.at[2])]
    fourth = [arrive(w_value_hbm, w_value, sems.at[3])]
    sent = []
    for at, (left, right, copies, out, out_hbm) in enumerate((
        (cotangent, w_out, first, grad_out, grad_out_hbm),
        (tokens, w_query, second, query, query_hbm),
        (tokens, w_key, third, keys, keys_hbm),
        (tokens, w_value, fourth, values, values_hbm),
    )):
        for copy in copies:
            copy.wait()
        for number, part in enumerate(parts):
            if at == 0:
                w_out_copies[number].wait()
                product = mul(left[...], right[part], LAST_LAST)
            else:
                product = mul(left[...], right[:, part])
            out[:, part] = product.astype(jnp.bfloat16)
        sent.append(arrive(out, out_hbm, out_sems.at[at]))
    rows = slices_ref.shape[2]
    for kind, (left, right) in enumerate(((keys, values), (query, grad_out))):
        for head in range(left.shape[1] // DH):
            lanes = pl.ds(head * DH, DH)
            state = mul(left[:, lanes], right[:, lanes], ROWS_ROWS).astype(jnp.bfloat16)
            for part in range(DH // rows):
                slices_ref[head * (DH // rows) + part, kind] = state[part * rows : (part + 1) * rows]
    for copy in sent:
        copy.wait()


def intra_kernel(query_ref, keys_ref, values_ref, grad_out_ref, grad_query_ref, grad_key_ref, grad_value_ref):
    rows = query_ref.shape[0]
    step = min(rows, 256)
    blocks = [pl.ds(at * step, step) for at in range(rows // step)]
    below = lax.broadcasted_iota(jnp.int32, (step, step), 0) >= lax.broadcasted_iota(jnp.int32, (step, step), 1)

    def score(left, right, masked):
        found = mul(left, right, LAST_LAST)
        return (jnp.where(below, found, 0.0) if masked else found).astype(jnp.bfloat16)

    for head in range(query_ref.shape[1] // DH):
        lanes = pl.ds(head * DH, DH)
        query_t = query_ref[:, lanes].T
        grad_out_t = grad_out_ref[:, lanes].T
        key_sums, value_sums = [None] * len(blocks), [None] * len(blocks)
        for t, mine in enumerate(blocks):
            span = slice(t * step, (t + 1) * step)
            query_sum = None
            for s, theirs in enumerate(blocks[: t + 1]):
                probe = score(grad_out_ref[mine, lanes], values_ref[theirs, lanes], s == t)
                attend = score(query_ref[mine, lanes], keys_ref[theirs, lanes], s == t)
                term = mul(probe, keys_ref[theirs, lanes])
                query_sum = term if query_sum is None else query_sum + term
                term = mul(query_t[:, span], probe)
                key_sums[s] = term if key_sums[s] is None else key_sums[s] + term
                term = mul(grad_out_t[:, span], attend)
                value_sums[s] = term if value_sums[s] is None else value_sums[s] + term
            grad_query_ref[mine, lanes] = query_sum.astype(jnp.bfloat16)
        for s, theirs in enumerate(blocks):
            grad_key_ref[theirs, lanes] = key_sums[s].T.astype(jnp.bfloat16)
            grad_value_ref[theirs, lanes] = value_sums[s].T.astype(jnp.bfloat16)


def finish_kernel(
    factor, keys_hbm, values_hbm, grad_out_hbm, intra_value_hbm, intra_key_hbm, intra_query_hbm, sums_hbm,
    w_value_hbm, w_key_hbm, w_query_hbm, out_hbm,
    lefts, intras, states, weights, grads, total, out, sems, out_sems,
):
    wide = w_query_hbm.shape[0]
    heads = keys_hbm.shape[1] // DH
    per_head = sums_hbm.shape[0] // heads
    parts = chunks(wide, 2 * PAIR)
    each = 2 + len(parts)
    states_copy = arrive(sums_hbm, states, sems.at[3 * each])
    copies = []
    for kind, (left_hbm, intra_hbm, weight_hbm) in enumerate((
        (keys_hbm, intra_value_hbm, w_value_hbm),
        (values_hbm, intra_key_hbm, w_key_hbm),
        (grad_out_hbm, intra_query_hbm, w_query_hbm),
    )):
        here = [
            arrive(left_hbm, lefts.at[kind], sems.at[each * kind]),
            arrive(intra_hbm, intras.at[kind], sems.at[each * kind + 1]),
        ]
        for at, columns in enumerate(parts):
            here.append(arrive(weight_hbm.at[columns], weights.at[kind, columns], sems.at[each * kind + 2 + at]))
        copies.append(here)
    states_copy.wait()
    sent = []
    for kind in range(3):
        copies[kind][0].wait()
        copies[kind][1].wait()
        for head in range(heads):
            lanes = pl.ds(head * DH, DH)
            state = states[pl.ds(head * per_head, per_head), 0 if kind == 2 else 1].reshape(DH, DH)
            inter = mul(lefts[kind, :, lanes], state, PLAIN if kind == 0 else LAST_LAST)
            grads[:, lanes] = (factor * (inter + intras[kind, :, lanes].astype(jnp.float32))).astype(jnp.bfloat16)
        for at, columns in enumerate(parts):
            copies[kind][2 + at].wait()
            term = mul(grads[...], weights[kind, columns], LAST_LAST)
            if kind == 0:
                total[:, columns] = term
            elif kind == 1:
                total[:, columns] += term
            else:
                out[:, columns] = (total[:, columns] + term).astype(jnp.bfloat16)
                sent.append(arrive(out.at[:, columns], out_hbm.at[:, columns], out_sems.at[at]))
    for copy in sent:
        copy.wait()


def shards(tokens, cotangent, w_query, w_key, w_value, w_out):
    rows, wide = tokens.shape
    columns = w_query.shape[1]
    heads = columns // DH
    homes = lax.axis_size(AXES)
    factor = 1.0 / math.sqrt(DH * rows * lax.axis_size(AXES))
    activation = pltpu.VMEM((rows, columns), jnp.bfloat16)
    weight = pltpu.VMEM((wide, columns), jnp.bfloat16)
    whole = pltpu.VMEM((rows, wide), jnp.bfloat16)
    columns_shape = jax.ShapeDtypeStruct((rows, columns), jnp.bfloat16)
    slices_shape = (homes, 2, columns // homes, DH)

    grad_out, query, keys, values, slices = pl.pallas_call(
        project_kernel,
        in_specs=[FAR] * 6,
        out_specs=[FAR] * 4 + [HELD],
        out_shape=[columns_shape] * 4 + [jax.ShapeDtypeStruct(slices_shape, jnp.bfloat16)],
        scratch_shapes=[whole, pltpu.VMEM((columns, wide), jnp.bfloat16), whole] + [weight] * 3 + [activation] * 4
        + [pltpu.SemaphoreType.DMA((5 + columns // PAIR,)), pltpu.SemaphoreType.DMA((4,))],
        compiler_params=params(60),
        cost_estimate=pl.CostEstimate(
            flops=8 * rows * wide * columns, bytes_accessed=4 * (rows + 2 * columns) * wide, transcendentals=0
        ),
        name="project",
    )(cotangent, w_out, tokens, w_query, w_key, w_value)
    sums = exclusive_scan(slices)
    part = pl.BlockSpec((rows, PAIR), lambda i: (0, i))
    intra_query, intra_key, intra_value = pl.pallas_call(
        intra_kernel,
        grid=(heads // 2,),
        in_specs=[part] * 4,
        out_specs=[part] * 3,
        out_shape=[columns_shape] * 3,
        compiler_params=params(60),
        cost_estimate=pl.CostEstimate(
            flops=10 * rows * rows * columns, bytes_accessed=14 * rows * columns, transcendentals=0
        ),
        name="intra",
    )(query, keys, values, grad_out)
    three = pltpu.VMEM((3, rows, columns), jnp.bfloat16)
    return pl.pallas_call(
        functools.partial(finish_kernel, factor),
        in_specs=[FAR] * 10,
        out_specs=FAR,
        out_shape=jax.ShapeDtypeStruct((rows, wide), jnp.bfloat16),
        scratch_shapes=[
            three, three, pltpu.VMEM(slices_shape, jnp.bfloat16), pltpu.VMEM((3, wide, columns), jnp.bfloat16), activation,
            pltpu.VMEM((rows, wide), jnp.float32), whole,
            pltpu.SemaphoreType.DMA((7 + 3 * (wide // (2 * PAIR)),)), pltpu.SemaphoreType.DMA((wide // (2 * PAIR),)),
        ],
        compiler_params=params(60),
        cost_estimate=pl.CostEstimate(
            flops=6 * rows * columns * (wide + DH), bytes_accessed=2 * (6 * rows * columns + 3 * wide * columns),
            transcendentals=0,
        ),
        name="finish",
    )(keys, values, grad_out, intra_value, intra_key, intra_query, sums, w_value, w_key, w_query)


def solution(mesh):
    placed = (P(AXES, None), P(AXES, None), P(), P(), P(), P())
    return jax.shard_map(
        shards, mesh=mesh, in_specs=placed, out_specs=P(AXES, None), check_vma=False
    )
```

```python
import functools
import math

import jax
import jax.numpy as jnp
from jax import lax
from jax.experimental import pallas as pl
from jax.experimental.pallas import tpu as pltpu
from jax.sharding import PartitionSpec as P

DH = 128
PAIR = 2 * DH
AXES = ("ctxa", "half", "rest")
HOMES = ("ctxa", "rest")
ROWS_ROWS = (((0,), (0,)), ((), ()))
LAST_LAST = (((1,), (1,)), ((), ()))
PLAIN = (((1,), (0,)), ((), ()))


def mul(left, right, dims=PLAIN):
    return lax.dot_general(left, right, dims, preferred_element_type=jnp.float32)


HELD = pl.BlockSpec(memory_space=pltpu.VMEM)
FAR = pl.BlockSpec(memory_space=pl.ANY)


def held(array):
    return pltpu.with_memory_space_constraint(array, pltpu.VMEM)


def far(array):
    return pltpu.with_memory_space_constraint(array, pltpu.HBM)


def params(mebibytes):
    return pltpu.CompilerParams(vmem_limit_bytes=mebibytes << 20)


def sums_kernel(slices_ref, sums_ref):
    groups = sums_ref.shape[0]
    each = slices_ref.shape[0] // groups
    for group in range(groups):
        total = slices_ref[group * each].astype(jnp.float32)
        for place in range(1, each):
            total = total + slices_ref[group * each + place].astype(jnp.float32)
        sums_ref[group] = total.astype(jnp.bfloat16)


def scan_kernel(slices_ref, others_ref, out_ref):
    groups = others_ref.shape[0]
    each = slices_ref.shape[0] // groups
    upper = lax.axis_index("half") == 1
    for kind in range(2):
        total = jnp.zeros(slices_ref.shape[2:], jnp.float32)
        for lap in range(groups):
            group = groups - 1 - lap if kind else lap
            other = others_ref[group, kind].astype(jnp.float32)
            ahead = jnp.where(upper, 0.0, other) if kind else jnp.where(upper, other, 0.0)
            total = total + ahead
            for step in range(each):
                place = group * each + (each - 1 - step if kind else step)
                out_ref[place, kind] = total.astype(jnp.bfloat16)
                total = total + slices_ref[place, kind].astype(jnp.float32)
            total = total + (other - ahead)


def exclusive_scan(slices):
    groups = lax.axis_size("ctxa")
    slices = lax.all_to_all(slices, HOMES, 0, 0, tiled=True)
    sums = pl.pallas_call(
        sums_kernel,
        in_specs=[HELD],
        out_specs=HELD,
        out_shape=pltpu.VMEM((groups,) + slices.shape[1:], jnp.bfloat16),
        compiler_params=params(8),
        name="sums",
    )(held(slices))
    others = lax.ppermute(sums, "half", [(0, 1), (1, 0)])
    sums = pl.pallas_call(
        scan_kernel,
        in_specs=[HELD, HELD],
        out_specs=HELD,
        out_shape=pltpu.VMEM(slices.shape, jnp.bfloat16),
        compiler_params=params(8),
        name="scan",
    )(held(slices), held(others))
    return lax.all_to_all(sums, HOMES, 0, 0, tiled=True)


def arrive(source, target, sem):
    copy = pltpu.make_async_copy(source, target, sem)
    copy.start()
    return copy


def halves(extent):
    return [pl.ds(half * (extent // 2), extent // 2) for half in range(2)]


def project_kernel(
    cotangent_hbm, w_out_hbm, tokens_hbm, w_query_hbm, w_key_hbm, w_value_hbm,
    grad_out_hbm, query_hbm, keys_hbm, values_hbm, slices_ref,
    cotangent, w_out, tokens, w_query, w_both, grad_out, query, both, sems, out_sems,
):
    columns = query.shape[1]
    keys_at, values_at = pl.ds(0, columns), pl.ds(columns, columns)
    parts = halves(tokens.shape[1])
    first = []
    for half, lanes in enumerate(parts):
        first.append([
            arrive(cotangent_hbm.at[:, lanes], cotangent.at[:, lanes], sems.at[2 * half]),
            arrive(w_out_hbm.at[:, lanes], w_out.at[:, lanes], sems.at[2 * half + 1]),
        ])
    second = [arrive(tokens_hbm, tokens, sems.at[4]), arrive(w_query_hbm, w_query, sems.at[5])]
    third = [
        arrive(w_key_hbm, w_both.at[:, keys_at], sems.at[6]),
        arrive(w_value_hbm, w_both.at[:, values_at], sems.at[7]),
    ]
    total = None
    for lanes, copies in zip(parts, first):
        for copy in copies:
            copy.wait()
        term = mul(cotangent[:, lanes], w_out[:, lanes], LAST_LAST)
        total = term if total is None else total + term
    grad_out[...] = total.astype(jnp.bfloat16)
    sent = [arrive(grad_out, grad_out_hbm, out_sems.at[0])]
    for copy in second:
        copy.wait()
    query[...] = mul(tokens[...], w_query[...]).astype(jnp.bfloat16)
    sent.append(arrive(query, query_hbm, out_sems.at[1]))
    for copy in third:
        copy.wait()
    both[...] = mul(tokens[...], w_both[...]).astype(jnp.bfloat16)
    sent.append(arrive(both.at[:, keys_at], keys_hbm, out_sems.at[2]))
    sent.append(arrive(both.at[:, values_at], values_hbm, out_sems.at[3]))
    rows = slices_ref.shape[2]
    for head in range(columns // DH):
        lanes = pl.ds(head * DH, DH)
        for kind, (left, right) in enumerate((
            (both[:, lanes], both[:, pl.ds(columns + head * DH, DH)]), (query[:, lanes], grad_out[:, lanes])
        )):
            state = mul(left, right, ROWS_ROWS).astype(jnp.bfloat16)
            for part in range(DH // rows):
                slices_ref[head * (DH // rows) + part, kind] = state[part * rows : (part + 1) * rows]
    for copy in sent:
        copy.wait()


def intra_kernel(query_ref, keys_ref, values_ref, grad_out_ref, grad_query_ref, grad_key_ref, grad_value_ref):
    rows = query_ref.shape[0]
    step = min(rows, 256)
    blocks = [pl.ds(at * step, step) for at in range(rows // step)]
    below = lax.broadcasted_iota(jnp.int32, (step, step), 0) >= lax.broadcasted_iota(jnp.int32, (step, step), 1)

    def score(left, right, masked):
        found = mul(left, right, LAST_LAST)
        return (jnp.where(below, found, 0.0) if masked else found).astype(jnp.bfloat16)

    for head in range(query_ref.shape[1] // DH):
        lanes = pl.ds(head * DH, DH)
        query_t = query_ref[:, lanes].T
        grad_out_t = grad_out_ref[:, lanes].T
        key_sums, value_sums = [None] * len(blocks), [None] * len(blocks)
        for t, mine in enumerate(blocks):
            span = slice(t * step, (t + 1) * step)
            query_sum = None
            for s, theirs in enumerate(blocks[: t + 1]):
                probe = score(grad_out_ref[mine, lanes], values_ref[theirs, lanes], s == t)
                attend = score(query_ref[mine, lanes], keys_ref[theirs, lanes], s == t)
                term = mul(probe, keys_ref[theirs, lanes])
                query_sum = term if query_sum is None else query_sum + term
                term = mul(query_t[:, span], probe)
                key_sums[s] = term if key_sums[s] is None else key_sums[s] + term
                term = mul(grad_out_t[:, span], attend)
                value_sums[s] = term if value_sums[s] is None else value_sums[s] + term
            grad_query_ref[mine, lanes] = query_sum.astype(jnp.bfloat16)
        for s, theirs in enumerate(blocks):
            grad_key_ref[theirs, lanes] = key_sums[s].T.astype(jnp.bfloat16)
            grad_value_ref[theirs, lanes] = value_sums[s].T.astype(jnp.bfloat16)


def finish_kernel(
    factor, keys_hbm, values_hbm, grad_out_hbm, intra_value_hbm, intra_key_hbm, intra_query_hbm, sums_ref,
    w_value_hbm, w_key_hbm, w_query_hbm, out_hbm,
    lefts, intras, weights, grads, total, out, sems, out_sems,
):
    wide = w_query_hbm.shape[0]
    heads = keys_hbm.shape[1] // DH
    per_head = sums_ref.shape[0] // heads
    parts = halves(wide)
    copies = []
    for kind, (left_hbm, intra_hbm, weight_hbm) in enumerate((
        (keys_hbm, intra_value_hbm, w_value_hbm),
        (values_hbm, intra_key_hbm, w_key_hbm),
        (grad_out_hbm, intra_query_hbm, w_query_hbm),
    )):
        here = [
            arrive(left_hbm, lefts.at[kind], sems.at[4 * kind]),
            arrive(intra_hbm, intras.at[kind], sems.at[4 * kind + 1]),
        ]
        for half, columns in enumerate(parts):
            here.append(arrive(weight_hbm.at[columns], weights.at[kind, columns], sems.at[4 * kind + 2 + half]))
        copies.append(here)
    sent = []
    for kind in range(3):
        copies[kind][0].wait()
        copies[kind][1].wait()
        for head in range(heads):
            lanes = pl.ds(head * DH, DH)
            state = sums_ref[pl.ds(head * per_head, per_head), 0 if kind == 2 else 1].reshape(DH, DH)
            inter = mul(lefts[kind, :, lanes], state, PLAIN if kind == 0 else LAST_LAST)
            grads[:, lanes] = (factor * (inter + intras[kind, :, lanes].astype(jnp.float32))).astype(jnp.bfloat16)
        if kind == 1:
            for copy in copies[kind][2:]:
                copy.wait()
            total[...] += mul(grads[...], weights[kind], LAST_LAST)
            continue
        for half, columns in enumerate(parts):
            copies[kind][2 + half].wait()
            term = mul(grads[...], weights[kind, columns], LAST_LAST)
            if kind == 0:
                total[:, columns] = term
            else:
                out[:, columns] = (total[:, columns] + term).astype(jnp.bfloat16)
                sent.append(arrive(out.at[:, columns], out_hbm.at[:, columns], out_sems.at[half]))
    for copy in sent:
        copy.wait()


def shards(tokens, cotangent, w_query, w_key, w_value, w_out):
    rows, wide = tokens.shape
    columns = w_query.shape[1]
    heads = columns // DH
    homes = lax.axis_size(HOMES)
    factor = 1.0 / math.sqrt(DH * rows * lax.axis_size(AXES))
    activation = pltpu.VMEM((rows, columns), jnp.bfloat16)
    weight = pltpu.VMEM((wide, columns), jnp.bfloat16)
    whole = pltpu.VMEM((rows, wide), jnp.bfloat16)
    columns_shape = jax.ShapeDtypeStruct((rows, columns), jnp.bfloat16)
    slices_shape = (homes, 2, columns // homes, DH)

    grad_out, query, keys, values, slices = pl.pallas_call(
        project_kernel,
        in_specs=[FAR] * 6,
        out_specs=[FAR] * 4 + [HELD],
        out_shape=[columns_shape] * 4 + [pltpu.VMEM(slices_shape, jnp.bfloat16)],
        scratch_shapes=[whole, pltpu.VMEM((columns, wide), jnp.bfloat16), whole, weight]
        + [pltpu.VMEM((wide, 2 * columns), jnp.bfloat16), activation, activation, pltpu.VMEM((rows, 2 * columns), jnp.bfloat16)]
        + [pltpu.SemaphoreType.DMA((8,)), pltpu.SemaphoreType.DMA((4,))],
        compiler_params=params(56),
        cost_estimate=pl.CostEstimate(
            flops=8 * rows * wide * columns, bytes_accessed=4 * (rows + 2 * columns) * wide, transcendentals=0
        ),
        name="project",
    )(*map(far, (cotangent, w_out, tokens, w_query, w_key, w_value)))
    sums = exclusive_scan(slices)
    part = pl.BlockSpec((rows, PAIR), lambda i: (0, i))
    intra_query, intra_key, intra_value = pl.pallas_call(
        intra_kernel,
        grid=(heads // 2,),
        in_specs=[part] * 4,
        out_specs=[part] * 3,
        out_shape=[columns_shape] * 3,
        compiler_params=params(56),
        cost_estimate=pl.CostEstimate(
            flops=10 * rows * rows * columns, bytes_accessed=14 * rows * columns, transcendentals=0
        ),
        name="intra",
    )(*map(far, (query, keys, values, grad_out)))
    three = pltpu.VMEM((3, rows, columns), jnp.bfloat16)
    return pl.pallas_call(
        functools.partial(finish_kernel, factor),
        in_specs=[FAR] * 6 + [HELD] + [FAR] * 3,
        out_specs=FAR,
        out_shape=jax.ShapeDtypeStruct((rows, wide), jnp.bfloat16),
        scratch_shapes=[
            three, three, pltpu.VMEM((3, wide, columns), jnp.bfloat16), activation,
            pltpu.VMEM((rows, wide), jnp.float32), whole,
            pltpu.SemaphoreType.DMA((12,)), pltpu.SemaphoreType.DMA((2,)),
        ],
        compiler_params=params(56),
        cost_estimate=pl.CostEstimate(
            flops=6 * rows * columns * (wide + DH), bytes_accessed=2 * (6 * rows * columns + 3 * wide * columns),
            transcendentals=0,
        ),
        name="finish",
    )(
        *map(far, (keys, values, grad_out, intra_value, intra_key, intra_query)), held(sums),
        *map(far, (w_value, w_key, w_query)),
    )


def solution(mesh):
    groups, places = mesh.devices.shape
    mesh = jax.sharding.Mesh(mesh.devices.reshape(groups, 2, places // 2), AXES)
    placed = (P(AXES, None), P(AXES, None), P(), P(), P(), P())
    return jax.shard_map(
        shards, mesh=mesh, in_specs=placed, out_specs=P(AXES, None), check_vma=False
    )
```

```python
import functools
import math

import jax
import jax.numpy as jnp
from jax import lax
from jax.experimental import pallas as pl
from jax.experimental.pallas import tpu as pltpu
from jax.sharding import PartitionSpec as P

DH = 128
PAIR = 2 * DH
AXES = ("ctxa", "half", "rest")
HOMES = ("ctxa", "rest")
ROWS_ROWS = (((0,), (0,)), ((), ()))
LAST_LAST = (((1,), (1,)), ((), ()))
PLAIN = (((1,), (0,)), ((), ()))


def mul(left, right, dims=PLAIN):
    return lax.dot_general(left, right, dims, preferred_element_type=jnp.float32)


HELD = pl.BlockSpec(memory_space=pltpu.VMEM)
FAR = pl.BlockSpec(memory_space=pl.ANY)


def held(array):
    return pltpu.with_memory_space_constraint(array, pltpu.VMEM)


def far(array):
    return pltpu.with_memory_space_constraint(array, pltpu.HBM)


def params(mebibytes):
    return pltpu.CompilerParams(vmem_limit_bytes=mebibytes << 20)


def my_home():
    return lax.axis_index("ctxa") * lax.axis_size("rest") + lax.axis_index("rest")


def exchange(pieces):
    homes = len(pieces)
    return [
        lax.ppermute(piece, HOMES, [(place, place ^ k) for place in range(homes)]) if k else piece
        for k, piece in enumerate(pieces)
    ]


def sums_kernel(*refs):
    *pieces, slices_ref, sums_ref = refs
    me = my_home()
    for k, piece in enumerate(pieces):
        slices_ref[me ^ k] = piece[...]
    groups = sums_ref.shape[0]
    each = slices_ref.shape[0] // groups
    for group in range(groups):
        total = slices_ref[group * each].astype(jnp.float32)
        for place in range(1, each):
            total = total + slices_ref[group * each + place].astype(jnp.float32)
        sums_ref[group] = total.astype(jnp.bfloat16)


def scan_kernel(slices_ref, others_ref, *refs):
    *pieces, out_ref = refs
    groups = others_ref.shape[0]
    each = slices_ref.shape[0] // groups
    upper = lax.axis_index("half") == 1
    for kind in range(2):
        total = jnp.zeros(slices_ref.shape[2:], jnp.float32)
        for lap in range(groups):
            group = groups - 1 - lap if kind else lap
            other = others_ref[group, kind].astype(jnp.float32)
            ahead = jnp.where(upper, 0.0, other) if kind else jnp.where(upper, other, 0.0)
            total = total + ahead
            for step in range(each):
                place = group * each + (each - 1 - step if kind else step)
                out_ref[place, kind] = total.astype(jnp.bfloat16)
                total = total + slices_ref[place, kind].astype(jnp.float32)
            total = total + (other - ahead)
    me = my_home()
    for k, piece in enumerate(pieces):
        piece[...] = out_ref[me ^ k]


def exclusive_scan(pieces):
    homes = len(pieces)
    piece = pieces[0].shape
    slices, sums = pl.pallas_call(
        sums_kernel,
        in_specs=[HELD] * homes,
        out_specs=[HELD] * 2,
        out_shape=[pltpu.VMEM((homes,) + piece, jnp.bfloat16), pltpu.VMEM((lax.axis_size("ctxa"),) + piece, jnp.bfloat16)],
        compiler_params=params(8),
        name="sums",
    )(*map(held, exchange(pieces)))
    others = lax.ppermute(sums, "half", [(0, 1), (1, 0)])
    return exchange(pl.pallas_call(
        scan_kernel,
        in_specs=[HELD, HELD],
        out_specs=[HELD] * homes,
        out_shape=[pltpu.VMEM(piece, jnp.bfloat16)] * homes,
        scratch_shapes=[pltpu.VMEM((homes,) + piece, jnp.bfloat16)],
        compiler_params=params(8),
        name="scan",
    )(held(slices), held(others)))


def arrive(source, target, sem):
    copy = pltpu.make_async_copy(source, target, sem)
    copy.start()
    return copy


def halves(extent):
    return [pl.ds(half * (extent // 2), extent // 2) for half in range(2)]


def project_kernel(
    cotangent_hbm, w_out_hbm, tokens_hbm, w_query_hbm, w_key_hbm, w_value_hbm,
    grad_out_hbm, query_hbm, keys_hbm, values_hbm, *refs,
):
    *pieces, slices_ref, cotangent, w_out, tokens, w_query, w_both, grad_out, query, both, sems, out_sems = refs
    columns = query.shape[1]
    keys_at, values_at = pl.ds(0, columns), pl.ds(columns, columns)
    parts = halves(tokens.shape[1])
    first = []
    for half, lanes in enumerate(parts):
        first.append([
            arrive(cotangent_hbm.at[:, lanes], cotangent.at[:, lanes], sems.at[2 * half]),
            arrive(w_out_hbm.at[:, lanes], w_out.at[:, lanes], sems.at[2 * half + 1]),
        ])
    second = [arrive(tokens_hbm, tokens, sems.at[4]), arrive(w_query_hbm, w_query, sems.at[5])]
    third = [
        arrive(w_key_hbm, w_both.at[:, keys_at], sems.at[6]),
        arrive(w_value_hbm, w_both.at[:, values_at], sems.at[7]),
    ]
    total = None
    for lanes, copies in zip(parts, first):
        for copy in copies:
            copy.wait()
        term = mul(cotangent[:, lanes], w_out[:, lanes], LAST_LAST)
        total = term if total is None else total + term
    grad_out[...] = total.astype(jnp.bfloat16)
    sent = [arrive(grad_out, grad_out_hbm, out_sems.at[0])]
    for copy in second:
        copy.wait()
    query[...] = mul(tokens[...], w_query[...]).astype(jnp.bfloat16)
    sent.append(arrive(query, query_hbm, out_sems.at[1]))
    for copy in third:
        copy.wait()
    both[...] = mul(tokens[...], w_both[...]).astype(jnp.bfloat16)
    sent.append(arrive(both.at[:, keys_at], keys_hbm, out_sems.at[2]))
    sent.append(arrive(both.at[:, values_at], values_hbm, out_sems.at[3]))
    rows = slices_ref.shape[2]
    for head in range(columns // DH):
        lanes = pl.ds(head * DH, DH)
        for kind, (left, right) in enumerate((
            (both[:, lanes], both[:, pl.ds(columns + head * DH, DH)]), (query[:, lanes], grad_out[:, lanes])
        )):
            state = mul(left, right, ROWS_ROWS).astype(jnp.bfloat16)
            for part in range(DH // rows):
                slices_ref[head * (DH // rows) + part, kind] = state[part * rows : (part + 1) * rows]
    me = my_home()
    for k, piece in enumerate(pieces):
        piece[...] = slices_ref[me ^ k]
    for copy in sent:
        copy.wait()


def intra_kernel(query_ref, keys_ref, values_ref, grad_out_ref, grad_query_ref, grad_key_ref, grad_value_ref):
    rows = query_ref.shape[0]
    step = min(rows, 256)
    blocks = [pl.ds(at * step, step) for at in range(rows // step)]
    below = lax.broadcasted_iota(jnp.int32, (step, step), 0) >= lax.broadcasted_iota(jnp.int32, (step, step), 1)

    def score(left, right, masked):
        found = mul(left, right, LAST_LAST)
        return (jnp.where(below, found, 0.0) if masked else found).astype(jnp.bfloat16)

    for head in range(query_ref.shape[1] // DH):
        lanes = pl.ds(head * DH, DH)
        query_t = query_ref[:, lanes].T
        grad_out_t = grad_out_ref[:, lanes].T
        key_sums, value_sums = [None] * len(blocks), [None] * len(blocks)
        for t, mine in enumerate(blocks):
            span = slice(t * step, (t + 1) * step)
            query_sum = None
            for s, theirs in enumerate(blocks[: t + 1]):
                probe = score(grad_out_ref[mine, lanes], values_ref[theirs, lanes], s == t)
                attend = score(query_ref[mine, lanes], keys_ref[theirs, lanes], s == t)
                term = mul(probe, keys_ref[theirs, lanes])
                query_sum = term if query_sum is None else query_sum + term
                term = mul(query_t[:, span], probe)
                key_sums[s] = term if key_sums[s] is None else key_sums[s] + term
                term = mul(grad_out_t[:, span], attend)
                value_sums[s] = term if value_sums[s] is None else value_sums[s] + term
            grad_query_ref[mine, lanes] = query_sum.astype(jnp.bfloat16)
        for s, theirs in enumerate(blocks):
            grad_key_ref[theirs, lanes] = key_sums[s].T.astype(jnp.bfloat16)
            grad_value_ref[theirs, lanes] = value_sums[s].T.astype(jnp.bfloat16)


def finish_kernel(
    factor, keys_hbm, values_hbm, grad_out_hbm, intra_value_hbm, intra_key_hbm, intra_query_hbm,
    w_value_hbm, w_key_hbm, w_query_hbm, *refs,
):
    *pieces, out_hbm, sums_ref, lefts, intras, weights, grads, total, out, sems, out_sems = refs
    wide = w_query_hbm.shape[0]
    heads = keys_hbm.shape[1] // DH
    per_head = sums_ref.shape[0] // heads
    parts = halves(wide)
    copies = []
    for kind, (left_hbm, intra_hbm, weight_hbm) in enumerate((
        (keys_hbm, intra_value_hbm, w_value_hbm),
        (values_hbm, intra_key_hbm, w_key_hbm),
        (grad_out_hbm, intra_query_hbm, w_query_hbm),
    )):
        here = [
            arrive(left_hbm, lefts.at[kind], sems.at[4 * kind]),
            arrive(intra_hbm, intras.at[kind], sems.at[4 * kind + 1]),
        ]
        for half, columns in enumerate(parts):
            here.append(arrive(weight_hbm.at[columns], weights.at[kind, columns], sems.at[4 * kind + 2 + half]))
        copies.append(here)
    me = my_home()
    for k, piece in enumerate(pieces):
        sums_ref[me ^ k] = piece[...]
    sent = []
    for kind in range(3):
        copies[kind][0].wait()
        copies[kind][1].wait()
        for head in range(heads):
            lanes = pl.ds(head * DH, DH)
            state = sums_ref[pl.ds(head * per_head, per_head), 0 if kind == 2 else 1].reshape(DH, DH)
            inter = mul(lefts[kind, :, lanes], state, PLAIN if kind == 0 else LAST_LAST)
            grads[:, lanes] = (factor * (inter + intras[kind, :, lanes].astype(jnp.float32))).astype(jnp.bfloat16)
        if kind == 1:
            for copy in copies[kind][2:]:
                copy.wait()
            total[...] += mul(grads[...], weights[kind], LAST_LAST)
            continue
        for half, columns in enumerate(parts):
            copies[kind][2 + half].wait()
            term = mul(grads[...], weights[kind, columns], LAST_LAST)
            if kind == 0:
                total[:, columns] = term
            else:
                out[:, columns] = (total[:, columns] + term).astype(jnp.bfloat16)
                sent.append(arrive(out.at[:, columns], out_hbm.at[:, columns], out_sems.at[half]))
    for copy in sent:
        copy.wait()


def shards(tokens, cotangent, w_query, w_key, w_value, w_out):
    rows, wide = tokens.shape
    columns = w_query.shape[1]
    heads = columns // DH
    homes = lax.axis_size(HOMES)
    factor = 1.0 / math.sqrt(DH * rows * lax.axis_size(AXES))
    activation = pltpu.VMEM((rows, columns), jnp.bfloat16)
    weight = pltpu.VMEM((wide, columns), jnp.bfloat16)
    whole = pltpu.VMEM((rows, wide), jnp.bfloat16)
    columns_shape = jax.ShapeDtypeStruct((rows, columns), jnp.bfloat16)
    slices_shape = (homes, 2, columns // homes, DH)

    grad_out, query, keys, values, *pieces = pl.pallas_call(
        project_kernel,
        in_specs=[FAR] * 6,
        out_specs=[FAR] * 4 + [HELD] * homes,
        out_shape=[columns_shape] * 4 + [pltpu.VMEM(slices_shape[1:], jnp.bfloat16)] * homes,
        scratch_shapes=[pltpu.VMEM(slices_shape, jnp.bfloat16), whole, pltpu.VMEM((columns, wide), jnp.bfloat16), whole, weight]
        + [pltpu.VMEM((wide, 2 * columns), jnp.bfloat16), activation, activation, pltpu.VMEM((rows, 2 * columns), jnp.bfloat16)]
        + [pltpu.SemaphoreType.DMA((8,)), pltpu.SemaphoreType.DMA((4,))],
        compiler_params=params(56),
        cost_estimate=pl.CostEstimate(
            flops=8 * rows * wide * columns, bytes_accessed=4 * (rows + 2 * columns) * wide, transcendentals=0
        ),
        name="project",
    )(*map(far, (cotangent, w_out, tokens, w_query, w_key, w_value)))
    pieces = exclusive_scan(pieces)
    part = pl.BlockSpec((rows, PAIR), lambda i: (0, i))
    intra_query, intra_key, intra_value = pl.pallas_call(
        intra_kernel,
        grid=(heads // 2,),
        in_specs=[part] * 4,
        out_specs=[part] * 3,
        out_shape=[columns_shape] * 3,
        compiler_params=params(56),
        cost_estimate=pl.CostEstimate(
            flops=10 * rows * rows * columns, bytes_accessed=14 * rows * columns, transcendentals=0
        ),
        name="intra",
    )(*map(far, (query, keys, values, grad_out)))
    three = pltpu.VMEM((3, rows, columns), jnp.bfloat16)
    return pl.pallas_call(
        functools.partial(finish_kernel, factor),
        in_specs=[FAR] * 9 + [HELD] * homes,
        out_specs=FAR,
        out_shape=jax.ShapeDtypeStruct((rows, wide), jnp.bfloat16),
        scratch_shapes=[
            pltpu.VMEM(slices_shape, jnp.bfloat16), three, three, pltpu.VMEM((3, wide, columns), jnp.bfloat16), activation,
            pltpu.VMEM((rows, wide), jnp.float32), whole,
            pltpu.SemaphoreType.DMA((12,)), pltpu.SemaphoreType.DMA((2,)),
        ],
        compiler_params=params(56),
        cost_estimate=pl.CostEstimate(
            flops=6 * rows * columns * (wide + DH), bytes_accessed=2 * (6 * rows * columns + 3 * wide * columns),
            transcendentals=0,
        ),
        name="finish",
    )(
        *map(far, (keys, values, grad_out, intra_value, intra_key, intra_query, w_value, w_key, w_query)),
        *map(held, pieces),
    )


def solution(mesh):
    groups, places = mesh.devices.shape
    mesh = jax.sharding.Mesh(mesh.devices.reshape(groups, 2, places // 2), AXES)
    placed = (P(AXES, None), P(AXES, None), P(), P(), P(), P())
    return jax.shard_map(
        shards, mesh=mesh, in_specs=placed, out_specs=P(AXES, None), check_vma=False
    )
```

```python
import functools
import math

import jax
import jax.numpy as jnp
from jax import lax
from jax.experimental import pallas as pl
from jax.experimental.pallas import tpu as pltpu
from jax.sharding import PartitionSpec as P

DH = 128
PAIR = 2 * DH
AXES = ("ctxa", "half", "rest")
ROWS_ROWS = (((0,), (0,)), ((), ()))
LAST_LAST = (((1,), (1,)), ((), ()))
PLAIN = (((1,), (0,)), ((), ()))


def mul(left, right, dims=PLAIN):
    return lax.dot_general(left, right, dims, preferred_element_type=jnp.float32)


HELD = pl.BlockSpec(memory_space=pltpu.VMEM)
FAR = pl.BlockSpec(memory_space=pl.ANY)


def held(array):
    return pltpu.with_memory_space_constraint(array, pltpu.VMEM)


def far(array):
    return pltpu.with_memory_space_constraint(array, pltpu.HBM)


def params(mebibytes):
    return pltpu.CompilerParams(vmem_limit_bytes=mebibytes << 20)


def swap(pieces, axis):
    places = len(pieces)
    swapped = list(pieces)
    for k in reversed(range(1, places)):
        swapped[k] = lax.ppermute(pieces[k], axis, [(place, place ^ k) for place in range(places)])
    return swapped


def group_kernel(*refs):
    places, groups = lax.axis_size("rest"), lax.axis_size("ctxa")
    slices, (slices_ref, sum_ref), sends = refs[:places], refs[places : places + 2], refs[places + 2 :]
    me, group = lax.axis_index("rest"), lax.axis_index("ctxa")
    total = None
    for k, piece in enumerate(slices):
        slices_ref[me ^ k] = piece[...]
        term = piece[...].astype(jnp.float32)
        total = term if total is None else total + term
    sum_ref[...] = total.astype(jnp.bfloat16)
    for k in range(1, groups):
        sends[k - 1][...] = sum_ref[jnp.where(group < (group ^ k), 0, 1)]


def half_kernel(*refs):
    sum_ref, *others, before_ref, cross_ref = refs
    group, upper = lax.axis_index("ctxa"), lax.axis_index("half")
    for kind in range(2):
        total = jnp.zeros(sum_ref.shape[1:], jnp.float32)
        for k, other in enumerate(others):
            ahead = (group ^ (k + 1)) > group if kind else (group ^ (k + 1)) < group
            total = total + jnp.where(ahead, other[...].astype(jnp.float32), 0.0)
        before_ref[kind] = total.astype(jnp.bfloat16)
        added = jnp.where(upper == kind, sum_ref[kind].astype(jnp.float32), 0.0)
        cross_ref[kind] = (total + added).astype(jnp.bfloat16)


def scan_kernel(slices_ref, before_ref, cross_ref, *refs):
    *pieces, out_ref = refs[1:]
    places = slices_ref.shape[0]
    for kind in range(2):
        total = before_ref[kind].astype(jnp.float32) + cross_ref[kind].astype(jnp.float32)
        for step in range(places):
            place = places - 1 - step if kind else step
            out_ref[place, kind] = total.astype(jnp.bfloat16)
            total = total + slices_ref[place, kind].astype(jnp.float32)
    me = lax.axis_index("rest")
    for k, piece in enumerate(pieces):
        piece[...] = out_ref[me ^ k]


def exclusive_scan(pieces, work):
    places, groups = len(pieces), lax.axis_size("ctxa")
    piece = pltpu.VMEM(pieces[0].shape, jnp.bfloat16)
    several = pltpu.VMEM((places,) + pieces[0].shape, jnp.bfloat16)
    slices, total, *sends = pl.pallas_call(
        group_kernel,
        in_specs=[HELD] * places,
        out_specs=[HELD] * (groups + 1),
        out_shape=[several, piece] + [pltpu.VMEM(pieces[0].shape[1:], jnp.bfloat16)] * (groups - 1),
        compiler_params=params(8),
        name="group",
    )(*map(held, swap(pieces, "rest")))
    before, cross = pl.pallas_call(
        half_kernel,
        in_specs=[HELD] * groups,
        out_specs=[HELD] * 2,
        out_shape=[piece] * 2,
        compiler_params=params(8),
        name="half",
    )(held(total), *map(held, swap([None] + sends, "ctxa")[1:]))
    done = work(before)
    cross = lax.ppermute(cross, "half", [(0, 1), (1, 0)])
    pieces = pl.pallas_call(
        scan_kernel,
        in_specs=[HELD] * 3 + [FAR],
        out_specs=[HELD] * places,
        out_shape=[piece] * places,
        scratch_shapes=[several],
        compiler_params=params(8),
        name="scan",
    )(held(slices), held(before), held(cross), far(done[0]))
    return swap(pieces, "rest"), done, pieces[0]


def arrive(source, target, sem):
    copy = pltpu.make_async_copy(source, target, sem)
    copy.start()
    return copy


def halves(extent):
    return [pl.ds(half * (extent // 2), extent // 2) for half in range(2)]


def project_kernel(
    cotangent_hbm, w_out_hbm, tokens_hbm, w_query_hbm, w_key_hbm, w_value_hbm,
    grad_out_hbm, query_hbm, keys_hbm, values_hbm, *refs,
):
    *pieces, slices_ref, cotangent, w_out, tokens, w_query, w_both, grad_out, query, both, sems, out_sems = refs
    columns = query.shape[1]
    keys_at, values_at = pl.ds(0, columns), pl.ds(columns, columns)
    parts = halves(tokens.shape[1])
    first = []
    for half, lanes in enumerate(parts):
        first.append([
            arrive(cotangent_hbm.at[:, lanes], cotangent.at[:, lanes], sems.at[2 * half]),
            arrive(w_out_hbm.at[:, lanes], w_out.at[:, lanes], sems.at[2 * half + 1]),
        ])
    second = [arrive(tokens_hbm, tokens, sems.at[4]), arrive(w_query_hbm, w_query, sems.at[5])]
    third = [
        arrive(w_key_hbm, w_both.at[:, keys_at], sems.at[6]),
        arrive(w_value_hbm, w_both.at[:, values_at], sems.at[7]),
    ]
    total = None
    for lanes, copies in zip(parts, first):
        for copy in copies:
            copy.wait()
        term = mul(cotangent[:, lanes], w_out[:, lanes], LAST_LAST)
        total = term if total is None else total + term
    grad_out[...] = total.astype(jnp.bfloat16)
    sent = [arrive(grad_out, grad_out_hbm, out_sems.at[0])]
    for copy in second:
        copy.wait()
    query[...] = mul(tokens[...], w_query[...]).astype(jnp.bfloat16)
    sent.append(arrive(query, query_hbm, out_sems.at[1]))
    for copy in third:
        copy.wait()
    both[...] = mul(tokens[...], w_both[...]).astype(jnp.bfloat16)
    sent.append(arrive(both.at[:, keys_at], keys_hbm, out_sems.at[2]))
    sent.append(arrive(both.at[:, values_at], values_hbm, out_sems.at[3]))
    for head in range(columns // DH):
        lanes = pl.ds(head * DH, DH)
        for kind, (left, right) in enumerate((
            (both[:, lanes], both[:, pl.ds(columns + head * DH, DH)]), (query[:, lanes], grad_out[:, lanes])
        )):
            slices_ref[kind, pl.ds(head * DH, DH)] = mul(left, right, ROWS_ROWS).astype(jnp.bfloat16)
    me = lax.axis_index("rest")
    rows = columns // len(pieces)
    for k, piece in enumerate(pieces):
        piece[...] = slices_ref[:, pl.ds(pl.multiple_of((me ^ k) * rows, rows), rows)]
    for copy in sent:
        copy.wait()


def intra_kernel(query_ref, keys_ref, values_ref, grad_out_ref, _, grad_query_ref, grad_key_ref, grad_value_ref):
    rows = query_ref.shape[0]
    step = min(rows, 256)
    blocks = [pl.ds(at * step, step) for at in range(rows // step)]
    below = lax.broadcasted_iota(jnp.int32, (step, step), 0) >= lax.broadcasted_iota(jnp.int32, (step, step), 1)

    def score(left, right, masked):
        found = mul(left, right, LAST_LAST)
        return (jnp.where(below, found, 0.0) if masked else found).astype(jnp.bfloat16)

    for head in range(query_ref.shape[1] // DH):
        lanes = pl.ds(head * DH, DH)
        query_t = query_ref[:, lanes].T
        grad_out_t = grad_out_ref[:, lanes].T
        key_sums, value_sums = [None] * len(blocks), [None] * len(blocks)
        for t, mine in enumerate(blocks):
            span = slice(t * step, (t + 1) * step)
            query_sum = None
            for s, theirs in enumerate(blocks[: t + 1]):
                probe = score(grad_out_ref[mine, lanes], values_ref[theirs, lanes], s == t)
                attend = score(query_ref[mine, lanes], keys_ref[theirs, lanes], s == t)
                term = mul(probe, keys_ref[theirs, lanes])
                query_sum = term if query_sum is None else query_sum + term
                term = mul(query_t[:, span], probe)
                key_sums[s] = term if key_sums[s] is None else key_sums[s] + term
                term = mul(grad_out_t[:, span], attend)
                value_sums[s] = term if value_sums[s] is None else value_sums[s] + term
            grad_query_ref[mine, lanes] = query_sum.astype(jnp.bfloat16)
        for s, theirs in enumerate(blocks):
            grad_key_ref[theirs, lanes] = key_sums[s].T.astype(jnp.bfloat16)
            grad_value_ref[theirs, lanes] = value_sums[s].T.astype(jnp.bfloat16)


def finish_kernel(
    factor, keys_hbm, values_hbm, grad_out_hbm, low_value_hbm, low_key_hbm, low_query_hbm,
    high_value_hbm, high_key_hbm, high_query_hbm, w_value_hbm, w_key_hbm, w_query_hbm, *refs,
):
    *pieces, out_hbm, sums_ref, lefts, intras, weights, grads, total, out, sems, out_sems = refs
    wide = w_query_hbm.shape[0]
    heads = keys_hbm.shape[1] // DH
    lower = low_query_hbm.shape[1]
    parts = halves(wide)
    copies = []
    for kind, (left_hbm, low_hbm, high_hbm, weight_hbm) in enumerate((
        (keys_hbm, low_value_hbm, high_value_hbm, w_value_hbm),
        (values_hbm, low_key_hbm, high_key_hbm, w_key_hbm),
        (grad_out_hbm, low_query_hbm, high_query_hbm, w_query_hbm),
    )):
        here = [
            arrive(left_hbm, lefts.at[kind], sems.at[5 * kind]),
            arrive(low_hbm, intras.at[kind, :, pl.ds(0, lower)], sems.at[5 * kind + 1]),
            arrive(high_hbm, intras.at[kind, :, pl.ds(lower, heads * DH - lower)], sems.at[5 * kind + 2]),
        ]
        for half, columns in enumerate(parts):
            here.append(arrive(weight_hbm.at[columns], weights.at[kind, columns], sems.at[5 * kind + 3 + half]))
        copies.append(here)
    me = lax.axis_index("rest")
    rows = heads * DH // len(pieces)
    for k, piece in enumerate(pieces):
        sums_ref[:, pl.ds(pl.multiple_of((me ^ k) * rows, rows), rows)] = piece[...]
    sent = []
    for kind in range(3):
        for copy in copies[kind][:3]:
            copy.wait()
        for head in range(heads):
            lanes = pl.ds(head * DH, DH)
            state = sums_ref[0 if kind == 2 else 1, lanes]
            inter = mul(lefts[kind, :, lanes], state, PLAIN if kind == 0 else LAST_LAST)
            grads[:, lanes] = (factor * (inter + intras[kind, :, lanes].astype(jnp.float32))).astype(jnp.bfloat16)
        if kind == 1:
            for copy in copies[kind][3:]:
                copy.wait()
            total[...] += mul(grads[...], weights[kind], LAST_LAST)
            continue
        for half, columns in enumerate(parts):
            copies[kind][3 + half].wait()
            term = mul(grads[...], weights[kind, columns], LAST_LAST)
            if kind == 0:
                total[:, columns] = term
            else:
                out[:, columns] = (total[:, columns] + term).astype(jnp.bfloat16)
                sent.append(arrive(out.at[:, columns], out_hbm.at[:, columns], out_sems.at[half]))
    for copy in sent:
        copy.wait()


def shards(tokens, cotangent, w_query, w_key, w_value, w_out):
    rows, wide = tokens.shape
    columns = w_query.shape[1]
    heads = columns // DH
    places = lax.axis_size("rest")
    factor = 1.0 / math.sqrt(DH * rows * lax.axis_size(AXES))
    activation = pltpu.VMEM((rows, columns), jnp.bfloat16)
    weight = pltpu.VMEM((wide, columns), jnp.bfloat16)
    whole = pltpu.VMEM((rows, wide), jnp.bfloat16)
    columns_shape = jax.ShapeDtypeStruct((rows, columns), jnp.bfloat16)
    states = pltpu.VMEM((2, columns, DH), jnp.bfloat16)

    grad_out, query, keys, values, *pieces = pl.pallas_call(
        project_kernel,
        in_specs=[FAR] * 6,
        out_specs=[FAR] * 4 + [HELD] * places,
        out_shape=[columns_shape] * 4 + [pltpu.VMEM((2, columns // places, DH), jnp.bfloat16)] * places,
        scratch_shapes=[states, whole, pltpu.VMEM((columns, wide), jnp.bfloat16), whole, weight]
        + [pltpu.VMEM((wide, 2 * columns), jnp.bfloat16), activation, activation, pltpu.VMEM((rows, 2 * columns), jnp.bfloat16)]
        + [pltpu.SemaphoreType.DMA((8,)), pltpu.SemaphoreType.DMA((4,))],
        compiler_params=params(56),
        cost_estimate=pl.CostEstimate(
            flops=8 * rows * wide * columns, bytes_accessed=4 * (rows + 2 * columns) * wide, transcendentals=0
        ),
        name="project",
    )(*map(far, (cotangent, w_out, tokens, w_query, w_key, w_value)))

    def intra(first, count, after):
        source = pl.BlockSpec((rows, PAIR), lambda i: (0, i + first // 2))
        part = pl.BlockSpec((rows, PAIR), lambda i: (0, i))
        return pl.pallas_call(
            intra_kernel,
            grid=(count // 2,),
            in_specs=[source] * 4 + [HELD],
            out_specs=[part] * 3,
            out_shape=[jax.ShapeDtypeStruct((rows, count * DH), jnp.bfloat16)] * 3,
            compiler_params=params(56),
            cost_estimate=pl.CostEstimate(
                flops=10 * rows * rows * count * DH, bytes_accessed=14 * rows * count * DH, transcendentals=0
            ),
            name="intra",
        )(*map(far, (query, keys, values, grad_out)), held(after))

    some = heads // 4 * 2
    pieces, low, after = exclusive_scan(pieces, lambda array: intra(0, some, array))
    high = intra(some, heads - some, after)
    three = pltpu.VMEM((3, rows, columns), jnp.bfloat16)
    return pl.pallas_call(
        functools.partial(finish_kernel, factor),
        in_specs=[FAR] * 12 + [HELD] * places,
        out_specs=FAR,
        out_shape=jax.ShapeDtypeStruct((rows, wide), jnp.bfloat16),
        scratch_shapes=[
            states, three, three, pltpu.VMEM((3, wide, columns), jnp.bfloat16), activation,
            pltpu.VMEM((rows, wide), jnp.float32), whole,
            pltpu.SemaphoreType.DMA((15,)), pltpu.SemaphoreType.DMA((2,)),
        ],
        compiler_params=params(56),
        cost_estimate=pl.CostEstimate(
            flops=6 * rows * columns * (wide + DH), bytes_accessed=2 * (6 * rows * columns + 3 * wide * columns),
            transcendentals=0,
        ),
        name="finish",
    )(
        *map(far, (keys, values, grad_out, *low[::-1], *high[::-1], w_value, w_key, w_query)),
        *map(held, pieces),
    )


def solution(mesh):
    groups, places = mesh.devices.shape
    mesh = jax.sharding.Mesh(mesh.devices.reshape(groups, 2, places // 2), AXES)
    placed = (P(AXES, None), P(AXES, None), P(), P(), P(), P())
    return jax.shard_map(
        shards, mesh=mesh, in_specs=placed, out_specs=P(AXES, None), check_vma=False
    )
```

```python
import functools
import math

import jax
import jax.numpy as jnp
from jax import lax
from jax.experimental import pallas as pl
from jax.experimental.pallas import tpu as pltpu
from jax.sharding import PartitionSpec as P

DH = 128
PAIR = 2 * DH
AXES = ("ctxa", "half", "rest")
ROWS_ROWS = (((0,), (0,)), ((), ()))
LAST_LAST = (((1,), (1,)), ((), ()))
PLAIN = (((1,), (0,)), ((), ()))


def mul(left, right, dims=PLAIN):
    return lax.dot_general(left, right, dims, preferred_element_type=jnp.float32)


HELD = pl.BlockSpec(memory_space=pltpu.VMEM)
FAR = pl.BlockSpec(memory_space=pl.ANY)


def held(array):
    return pltpu.with_memory_space_constraint(array, pltpu.VMEM)


def far(array):
    return pltpu.with_memory_space_constraint(array, pltpu.HBM)


def params(mebibytes):
    return pltpu.CompilerParams(vmem_limit_bytes=mebibytes << 20)


def swap(pieces, axis):
    places = len(pieces)
    swapped = list(pieces)
    for k in reversed(range(1, places)):
        swapped[k] = lax.ppermute(pieces[k], axis, [(place, place ^ k) for place in range(places)])
    return swapped


def group_kernel(*refs):
    places, groups = lax.axis_size("rest"), lax.axis_size("ctxa")
    slices, (slices_ref, sum_ref), sends = refs[:places], refs[places : places + 2], refs[places + 2 :]
    me, group = lax.axis_index("rest"), lax.axis_index("ctxa")
    total = None
    for k, piece in enumerate(slices):
        slices_ref[me ^ k] = piece[...]
        term = piece[...].astype(jnp.float32)
        total = term if total is None else total + term
    sum_ref[...] = total.astype(jnp.bfloat16)
    for k in range(1, groups):
        sends[k - 1][...] = sum_ref[jnp.where(group < (group ^ k), 0, 1)]


def half_kernel(*refs):
    sum_ref, *others, before_ref, cross_ref = refs
    group, upper = lax.axis_index("ctxa"), lax.axis_index("half")
    for kind in range(2):
        total = jnp.zeros(sum_ref.shape[1:], jnp.float32)
        for k, other in enumerate(others):
            ahead = (group ^ (k + 1)) > group if kind else (group ^ (k + 1)) < group
            total = total + jnp.where(ahead, other[...].astype(jnp.float32), 0.0)
        before_ref[kind] = total.astype(jnp.bfloat16)
        added = jnp.where(upper == kind, sum_ref[kind].astype(jnp.float32), 0.0)
        cross_ref[kind] = (total + added).astype(jnp.bfloat16)


def scan_kernel(slices_ref, before_ref, cross_ref, *refs):
    *pieces, out_ref = refs[1:]
    places = slices_ref.shape[0]
    for kind in range(2):
        total = before_ref[kind].astype(jnp.float32) + cross_ref[kind].astype(jnp.float32)
        for step in range(places):
            place = places - 1 - step if kind else step
            out_ref[place, kind] = total.astype(jnp.bfloat16)
            total = total + slices_ref[place, kind].astype(jnp.float32)
    me = lax.axis_index("rest")
    for k, piece in enumerate(pieces):
        piece[...] = out_ref[me ^ k]


def exclusive_scan(pieces, work):
    places, groups = len(pieces), lax.axis_size("ctxa")
    piece = pltpu.VMEM(pieces[0].shape, jnp.bfloat16)
    several = pltpu.VMEM((places,) + pieces[0].shape, jnp.bfloat16)
    slices, total, *sends = pl.pallas_call(
        group_kernel,
        in_specs=[HELD] * places,
        out_specs=[HELD] * (groups + 1),
        out_shape=[several, piece] + [pltpu.VMEM(pieces[0].shape[1:], jnp.bfloat16)] * (groups - 1),
        compiler_params=params(8),
        name="group",
    )(*map(held, swap(pieces, "rest")))
    before, cross = pl.pallas_call(
        half_kernel,
        in_specs=[HELD] * groups,
        out_specs=[HELD] * 2,
        out_shape=[piece] * 2,
        compiler_params=params(8),
        name="half",
    )(held(total), *map(held, swap([None] + sends, "ctxa")[1:]))
    done = work(before)
    cross = lax.ppermute(cross, "half", [(0, 1), (1, 0)])
    pieces = pl.pallas_call(
        scan_kernel,
        in_specs=[HELD] * 4,
        out_specs=[HELD] * places,
        out_shape=[piece] * places,
        scratch_shapes=[several],
        compiler_params=params(8),
        name="scan",
    )(held(slices), held(before), held(cross), held(done[0]))
    return swap(pieces, "rest"), done


def arrive(source, target, sem):
    copy = pltpu.make_async_copy(source, target, sem)
    copy.start()
    return copy


def halves(extent):
    return [pl.ds(half * (extent // 2), extent // 2) for half in range(2)]


def project_kernel(
    cotangent_hbm, w_out_hbm, tokens_hbm, w_query_hbm, w_key_hbm, w_value_hbm,
    grad_out, query, both, w_query, w_both, *refs,
):
    *pieces, slices_ref, cotangent, w_out, tokens, sems = refs
    columns = query.shape[1]
    keys_at, values_at = pl.ds(0, columns), pl.ds(columns, columns)
    parts = halves(tokens.shape[1])
    first = []
    for half, lanes in enumerate(parts):
        first.append([
            arrive(cotangent_hbm.at[:, lanes], cotangent.at[:, lanes], sems.at[2 * half]),
            arrive(w_out_hbm.at[:, lanes], w_out.at[:, lanes], sems.at[2 * half + 1]),
        ])
    second = [arrive(tokens_hbm, tokens, sems.at[4]), arrive(w_query_hbm, w_query, sems.at[5])]
    third = [
        arrive(w_key_hbm, w_both.at[:, keys_at], sems.at[6]),
        arrive(w_value_hbm, w_both.at[:, values_at], sems.at[7]),
    ]
    total = None
    for lanes, copies in zip(parts, first):
        for copy in copies:
            copy.wait()
        term = mul(cotangent[:, lanes], w_out[:, lanes], LAST_LAST)
        total = term if total is None else total + term
    grad_out[...] = total.astype(jnp.bfloat16)
    for copy in second:
        copy.wait()
    query[...] = mul(tokens[...], w_query[...]).astype(jnp.bfloat16)
    for copy in third:
        copy.wait()
    both[...] = mul(tokens[...], w_both[...]).astype(jnp.bfloat16)
    for head in range(columns // DH):
        lanes = pl.ds(head * DH, DH)
        for kind, (left, right) in enumerate((
            (both[:, lanes], both[:, pl.ds(columns + head * DH, DH)]), (query[:, lanes], grad_out[:, lanes])
        )):
            slices_ref[kind, pl.ds(head * DH, DH)] = mul(left, right, ROWS_ROWS).astype(jnp.bfloat16)
    me = lax.axis_index("rest")
    rows = columns // len(pieces)
    for k, piece in enumerate(pieces):
        piece[...] = slices_ref[:, pl.ds(pl.multiple_of((me ^ k) * rows, rows), rows)]


def intra_kernel(query_ref, both_ref, grad_out_ref, _, grad_query_ref, grad_key_ref, grad_value_ref):
    columns = query_ref.shape[1]
    rows = query_ref.shape[0]
    step = min(rows, 256)
    blocks = [pl.ds(at * step, step) for at in range(rows // step)]
    below = lax.broadcasted_iota(jnp.int32, (step, step), 0) >= lax.broadcasted_iota(jnp.int32, (step, step), 1)

    def score(left, right, masked):
        found = mul(left, right, LAST_LAST)
        return (jnp.where(below, found, 0.0) if masked else found).astype(jnp.bfloat16)

    for head in range(columns // DH):
        lanes, values_at = pl.ds(head * DH, DH), pl.ds(columns + head * DH, DH)
        query_t = query_ref[:, lanes].T
        grad_out_t = grad_out_ref[:, lanes].T
        key_sums, value_sums = [None] * len(blocks), [None] * len(blocks)
        for t, mine in enumerate(blocks):
            span = slice(t * step, (t + 1) * step)
            query_sum = None
            for s, theirs in enumerate(blocks[: t + 1]):
                probe = score(grad_out_ref[mine, lanes], both_ref[theirs, values_at], s == t)
                attend = score(query_ref[mine, lanes], both_ref[theirs, lanes], s == t)
                term = mul(probe, both_ref[theirs, lanes])
                query_sum = term if query_sum is None else query_sum + term
                term = mul(query_t[:, span], probe)
                key_sums[s] = term if key_sums[s] is None else key_sums[s] + term
                term = mul(grad_out_t[:, span], attend)
                value_sums[s] = term if value_sums[s] is None else value_sums[s] + term
            grad_query_ref[mine, lanes] = query_sum.astype(jnp.bfloat16)
        for s, theirs in enumerate(blocks):
            grad_key_ref[theirs, lanes] = key_sums[s].T.astype(jnp.bfloat16)
            grad_value_ref[theirs, lanes] = value_sums[s].T.astype(jnp.bfloat16)


def finish_kernel(
    factor, query_part, key_part, value_part, both, grad_out, w_query, w_both, *refs,
):
    *pieces, out_hbm, sums_ref, grads, total, out, sems = refs
    columns = grad_out.shape[1]
    keys_at, values_at = pl.ds(0, columns), pl.ds(columns, columns)
    parts = halves(w_query.shape[0])
    me = lax.axis_index("rest")
    rows = columns // len(pieces)
    for k, piece in enumerate(pieces):
        sums_ref[:, pl.ds(pl.multiple_of((me ^ k) * rows, rows), rows)] = piece[...]
    sent = []
    for kind, (part, left, weight) in enumerate((
        (value_part, both.at[:, keys_at], w_both.at[:, values_at]),
        (key_part, both.at[:, values_at], w_both.at[:, keys_at]),
        (query_part, grad_out, w_query),
    )):
        for head in range(columns // DH):
            lanes = pl.ds(head * DH, DH)
            state = sums_ref[0 if kind == 2 else 1, lanes]
            inter = mul(left[:, lanes], state, PLAIN if kind == 0 else LAST_LAST)
            grads[:, lanes] = (factor * (inter + part[:, lanes].astype(jnp.float32))).astype(jnp.bfloat16)
        if kind == 0:
            total[...] = mul(grads[...], weight[...], LAST_LAST)
        elif kind == 1:
            total[...] += mul(grads[...], weight[...], LAST_LAST)
        else:
            for half, rows in enumerate(parts):
                term = mul(grads[...], weight[rows], LAST_LAST)
                out[:, rows] = (total[:, rows] + term).astype(jnp.bfloat16)
                sent.append(arrive(out.at[:, rows], out_hbm.at[:, rows], sems.at[half]))
    for copy in sent:
        copy.wait()


def shards(tokens, cotangent, w_query, w_key, w_value, w_out):
    rows, wide = tokens.shape
    columns = w_query.shape[1]
    places = lax.axis_size("rest")
    factor = 1.0 / math.sqrt(DH * rows * lax.axis_size(AXES))
    activation = pltpu.VMEM((rows, columns), jnp.bfloat16)
    whole = pltpu.VMEM((rows, wide), jnp.bfloat16)
    states = pltpu.VMEM((2, columns, DH), jnp.bfloat16)

    def cost(flops, bytes_accessed):
        return pl.CostEstimate(flops=flops, bytes_accessed=bytes_accessed, transcendentals=0)

    grad_out, query, both, w_query, w_both, *pieces = pl.pallas_call(
        project_kernel,
        in_specs=[FAR] * 6,
        out_specs=[HELD] * (5 + places),
        out_shape=[
            activation, activation, pltpu.VMEM((rows, 2 * columns), jnp.bfloat16),
            pltpu.VMEM((wide, columns), jnp.bfloat16), pltpu.VMEM((wide, 2 * columns), jnp.bfloat16),
        ] + [pltpu.VMEM((2, columns // places, DH), jnp.bfloat16)] * places,
        scratch_shapes=[states, whole, pltpu.VMEM((columns, wide), jnp.bfloat16), whole, pltpu.SemaphoreType.DMA((8,))],
        compiler_params=params(32),
        cost_estimate=cost(8 * rows * wide * columns, 4 * (rows + 2 * columns) * wide),
        name="project",
    )(*map(far, (cotangent, w_out, tokens, w_query, w_key, w_value)))

    def intra(after):
        return pl.pallas_call(
            intra_kernel,
            in_specs=[HELD] * 4,
            out_specs=[HELD] * 3,
            out_shape=[activation] * 3,
            compiler_params=params(16),
            cost_estimate=cost(10 * rows * rows * columns, 14 * rows * columns),
            name="intra",
        )(*map(held, (query, both, grad_out, after)))

    pieces, done = exclusive_scan(pieces, intra)
    return pl.pallas_call(
        functools.partial(finish_kernel, factor),
        in_specs=[HELD] * (7 + places),
        out_specs=FAR,
        out_shape=jax.ShapeDtypeStruct((rows, wide), jnp.bfloat16),
        scratch_shapes=[states, activation, pltpu.VMEM((rows, wide), jnp.float32), whole, pltpu.SemaphoreType.DMA((2,))],
        compiler_params=params(32),
        cost_estimate=cost(6 * rows * columns * (wide + DH), 2 * (6 * rows * columns + 3 * wide * columns)),
        name="finish",
    )(*map(held, (*done, both, grad_out, w_query, w_both, *pieces)))


def solution(mesh):
    groups, places = mesh.devices.shape
    mesh = jax.sharding.Mesh(mesh.devices.reshape(groups, 2, places // 2), AXES)
    placed = (P(AXES, None), P(AXES, None), P(), P(), P(), P())
    return jax.shard_map(
        shards, mesh=mesh, in_specs=placed, out_specs=P(AXES, None), check_vma=False
    )
```

```python
import functools
import math

import jax
import jax.numpy as jnp
from jax import lax
from jax.experimental import pallas as pl
from jax.experimental.pallas import tpu as pltpu
from jax.sharding import PartitionSpec as P

DH = 128
AXES = ("ctxa", "half", "rest")
ROWS_ROWS = (((0,), (0,)), ((), ()))
LAST_LAST = (((1,), (1,)), ((), ()))
PLAIN = (((1,), (0,)), ((), ()))


def mul(left, right, dims=PLAIN):
    return lax.dot_general(left, right, dims, preferred_element_type=jnp.float32)


HELD = pl.BlockSpec(memory_space=pltpu.VMEM)
FAR = pl.BlockSpec(memory_space=pl.ANY)


def held(array):
    return pltpu.with_memory_space_constraint(array, pltpu.VMEM)


def far(array):
    return pltpu.with_memory_space_constraint(array, pltpu.HBM)


def params(mebibytes):
    return pltpu.CompilerParams(vmem_limit_bytes=mebibytes << 20)


def swap(pieces, axis):
    places = len(pieces)
    swapped = list(pieces)
    for k in reversed(range(1, places)):
        swapped[k] = lax.ppermute(pieces[k], axis, [(place, place ^ k) for place in range(places)])
    return swapped


def group_kernel(*refs):
    places, groups = lax.axis_size("rest"), lax.axis_size("ctxa")
    slices, (slices_ref, sum_ref), sends = refs[:places], refs[places : places + 2], refs[places + 2 :]
    me, group = lax.axis_index("rest"), lax.axis_index("ctxa")
    total = None
    for k, piece in enumerate(slices):
        slices_ref[me ^ k] = piece[...]
        term = piece[...].astype(jnp.float32)
        total = term if total is None else total + term
    sum_ref[...] = total.astype(jnp.bfloat16)
    for k in range(1, groups):
        sends[k - 1][...] = sum_ref[jnp.where(group < (group ^ k), 0, 1)]


def half_kernel(*refs):
    sum_ref, *others, before_ref, cross_ref = refs
    group, upper = lax.axis_index("ctxa"), lax.axis_index("half")
    for kind in range(2):
        total = jnp.zeros(sum_ref.shape[1:], jnp.float32)
        for k, other in enumerate(others):
            ahead = (group ^ (k + 1)) > group if kind else (group ^ (k + 1)) < group
            total = total + jnp.where(ahead, other[...].astype(jnp.float32), 0.0)
        before_ref[kind] = total.astype(jnp.bfloat16)
        added = jnp.where(upper == kind, sum_ref[kind].astype(jnp.float32), 0.0)
        cross_ref[kind] = (total + added).astype(jnp.bfloat16)


def scan_kernel(slices_ref, before_ref, cross_ref, *refs):
    *pieces, out_ref = refs[1:]
    places = slices_ref.shape[0]
    for kind in range(2):
        total = before_ref[kind].astype(jnp.float32) + cross_ref[kind].astype(jnp.float32)
        for step in range(places):
            place = places - 1 - step if kind else step
            out_ref[place, kind] = total.astype(jnp.bfloat16)
            total = total + slices_ref[place, kind].astype(jnp.float32)
    me = lax.axis_index("rest")
    for k, piece in enumerate(pieces):
        piece[...] = out_ref[me ^ k]


def exclusive_scan(pieces, work):
    places, groups = len(pieces), lax.axis_size("ctxa")
    piece = pltpu.VMEM(pieces[0].shape, jnp.bfloat16)
    several = pltpu.VMEM((places,) + pieces[0].shape, jnp.bfloat16)
    slices, total, *sends = pl.pallas_call(
        group_kernel,
        in_specs=[HELD] * places,
        out_specs=[HELD] * (groups + 1),
        out_shape=[several, piece] + [pltpu.VMEM(pieces[0].shape[1:], jnp.bfloat16)] * (groups - 1),
        compiler_params=params(8),
        name="group",
    )(*map(held, swap(pieces, "rest")))
    before, cross = pl.pallas_call(
        half_kernel,
        in_specs=[HELD] * groups,
        out_specs=[HELD] * 2,
        out_shape=[piece] * 2,
        compiler_params=params(8),
        name="half",
    )(held(total), *map(held, swap([None] + sends, "ctxa")[1:]))
    done = work(before)
    cross = lax.ppermute(cross, "half", [(0, 1), (1, 0)])
    pieces = pl.pallas_call(
        scan_kernel,
        in_specs=[HELD] * 4,
        out_specs=[HELD] * places,
        out_shape=[piece] * places,
        scratch_shapes=[several],
        compiler_params=params(8),
        name="scan",
    )(held(slices), held(before), held(cross), held(done))
    return swap(pieces, "rest"), done


def arrive(source, target, sem):
    copy = pltpu.make_async_copy(source, target, sem)
    copy.start()
    return copy


def halves(extent):
    return [pl.ds(half * (extent // 2), extent // 2) for half in range(2)]


def states_of(queries, keys, values, grads, state_ref):
    for head in range(state_ref.shape[1] // DH):
        lanes = pl.ds(head * DH, DH)
        for kind, (left, right) in enumerate(((keys, values), (queries, grads))):
            state_ref[kind, lanes] = mul(left[:, lanes], right[:, lanes], ROWS_ROWS).astype(jnp.bfloat16)


def kinds_of(ref, piece, width):
    return [ref.at[:, pl.ds((3 * piece + kind) * width, width)] for kind in range(3)]


def others_kernel(
    cotangent_hbm, w_out_hbm, tokens_hbm, w_query_hbm, w_key_hbm, w_value_hbm,
    cotangent, tokens, w_own, w_all, grad_out, projected, *refs,
):
    *states, w_out, sems = refs
    places = len(states) + 1
    width = w_own.shape[0]
    me = lax.axis_index("rest")
    homes = [pl.ds(pl.multiple_of((me ^ k) * width, width), width) for k in range(places)]
    count = [0]

    def bring(source, target):
        count[0] += 1
        return arrive(source, target, sems.at[count[0] - 1])

    parts = halves(tokens.shape[1])
    first = []
    for lanes in parts:
        here = [bring(cotangent_hbm.at[:, lanes], cotangent.at[:, lanes])]
        for k in range(1, places):
            here.append(bring(w_out_hbm.at[homes[k], lanes], w_out.at[pl.ds((k - 1) * width, width), lanes]))
        first.append(here)
    tokens_copy = bring(tokens_hbm, tokens)
    copies = {}
    for k in list(range(1, places)) + [0]:
        if k == 0:
            own = bring(w_out_hbm.at[homes[0]], w_own)
        copies[k] = [
            bring(source.at[:, homes[k]], target)
            for source, target in zip((w_query_hbm, w_key_hbm, w_value_hbm), kinds_of(w_all, k, width))
        ]
    total = None
    for lanes, here in zip(parts, first):
        for copy in here:
            copy.wait()
        term = mul(cotangent[:, lanes], w_out[:, lanes], LAST_LAST)
        total = term if total is None else total + term
    grad_out[...] = total.astype(jnp.bfloat16)
    tokens_copy.wait()
    for k in range(1, places):
        for copy in copies[k]:
            copy.wait()
        product = mul(tokens[...], w_all[:, pl.ds(3 * k * width, 3 * width)])
        projected[:, pl.ds(3 * (k - 1) * width, 3 * width)] = product.astype(jnp.bfloat16)
        states_of(*kinds_of(projected, k - 1, width), grad_out.at[:, pl.ds((k - 1) * width, width)], states[k - 1])
    for copy in [own] + copies[0]:
        copy.wait()


def own_kernel(cotangent, tokens, w_own, w_all, grad_out, projected, state):
    width = w_own.shape[0]
    grad_out[...] = mul(cotangent[...], w_own[...], LAST_LAST).astype(jnp.bfloat16)
    projected[...] = mul(tokens[...], w_all[:, pl.ds(0, 3 * width)]).astype(jnp.bfloat16)
    states_of(*kinds_of(projected, 0, width), grad_out, state)


def operands_of(piece, own, others, own_grad, others_grad):
    width = own_grad.shape[1]
    if piece == 0:
        return (*kinds_of(own, 0, width), own_grad)
    return (*kinds_of(others, piece - 1, width), others_grad.at[:, pl.ds((piece - 1) * width, width)])


def intra_kernel(own, others, own_grad, others_grad, _, parts):
    rows, width = own_grad.shape
    step = min(rows, 256)
    blocks = [pl.ds(at * step, step) for at in range(rows // step)]
    below = lax.broadcasted_iota(jnp.int32, (step, step), 0) >= lax.broadcasted_iota(jnp.int32, (step, step), 1)

    def score(left, right, masked):
        found = mul(left, right, LAST_LAST)
        return (jnp.where(below, found, 0.0) if masked else found).astype(jnp.bfloat16)

    for piece in range(parts.shape[1] // (3 * width)):
        query_ref, keys_ref, values_ref, grad_out_ref = operands_of(piece, own, others, own_grad, others_grad)
        grad_query_ref, grad_key_ref, grad_value_ref = kinds_of(parts, piece, width)
        for head in range(width // DH):
            lanes = pl.ds(head * DH, DH)
            query_t = query_ref[:, lanes].T
            grad_out_t = grad_out_ref[:, lanes].T
            key_sums, value_sums = [None] * len(blocks), [None] * len(blocks)
            for t, mine in enumerate(blocks):
                span = slice(t * step, (t + 1) * step)
                query_sum = None
                for s, theirs in enumerate(blocks[: t + 1]):
                    probe = score(grad_out_ref[mine, lanes], values_ref[theirs, lanes], s == t)
                    attend = score(query_ref[mine, lanes], keys_ref[theirs, lanes], s == t)
                    term = mul(probe, keys_ref[theirs, lanes])
                    query_sum = term if query_sum is None else query_sum + term
                    term = mul(query_t[:, span], probe)
                    key_sums[s] = term if key_sums[s] is None else key_sums[s] + term
                    term = mul(grad_out_t[:, span], attend)
                    value_sums[s] = term if value_sums[s] is None else value_sums[s] + term
                grad_query_ref[mine, lanes] = query_sum.astype(jnp.bfloat16)
            for s, theirs in enumerate(blocks):
                grad_key_ref[theirs, lanes] = key_sums[s].T.astype(jnp.bfloat16)
                grad_value_ref[theirs, lanes] = value_sums[s].T.astype(jnp.bfloat16)


def finish_kernel(factor, begin, end, last, parts, own, others, own_grad, others_grad, w_all, *refs):
    sums, refs = refs[: end - begin], refs[end - begin :]
    width = own_grad.shape[1]
    if last:
        total, out_hbm, grads, out, sems = refs
    elif begin:
        total, out, grads = refs
    else:
        out, grads = refs
    for at, piece in enumerate(range(begin, end)):
        _, keys, values, grad_out = operands_of(piece, own, others, own_grad, others_grad)
        for head in range(width // DH):
            lanes = pl.ds(head * DH, DH)
            prior, later = sums[at][0, lanes], sums[at][1, lanes]
            inters = (
                mul(grad_out[:, lanes], prior, LAST_LAST),
                mul(values[:, lanes], later, LAST_LAST),
                mul(keys[:, lanes], later),
            )
            for inter, part, grad in zip(inters, kinds_of(parts, piece, width), kinds_of(grads, at, width)):
                grad[:, lanes] = (factor * (inter + part[:, lanes].astype(jnp.float32))).astype(jnp.bfloat16)
    columns = pl.ds(3 * begin * width, 3 * (end - begin) * width)
    if not last:
        term = mul(grads[...], w_all[:, columns], LAST_LAST)
        out[...] = total[...] + term if begin else term
        return
    sent = []
    for half, rows in enumerate(halves(w_all.shape[0])):
        term = mul(grads[...], w_all[rows, columns], LAST_LAST)
        out[:, rows] = (total[:, rows] + term).astype(jnp.bfloat16)
        sent.append(arrive(out.at[:, rows], out_hbm.at[:, rows], sems.at[half]))
    for copy in sent:
        copy.wait()


def shards(tokens, cotangent, w_query, w_key, w_value, w_out):
    rows, wide = tokens.shape
    columns = w_query.shape[1]
    places = lax.axis_size("rest")
    width = columns // places
    factor = 1.0 / math.sqrt(DH * rows * lax.axis_size(AXES))

    def vmem(*shape):
        return pltpu.VMEM(shape, jnp.bfloat16)

    def cost(flops, bytes_accessed):
        return pl.CostEstimate(flops=flops, bytes_accessed=bytes_accessed, transcendentals=0)

    piece = vmem(2, width, DH)
    cotangent, tokens, w_own, w_all, others_grad, others, *pieces = pl.pallas_call(
        others_kernel,
        in_specs=[FAR] * 6,
        out_specs=[HELD] * (5 + places),
        out_shape=[
            vmem(rows, wide), vmem(rows, wide), vmem(width, wide), vmem(wide, 3 * columns),
            vmem(rows, columns - width), vmem(rows, 3 * (columns - width)),
        ] + [piece] * (places - 1),
        scratch_shapes=[vmem(columns - width, wide), pltpu.SemaphoreType.DMA((6 * places + 2,))],
        compiler_params=params(24),
        cost_estimate=cost(8 * rows * wide * (columns - width), 4 * (rows + 2 * columns) * wide),
        name="project_others",
    )(*map(far, (cotangent, w_out, tokens, w_query, w_key, w_value)))
    own_grad, own, own_piece = pl.pallas_call(
        own_kernel,
        in_specs=[HELD] * 4,
        out_specs=[HELD] * 3,
        out_shape=[vmem(rows, width), vmem(rows, 3 * width), piece],
        compiler_params=params(16),
        cost_estimate=cost(8 * rows * wide * width, 4 * (rows + 2 * width) * wide),
        name="project_own",
    )(*map(held, (cotangent, tokens, w_own, w_all)))
    operands = own, others, own_grad, others_grad

    def intra(after):
        return pl.pallas_call(
            intra_kernel,
            in_specs=[HELD] * 5,
            out_specs=HELD,
            out_shape=vmem(rows, 3 * columns),
            compiler_params=params(16),
            cost_estimate=cost(10 * rows * rows * columns, 14 * rows * columns),
            name="intra",
        )(*map(held, (*operands, after)))

    pieces, parts = exclusive_scan([own_piece] + pieces, intra)

    def finish(begin, end, total):
        last = begin == 1
        wait = [] if total is None else [total]
        summed = (end - begin) * 3 * width
        return pl.pallas_call(
            functools.partial(finish_kernel, factor, begin, end, last),
            in_specs=[HELD] * (6 + end - begin + len(wait)),
            out_specs=FAR if last else HELD,
            out_shape=jax.ShapeDtypeStruct((rows, wide), jnp.bfloat16) if last else pltpu.VMEM((rows, wide), jnp.float32),
            scratch_shapes=[vmem(rows, summed)] + ([vmem(rows, wide), pltpu.SemaphoreType.DMA((2,))] if last else []),
            compiler_params=params(20),
            cost_estimate=cost(2 * rows * summed * (wide + DH), 2 * (rows + wide) * summed),
            name="finish",
        )(*map(held, (parts, *operands, w_all, *pieces[begin:end], *wait)))

    total = finish(0, 1, None)
    if places > 2:
        total = finish(2, places, total)
    return finish(1, 2, total)


def solution(mesh):
    groups, places = mesh.devices.shape
    mesh = jax.sharding.Mesh(mesh.devices.reshape(groups, 2, places // 2), AXES)
    placed = (P(AXES, None), P(AXES, None), P(), P(), P(), P())
    return jax.shard_map(
        shards, mesh=mesh, in_specs=placed, out_specs=P(AXES, None), check_vma=False
    )
```

```python
import functools
import math

import jax
import jax.numpy as jnp
from jax import lax
from jax.experimental import pallas as pl
from jax.experimental.pallas import tpu as pltpu
from jax.sharding import PartitionSpec as P

DH = 128
AXES = ("ctxa", "half", "rest")
ROWS_ROWS = (((0,), (0,)), ((), ()))
LAST_LAST = (((1,), (1,)), ((), ()))
PLAIN = (((1,), (0,)), ((), ()))


def mul(left, right, dims=PLAIN):
    return lax.dot_general(left, right, dims, preferred_element_type=jnp.float32)


HELD = pl.BlockSpec(memory_space=pltpu.VMEM)
FAR = pl.BlockSpec(memory_space=pl.ANY)


def held(array):
    return pltpu.with_memory_space_constraint(array, pltpu.VMEM)


def far(array):
    return pltpu.with_memory_space_constraint(array, pltpu.HBM)


def params(mebibytes):
    return pltpu.CompilerParams(vmem_limit_bytes=mebibytes << 20)


def swap(pieces, axis):
    places = len(pieces)
    swapped = list(pieces)
    for k in reversed(range(1, places)):
        swapped[k] = lax.ppermute(pieces[k], axis, [(place, place ^ k) for place in range(places)])
    return swapped


def group_kernel(*refs):
    places, groups = lax.axis_size("rest"), lax.axis_size("ctxa")
    slices, (slices_ref, sum_ref), sends = refs[:places], refs[places : places + 2], refs[places + 2 :]
    me, group = lax.axis_index("rest"), lax.axis_index("ctxa")
    total = None
    for k, piece in enumerate(slices):
        slices_ref[me ^ k] = piece[...]
        term = piece[...].astype(jnp.float32)
        total = term if total is None else total + term
    sum_ref[...] = total.astype(jnp.bfloat16)
    for k in range(1, groups):
        sends[k - 1][...] = sum_ref[jnp.where(group < (group ^ k), 0, 1)]


def half_kernel(*refs):
    sum_ref, *others, before_ref, cross_ref = refs
    group, upper = lax.axis_index("ctxa"), lax.axis_index("half")
    for kind in range(2):
        total = jnp.zeros(sum_ref.shape[1:], jnp.float32)
        for k, other in enumerate(others):
            ahead = (group ^ (k + 1)) > group if kind else (group ^ (k + 1)) < group
            total = total + jnp.where(ahead, other[...].astype(jnp.float32), 0.0)
        before_ref[kind] = total.astype(jnp.bfloat16)
        added = jnp.where(upper == kind, sum_ref[kind].astype(jnp.float32), 0.0)
        cross_ref[kind] = (total + added).astype(jnp.bfloat16)


def scan_kernel(slices_ref, before_ref, cross_ref, *refs):
    *pieces, out_ref = refs[1:]
    places = slices_ref.shape[0]
    for kind in range(2):
        total = before_ref[kind].astype(jnp.float32) + cross_ref[kind].astype(jnp.float32)
        for step in range(places):
            place = places - 1 - step if kind else step
            out_ref[place, kind] = total.astype(jnp.bfloat16)
            total = total + slices_ref[place, kind].astype(jnp.float32)
    me = lax.axis_index("rest")
    for k, piece in enumerate(pieces):
        piece[...] = out_ref[me ^ k]


def exclusive_scan(pieces, work):
    places, groups = len(pieces), lax.axis_size("ctxa")
    piece = pltpu.VMEM(pieces[0].shape, jnp.bfloat16)
    several = pltpu.VMEM((places,) + pieces[0].shape, jnp.bfloat16)
    slices, total, *sends = pl.pallas_call(
        group_kernel,
        in_specs=[HELD] * places,
        out_specs=[HELD] * (groups + 1),
        out_shape=[several, piece] + [pltpu.VMEM(pieces[0].shape[1:], jnp.bfloat16)] * (groups - 1),
        compiler_params=params(8),
        name="group",
    )(*map(held, swap(pieces, "rest")))
    before, cross = pl.pallas_call(
        half_kernel,
        in_specs=[HELD] * groups,
        out_specs=[HELD] * 2,
        out_shape=[piece] * 2,
        compiler_params=params(8),
        name="half",
    )(held(total), *map(held, swap([None] + sends, "ctxa")[1:]))
    done = work(before)
    cross = lax.ppermute(cross, "half", [(0, 1), (1, 0)])
    pieces = pl.pallas_call(
        scan_kernel,
        in_specs=[HELD] * 4,
        out_specs=[HELD] * places,
        out_shape=[piece] * places,
        scratch_shapes=[several],
        compiler_params=params(8),
        name="scan",
    )(held(slices), held(before), held(cross), held(done))
    return swap(pieces, "rest"), done


def arrive(source, target, sem):
    copy = pltpu.make_async_copy(source, target, sem)
    copy.start()
    return copy


def halves(extent):
    return [pl.ds(half * (extent // 2), extent // 2) for half in range(2)]


def states_of(queries, keys, values, grads, state_ref):
    for head in range(state_ref.shape[1] // DH):
        lanes = pl.ds(head * DH, DH)
        for kind, (left, right) in enumerate(((keys, values), (queries, grads))):
            state_ref[kind, lanes] = mul(left[:, lanes], right[:, lanes], ROWS_ROWS).astype(jnp.bfloat16)


def kinds_of(ref, piece, width):
    return [ref.at[:, pl.ds((3 * piece + kind) * width, width)] for kind in range(3)]


def others_kernel(
    cotangent_hbm, w_out_hbm, tokens_hbm, w_query_hbm, w_key_hbm, w_value_hbm,
    cotangent, tokens, w_others, grad_out, projected, *refs,
):
    *states, w_out, sems = refs
    places = len(states) + 1
    width = grad_out.shape[1] // (places - 1)
    me = lax.axis_index("rest")
    homes = [pl.ds(pl.multiple_of((me ^ k) * width, width), width) for k in range(places)]
    count = [0]

    def bring(source, target):
        count[0] += 1
        return arrive(source, target, sems.at[count[0] - 1])

    parts = halves(tokens.shape[1])
    first = []
    for lanes in parts:
        here = [bring(cotangent_hbm.at[:, lanes], cotangent.at[:, lanes])]
        for k in range(1, places):
            here.append(bring(w_out_hbm.at[homes[k], lanes], w_out.at[pl.ds((k - 1) * width, width), lanes]))
        first.append(here)
    tokens_copy = bring(tokens_hbm, tokens)
    copies = {}
    for k in range(1, places):
        copies[k] = [
            bring(source.at[:, homes[k]], target)
            for source, target in zip((w_query_hbm, w_key_hbm, w_value_hbm), kinds_of(w_others, k - 1, width))
        ]
    total = None
    for lanes, here in zip(parts, first):
        for copy in here:
            copy.wait()
        term = mul(cotangent[:, lanes], w_out[:, lanes], LAST_LAST)
        total = term if total is None else total + term
    grad_out[...] = total.astype(jnp.bfloat16)
    tokens_copy.wait()
    for k in range(1, places):
        for copy in copies[k]:
            copy.wait()
        product = mul(tokens[...], w_others[:, pl.ds(3 * (k - 1) * width, 3 * width)])
        projected[:, pl.ds(3 * (k - 1) * width, 3 * width)] = product.astype(jnp.bfloat16)
        states_of(*kinds_of(projected, k - 1, width), grad_out.at[:, pl.ds((k - 1) * width, width)], states[k - 1])


def own_kernel(
    cotangent, tokens, w_out_hbm, w_query_hbm, w_key_hbm, w_value_hbm, w_own, grad_out, projected, state, w_out, sems,
):
    width = w_out.shape[0]
    home = pl.ds(pl.multiple_of(lax.axis_index("rest") * width, width), width)
    w_out_copy = arrive(w_out_hbm.at[home], w_out, sems.at[3])
    copies = [
        arrive(source.at[:, home], target, sems.at[at])
        for at, (source, target) in enumerate(zip((w_query_hbm, w_key_hbm, w_value_hbm), kinds_of(w_own, 0, width)))
    ]
    w_out_copy.wait()
    grad_out[...] = mul(cotangent[...], w_out[...], LAST_LAST).astype(jnp.bfloat16)
    for copy, weight, target in zip(copies, kinds_of(w_own, 0, width), kinds_of(projected, 0, width)):
        copy.wait()
        target[...] = mul(tokens[...], weight[...]).astype(jnp.bfloat16)
    states_of(*kinds_of(projected, 0, width), grad_out, state)


def operands_of(piece, own, others, own_grad, others_grad):
    width = own_grad.shape[1]
    if piece == 0:
        return (*kinds_of(own, 0, width), own_grad)
    return (*kinds_of(others, piece - 1, width), others_grad.at[:, pl.ds((piece - 1) * width, width)])


def intra_kernel(own, others, own_grad, others_grad, _, parts):
    rows, width = own_grad.shape
    step = min(rows, 256)
    blocks = [pl.ds(at * step, step) for at in range(rows // step)]
    below = lax.broadcasted_iota(jnp.int32, (step, step), 0) >= lax.broadcasted_iota(jnp.int32, (step, step), 1)

    def score(left, right, masked):
        found = mul(left, right, LAST_LAST)
        return (jnp.where(below, found, 0.0) if masked else found).astype(jnp.bfloat16)

    for piece in range(parts.shape[1] // (3 * width)):
        query_ref, keys_ref, values_ref, grad_out_ref = operands_of(piece, own, others, own_grad, others_grad)
        grad_query_ref, grad_key_ref, grad_value_ref = kinds_of(parts, piece, width)
        for head in range(width // DH):
            lanes = pl.ds(head * DH, DH)
            query_t = query_ref[:, lanes].T
            grad_out_t = grad_out_ref[:, lanes].T
            key_sums, value_sums = [None] * len(blocks), [None] * len(blocks)
            for t, mine in enumerate(blocks):
                span = slice(t * step, (t + 1) * step)
                query_sum = None
                for s, theirs in enumerate(blocks[: t + 1]):
                    probe = score(grad_out_ref[mine, lanes], values_ref[theirs, lanes], s == t)
                    attend = score(query_ref[mine, lanes], keys_ref[theirs, lanes], s == t)
                    term = mul(probe, keys_ref[theirs, lanes])
                    query_sum = term if query_sum is None else query_sum + term
                    term = mul(query_t[:, span], probe)
                    key_sums[s] = term if key_sums[s] is None else key_sums[s] + term
                    term = mul(grad_out_t[:, span], attend)
                    value_sums[s] = term if value_sums[s] is None else value_sums[s] + term
                grad_query_ref[mine, lanes] = query_sum.astype(jnp.bfloat16)
            for s, theirs in enumerate(blocks):
                grad_key_ref[theirs, lanes] = key_sums[s].T.astype(jnp.bfloat16)
                grad_value_ref[theirs, lanes] = value_sums[s].T.astype(jnp.bfloat16)


def finish_kernel(factor, piece, last, *refs):
    if piece:
        total, *refs = refs
    parts, own, others, own_grad, others_grad, weight, sums, *refs = refs
    width = own_grad.shape[1]
    if last:
        out_hbm, grads, out, sems = refs
    else:
        out, grads = refs
    _, keys, values, grad_out = operands_of(piece, own, others, own_grad, others_grad)
    for head in range(width // DH):
        lanes = pl.ds(head * DH, DH)
        prior, later = sums[0, lanes], sums[1, lanes]
        inters = (
            mul(grad_out[:, lanes], prior, LAST_LAST),
            mul(values[:, lanes], later, LAST_LAST),
            mul(keys[:, lanes], later),
        )
        for inter, part, grad in zip(inters, kinds_of(parts, piece, width), kinds_of(grads, 0, width)):
            grad[:, lanes] = (factor * (inter + part[:, lanes].astype(jnp.float32))).astype(jnp.bfloat16)
    columns = pl.ds(3 * max(piece - 1, 0) * width, 3 * width)
    if not last:
        term = mul(grads[...], weight[:, columns], LAST_LAST)
        out[...] = total[...] + term if piece else term
        return
    sent = []
    for half, rows in enumerate(halves(weight.shape[0])):
        term = mul(grads[...], weight[rows, columns], LAST_LAST)
        out[:, rows] = (total[:, rows] + term).astype(jnp.bfloat16)
        sent.append(arrive(out.at[:, rows], out_hbm.at[:, rows], sems.at[half]))
    for copy in sent:
        copy.wait()


def shards(tokens, cotangent, w_query, w_key, w_value, w_out):
    rows, wide = tokens.shape
    columns = w_query.shape[1]
    places = lax.axis_size("rest")
    width = columns // places
    factor = 1.0 / math.sqrt(DH * rows * lax.axis_size(AXES))

    def vmem(*shape):
        return pltpu.VMEM(shape, jnp.bfloat16)

    def cost(flops, bytes_accessed):
        return pl.CostEstimate(flops=flops, bytes_accessed=bytes_accessed, transcendentals=0)

    piece = vmem(2, width, DH)
    near_cotangent, near_tokens, w_others, others_grad, others, *pieces = pl.pallas_call(
        others_kernel,
        in_specs=[FAR] * 6,
        out_specs=[HELD] * (4 + places),
        out_shape=[
            vmem(rows, wide), vmem(rows, wide), vmem(wide, 3 * (columns - width)),
            vmem(rows, columns - width), vmem(rows, 3 * (columns - width)),
        ] + [piece] * (places - 1),
        scratch_shapes=[vmem(columns - width, wide), pltpu.SemaphoreType.DMA((6 * places + 2,))],
        compiler_params=params(24),
        cost_estimate=cost(8 * rows * wide * (columns - width), 4 * (rows + 2 * columns) * wide),
        name="project_others",
    )(*map(far, (cotangent, w_out, tokens, w_query, w_key, w_value)))
    w_own, own_grad, own, own_piece = pl.pallas_call(
        own_kernel,
        in_specs=[HELD] * 2 + [FAR] * 4,
        out_specs=[HELD] * 4,
        out_shape=[vmem(wide, 3 * width), vmem(rows, width), vmem(rows, 3 * width), piece],
        scratch_shapes=[vmem(width, wide), pltpu.SemaphoreType.DMA((4,))],
        compiler_params=params(16),
        cost_estimate=cost(8 * rows * wide * width, 8 * wide * width),
        name="project_own",
    )(*map(held, (near_cotangent, near_tokens)), *map(far, (w_out, w_query, w_key, w_value)))
    operands = own, others, own_grad, others_grad

    def intra(after):
        return pl.pallas_call(
            intra_kernel,
            in_specs=[HELD] * 5,
            out_specs=HELD,
            out_shape=vmem(rows, 3 * columns),
            compiler_params=params(16),
            cost_estimate=cost(10 * rows * rows * columns, 14 * rows * columns),
            name="intra",
        )(*map(held, (*operands, after)))

    pieces, parts = exclusive_scan([own_piece] + pieces, intra)

    total = []
    for k in range(places):
        last = k == places - 1
        total = [pl.pallas_call(
            functools.partial(finish_kernel, factor, k, last),
            in_specs=[HELD] * (7 + len(total)),
            out_specs=FAR if last else HELD,
            out_shape=jax.ShapeDtypeStruct((rows, wide), jnp.bfloat16) if last else pltpu.VMEM((rows, wide), jnp.float32),
            scratch_shapes=[vmem(rows, 3 * width)] + ([vmem(rows, wide), pltpu.SemaphoreType.DMA((2,))] if last else []),
            compiler_params=params(20),
            cost_estimate=cost(6 * rows * width * (wide + DH), 6 * (rows + wide) * width),
            name="finish",
        )(*map(held, (*total, parts, *operands, w_others if k else w_own, pieces[k])))]
    return total[0]


def solution(mesh):
    groups, places = mesh.devices.shape
    mesh = jax.sharding.Mesh(mesh.devices.reshape(groups, 2, places // 2), AXES)
    placed = (P(AXES, None), P(AXES, None), P(), P(), P(), P())
    return jax.shard_map(
        shards, mesh=mesh, in_specs=placed, out_specs=P(AXES, None), check_vma=False
    )
```

```python
import functools
import math

import jax
import jax.numpy as jnp
from jax import lax
from jax.experimental import pallas as pl
from jax.experimental.pallas import tpu as pltpu
from jax.sharding import PartitionSpec as P

DH = 128
AXES = ("ctxa", "half", "rest")
ROWS_ROWS = (((0,), (0,)), ((), ()))
LAST_LAST = (((1,), (1,)), ((), ()))
PLAIN = (((1,), (0,)), ((), ()))


def mul(left, right, dims=PLAIN):
    return lax.dot_general(left, right, dims, preferred_element_type=jnp.float32)


HELD = pl.BlockSpec(memory_space=pltpu.VMEM)
FAR = pl.BlockSpec(memory_space=pl.ANY)


def held(array):
    return pltpu.with_memory_space_constraint(array, pltpu.VMEM)


def far(array):
    return pltpu.with_memory_space_constraint(array, pltpu.HBM)


def params(mebibytes):
    return pltpu.CompilerParams(vmem_limit_bytes=mebibytes << 20)


def swap(pieces, axis):
    places = len(pieces)
    swapped = list(pieces)
    for k in reversed(range(1, places)):
        swapped[k] = lax.ppermute(pieces[k], axis, [(place, place ^ k) for place in range(places)])
    return swapped


def group_kernel(*refs):
    places, groups = lax.axis_size("rest"), lax.axis_size("ctxa")
    slices, (slices_ref, sum_ref), sends = refs[:places], refs[places : places + 2], refs[places + 2 :]
    me, group = lax.axis_index("rest"), lax.axis_index("ctxa")
    total = None
    for k, piece in enumerate(slices):
        slices_ref[me ^ k] = piece[...]
        term = piece[...].astype(jnp.float32)
        total = term if total is None else total + term
    sum_ref[...] = total.astype(jnp.bfloat16)
    for k in range(1, groups):
        sends[k - 1][...] = sum_ref[jnp.where(group < (group ^ k), 0, 1)]


def half_kernel(*refs):
    sum_ref, *others, before_ref, cross_ref = refs
    group, upper = lax.axis_index("ctxa"), lax.axis_index("half")
    for kind in range(2):
        total = jnp.zeros(sum_ref.shape[1:], jnp.float32)
        for k, other in enumerate(others):
            ahead = (group ^ (k + 1)) > group if kind else (group ^ (k + 1)) < group
            total = total + jnp.where(ahead, other[...].astype(jnp.float32), 0.0)
        before_ref[kind] = total.astype(jnp.bfloat16)
        added = jnp.where(upper == kind, sum_ref[kind].astype(jnp.float32), 0.0)
        cross_ref[kind] = (total + added).astype(jnp.bfloat16)


def scan_kernel(slices_ref, before_ref, cross_ref, *refs):
    *pieces, out_ref = refs[1:]
    places = slices_ref.shape[0]
    for kind in range(2):
        total = before_ref[kind].astype(jnp.float32) + cross_ref[kind].astype(jnp.float32)
        for step in range(places):
            place = places - 1 - step if kind else step
            out_ref[place, kind] = total.astype(jnp.bfloat16)
            total = total + slices_ref[place, kind].astype(jnp.float32)
    me = lax.axis_index("rest")
    for k, piece in enumerate(pieces):
        piece[...] = out_ref[me ^ k]


def exclusive_scan(pieces, work):
    places, groups = len(pieces), lax.axis_size("ctxa")
    piece = pltpu.VMEM(pieces[0].shape, jnp.bfloat16)
    several = pltpu.VMEM((places,) + pieces[0].shape, jnp.bfloat16)
    slices, total, *sends = pl.pallas_call(
        group_kernel,
        in_specs=[HELD] * places,
        out_specs=[HELD] * (groups + 1),
        out_shape=[several, piece] + [pltpu.VMEM(pieces[0].shape[1:], jnp.bfloat16)] * (groups - 1),
        compiler_params=params(8),
        name="group",
    )(*map(held, swap(pieces, "rest")))
    before, cross = pl.pallas_call(
        half_kernel,
        in_specs=[HELD] * groups,
        out_specs=[HELD] * 2,
        out_shape=[piece] * 2,
        compiler_params=params(8),
        name="half",
    )(held(total), *map(held, swap([None] + sends, "ctxa")[1:]))
    done = work(before)
    cross = lax.ppermute(cross, "half", [(0, 1), (1, 0)])
    pieces = pl.pallas_call(
        scan_kernel,
        in_specs=[HELD] * 4,
        out_specs=[HELD] * places,
        out_shape=[piece] * places,
        scratch_shapes=[several],
        compiler_params=params(8),
        name="scan",
    )(held(slices), held(before), held(cross), held(done))
    return swap(pieces, "rest"), done


def arrive(source, target, sem):
    copy = pltpu.make_async_copy(source, target, sem)
    copy.start()
    return copy


def halves(extent):
    return [pl.ds(half * (extent // 2), extent // 2) for half in range(2)]


def states_of(queries, keys, values, grads, state_ref):
    for head in range(state_ref.shape[1] // DH):
        lanes = pl.ds(head * DH, DH)
        for kind, (left, right) in enumerate(((keys, values), (queries, grads))):
            state_ref[kind, lanes] = mul(left[:, lanes], right[:, lanes], ROWS_ROWS).astype(jnp.bfloat16)


def kinds_of(ref, piece, width):
    return [ref.at[:, pl.ds((3 * piece + kind) * width, width)] for kind in range(3)]


def home_of(k, width):
    return pl.ds(pl.multiple_of((lax.axis_index("rest") ^ k) * width, width), width)


def others_kernel(
    cotangent_hbm, w_out_hbm, tokens_hbm, w_query_hbm, w_key_hbm, w_value_hbm,
    cotangent, tokens, w_own, w_query, w_key, w_value, grad_out, projected, *refs,
):
    *states, w_out, sems = refs
    places = len(states) + 1
    width = w_own.shape[0]
    count = [0]

    def bring(source, target):
        count[0] += 1
        return arrive(source, target, sems.at[count[0] - 1])

    parts = halves(tokens.shape[1])
    first = []
    for lanes in parts:
        here = [bring(cotangent_hbm.at[:, lanes], cotangent.at[:, lanes])]
        for k in range(1, places):
            here.append(bring(w_out_hbm.at[home_of(k, width), lanes], w_out.at[pl.ds((k - 1) * width, width), lanes]))
        first.append(here)
    tokens_copy = bring(tokens_hbm, tokens)
    weights = w_query, w_key, w_value
    copies = [bring(*pair) for pair in zip((w_query_hbm, w_key_hbm, w_value_hbm), weights)]
    own_copy = bring(w_out_hbm.at[home_of(0, width)], w_own)
    total = None
    for lanes, here in zip(parts, first):
        for copy in here:
            copy.wait()
        term = mul(cotangent[:, lanes], w_out[:, lanes], LAST_LAST)
        total = term if total is None else total + term
    grad_out[...] = total.astype(jnp.bfloat16)
    tokens_copy.wait()
    for kind, (copy, weight) in enumerate(zip(copies, weights)):
        copy.wait()
        for k in range(1, places):
            product = mul(tokens[...], weight[:, home_of(k, width)])
            kinds_of(projected, k - 1, width)[kind][...] = product.astype(jnp.bfloat16)
    for k in range(1, places):
        states_of(*kinds_of(projected, k - 1, width), grad_out.at[:, pl.ds((k - 1) * width, width)], states[k - 1])
    own_copy.wait()


def own_kernel(cotangent, tokens, w_own, w_query, w_key, w_value, w_all, grad_out, projected, state):
    width = w_own.shape[0]
    weights = w_query, w_key, w_value
    for k in range(w_query.shape[1] // width):
        for source, target in zip(weights, kinds_of(w_all, k, width)):
            target[...] = source[:, home_of(k, width)]
    grad_out[...] = mul(cotangent[...], w_own[...], LAST_LAST).astype(jnp.bfloat16)
    projected[...] = mul(tokens[...], w_all[:, pl.ds(0, 3 * width)]).astype(jnp.bfloat16)
    states_of(*kinds_of(projected, 0, width), grad_out, state)


def operands_of(piece, own, others, own_grad, others_grad):
    width = own_grad.shape[1]
    if piece == 0:
        return (*kinds_of(own, 0, width), own_grad)
    return (*kinds_of(others, piece - 1, width), others_grad.at[:, pl.ds((piece - 1) * width, width)])


def intra_kernel(own, others, own_grad, others_grad, _, parts):
    rows, width = own_grad.shape
    step = min(rows, 256)
    blocks = [pl.ds(at * step, step) for at in range(rows // step)]
    below = lax.broadcasted_iota(jnp.int32, (step, step), 0) >= lax.broadcasted_iota(jnp.int32, (step, step), 1)

    def score(left, right, masked):
        found = mul(left, right, LAST_LAST)
        return (jnp.where(below, found, 0.0) if masked else found).astype(jnp.bfloat16)

    for piece in range(parts.shape[1] // (3 * width)):
        query_ref, keys_ref, values_ref, grad_out_ref = operands_of(piece, own, others, own_grad, others_grad)
        grad_query_ref, grad_key_ref, grad_value_ref = kinds_of(parts, piece, width)
        for head in range(width // DH):
            lanes = pl.ds(head * DH, DH)
            query_t = query_ref[:, lanes].T
            grad_out_t = grad_out_ref[:, lanes].T
            key_sums, value_sums = [None] * len(blocks), [None] * len(blocks)
            for t, mine in enumerate(blocks):
                span = slice(t * step, (t + 1) * step)
                query_sum = None
                for s, theirs in enumerate(blocks[: t + 1]):
                    probe = score(grad_out_ref[mine, lanes], values_ref[theirs, lanes], s == t)
                    attend = score(query_ref[mine, lanes], keys_ref[theirs, lanes], s == t)
                    term = mul(probe, keys_ref[theirs, lanes])
                    query_sum = term if query_sum is None else query_sum + term
                    term = mul(query_t[:, span], probe)
                    key_sums[s] = term if key_sums[s] is None else key_sums[s] + term
                    term = mul(grad_out_t[:, span], attend)
                    value_sums[s] = term if value_sums[s] is None else value_sums[s] + term
                grad_query_ref[mine, lanes] = query_sum.astype(jnp.bfloat16)
            for s, theirs in enumerate(blocks):
                grad_key_ref[theirs, lanes] = key_sums[s].T.astype(jnp.bfloat16)
                grad_value_ref[theirs, lanes] = value_sums[s].T.astype(jnp.bfloat16)


def finish_kernel(factor, piece, last, *refs):
    if piece:
        total, *refs = refs
    parts, own, others, own_grad, others_grad, weight, sums, *refs = refs
    width = own_grad.shape[1]
    if last:
        out_hbm, grads, out, sems = refs
    else:
        out, grads = refs
    _, keys, values, grad_out = operands_of(piece, own, others, own_grad, others_grad)
    for head in range(width // DH):
        lanes = pl.ds(head * DH, DH)
        prior, later = sums[0, lanes], sums[1, lanes]
        inters = (
            mul(grad_out[:, lanes], prior, LAST_LAST),
            mul(values[:, lanes], later, LAST_LAST),
            mul(keys[:, lanes], later),
        )
        for inter, part, grad in zip(inters, kinds_of(parts, piece, width), kinds_of(grads, 0, width)):
            grad[:, lanes] = (factor * (inter + part[:, lanes].astype(jnp.float32))).astype(jnp.bfloat16)
    columns = pl.ds(3 * piece * width, 3 * width)
    if not last:
        term = mul(grads[...], weight[:, columns], LAST_LAST)
        out[...] = total[...] + term if piece else term
        return
    sent = []
    for half, rows in enumerate(halves(weight.shape[0])):
        term = mul(grads[...], weight[rows, columns], LAST_LAST)
        out[:, rows] = (total[:, rows] + term).astype(jnp.bfloat16)
        sent.append(arrive(out.at[:, rows], out_hbm.at[:, rows], sems.at[half]))
    for copy in sent:
        copy.wait()


def shards(tokens, cotangent, w_query, w_key, w_value, w_out):
    rows, wide = tokens.shape
    columns = w_query.shape[1]
    places = lax.axis_size("rest")
    width = columns // places
    factor = 1.0 / math.sqrt(DH * rows * lax.axis_size(AXES))

    def vmem(*shape):
        return pltpu.VMEM(shape, jnp.bfloat16)

    def cost(flops, bytes_accessed):
        return pl.CostEstimate(flops=flops, bytes_accessed=bytes_accessed, transcendentals=0)

    piece = vmem(2, width, DH)
    weight = vmem(wide, columns)
    found = pl.pallas_call(
        others_kernel,
        in_specs=[FAR] * 6,
        out_specs=[HELD] * (7 + places),
        out_shape=[
            vmem(rows, wide), vmem(rows, wide), vmem(width, wide), weight, weight, weight,
            vmem(rows, columns - width), vmem(rows, 3 * (columns - width)),
        ] + [piece] * (places - 1),
        scratch_shapes=[vmem(columns - width, wide), pltpu.SemaphoreType.DMA((2 * places + 5,))],
        compiler_params=params(16),
        cost_estimate=cost(8 * rows * wide * (columns - width), 4 * (rows + 2 * columns) * wide),
        name="project_others",
    )(*map(far, (cotangent, w_out, tokens, w_query, w_key, w_value)))
    near, (others_grad, others), pieces = found[:6], found[6:8], found[8:]
    w_all, own_grad, own, own_piece = pl.pallas_call(
        own_kernel,
        in_specs=[HELD] * 6,
        out_specs=[HELD] * 4,
        out_shape=[vmem(wide, 3 * columns), vmem(rows, width), vmem(rows, 3 * width), piece],
        compiler_params=params(12),
        cost_estimate=cost(8 * rows * wide * width, 12 * wide * columns),
        name="project_own",
    )(*map(held, near))
    operands = own, others, own_grad, others_grad

    def intra(after):
        return pl.pallas_call(
            intra_kernel,
            in_specs=[HELD] * 5,
            out_specs=HELD,
            out_shape=vmem(rows, 3 * columns),
            compiler_params=params(16),
            cost_estimate=cost(10 * rows * rows * columns, 14 * rows * columns),
            name="intra",
        )(*map(held, (*operands, after)))

    pieces, parts = exclusive_scan([own_piece, *pieces], intra)

    total = []
    for k in range(places):
        last = k == places - 1
        total = [pl.pallas_call(
            functools.partial(finish_kernel, factor, k, last),
            in_specs=[HELD] * (7 + len(total)),
            out_specs=FAR if last else HELD,
            out_shape=jax.ShapeDtypeStruct((rows, wide), jnp.bfloat16) if last else pltpu.VMEM((rows, wide), jnp.float32),
            scratch_shapes=[vmem(rows, 3 * width)] + ([vmem(rows, wide), pltpu.SemaphoreType.DMA((2,))] if last else []),
            compiler_params=params(20),
            cost_estimate=cost(6 * rows * width * (wide + DH), 6 * (rows + wide) * width),
            name="finish",
        )(*map(held, (*total, parts, *operands, w_all, pieces[k])))]
    return total[0]


def solution(mesh):
    groups, places = mesh.devices.shape
    mesh = jax.sharding.Mesh(mesh.devices.reshape(groups, 2, places // 2), AXES)
    placed = (P(AXES, None), P(AXES, None), P(), P(), P(), P())
    return jax.shard_map(
        shards, mesh=mesh, in_specs=placed, out_specs=P(AXES, None), check_vma=False
    )
```

```python
import functools
import math

import jax
import jax.numpy as jnp
from jax import lax
from jax.experimental import pallas as pl
from jax.experimental.pallas import tpu as pltpu
from jax.sharding import PartitionSpec as P

DH = 128
AXES = ("x", "core", "half", "rest")
ROWS_ROWS = (((0,), (0,)), ((), ()))
LAST_LAST = (((1,), (1,)), ((), ()))
PLAIN = (((1,), (0,)), ((), ()))


def mul(left, right, dims=PLAIN):
    return lax.dot_general(left, right, dims, preferred_element_type=jnp.float32)


HELD = pl.BlockSpec(memory_space=pltpu.VMEM)
FAR = pl.BlockSpec(memory_space=pl.ANY)


def held(array):
    return pltpu.with_memory_space_constraint(array, pltpu.VMEM)


def far(array):
    return pltpu.with_memory_space_constraint(array, pltpu.HBM)


def params(mebibytes):
    return pltpu.CompilerParams(vmem_limit_bytes=mebibytes << 20)


def swap(pieces, axis):
    places = len(pieces)
    swapped = list(pieces)
    for k in reversed(range(1, places)):
        swapped[k] = lax.ppermute(pieces[k], axis, [(place, place ^ k) for place in range(places)])
    return swapped


def group_kernel(*refs):
    *slices, slices_ref, sum_ref = refs
    me = lax.axis_index("rest")
    total = None
    for k, piece in enumerate(reversed(slices)):
        slices_ref[me ^ k] = piece[...]
        term = piece[...].astype(jnp.float32)
        total = term if total is None else total + term
    sum_ref[...] = total.astype(jnp.bfloat16)


def chip_kernel(sum_ref, other_ref, *sends):
    chip = lax.axis_index("x")
    for k, send in enumerate(sends):
        kind = jnp.where(chip < (chip ^ (k + 1)), 0, 1)
        send[...] = (sum_ref[kind].astype(jnp.float32) + other_ref[kind].astype(jnp.float32)).astype(jnp.bfloat16)


def half_kernel(sum_ref, other_ref, *refs):
    *chips, before_ref, cross_ref = refs
    chip, core, upper = lax.axis_index("x"), lax.axis_index("core"), lax.axis_index("half")
    for kind in range(2):
        total = jnp.where(core != kind, other_ref[kind].astype(jnp.float32), 0.0)
        for k, other in enumerate(chips):
            ahead = (chip ^ (k + 1)) > chip if kind else (chip ^ (k + 1)) < chip
            total = total + jnp.where(ahead, other[...].astype(jnp.float32), 0.0)
        before_ref[kind] = total.astype(jnp.bfloat16)
        added = jnp.where(upper == kind, sum_ref[kind].astype(jnp.float32), 0.0)
        cross_ref[kind] = (total + added).astype(jnp.bfloat16)


def scan_kernel(slices_ref, before_ref, cross_ref, *refs):
    *pieces, out_ref = refs[1:]
    places = slices_ref.shape[0]
    for kind in range(2):
        total = before_ref[kind].astype(jnp.float32) + cross_ref[kind].astype(jnp.float32)
        for step in range(places):
            place = places - 1 - step if kind else step
            out_ref[place, kind] = total.astype(jnp.bfloat16)
            total = total + slices_ref[place, kind].astype(jnp.float32)
    me = lax.axis_index("rest")
    for k, piece in enumerate(pieces):
        piece[...] = out_ref[me ^ k]


def exclusive_scan(pieces, work):
    places, chips = len(pieces), lax.axis_size("x")
    piece = pltpu.VMEM(pieces[0].shape, jnp.bfloat16)
    several = pltpu.VMEM((places,) + pieces[0].shape, jnp.bfloat16)
    slices, total = pl.pallas_call(
        group_kernel,
        in_specs=[HELD] * places,
        out_specs=[HELD] * 2,
        out_shape=[several, piece],
        compiler_params=params(8),
        name="group",
    )(*map(held, reversed(swap(pieces, "rest"))))
    other = lax.ppermute(total, "core", [(0, 1), (1, 0)])
    sends = pl.pallas_call(
        chip_kernel,
        in_specs=[HELD] * 2,
        out_specs=[HELD] * (chips - 1),
        out_shape=[pltpu.VMEM(pieces[0].shape[1:], jnp.bfloat16)] * (chips - 1),
        compiler_params=params(8),
        name="chip",
    )(held(total), held(other))
    before, cross = pl.pallas_call(
        half_kernel,
        in_specs=[HELD] * (chips + 1),
        out_specs=[HELD] * 2,
        out_shape=[piece] * 2,
        compiler_params=params(8),
        name="half",
    )(held(total), held(other), *map(held, swap([None, *sends], "x")[1:]))
    done = work(before)
    cross = lax.ppermute(cross, "half", [(0, 1), (1, 0)])
    pieces = pl.pallas_call(
        scan_kernel,
        in_specs=[HELD] * 4,
        out_specs=[HELD] * places,
        out_shape=[piece] * places,
        scratch_shapes=[several],
        compiler_params=params(8),
        name="scan",
    )(held(slices), held(before), held(cross), held(done))
    return swap(pieces, "rest"), done


def arrive(source, target, sem):
    copy = pltpu.make_async_copy(source, target, sem)
    copy.start()
    return copy


def halves(extent):
    return [pl.ds(half * (extent // 2), extent // 2) for half in range(2)]


def states_of(queries, keys, values, grads, state_ref):
    for head in range(state_ref.shape[1] // DH):
        lanes = pl.ds(head * DH, DH)
        for kind, (left, right) in enumerate(((keys, values), (queries, grads))):
            state_ref[kind, lanes] = mul(left[:, lanes], right[:, lanes], ROWS_ROWS).astype(jnp.bfloat16)


def kinds_of(ref, piece, width):
    return [ref.at[:, pl.ds((3 * piece + kind) * width, width)] for kind in range(3)]


def home_of(k, width):
    return pl.ds(pl.multiple_of((lax.axis_index("rest") ^ k) * width, width), width)


def others_kernel(
    cotangent_hbm, w_out_hbm, tokens_hbm, w_query_hbm, w_key_hbm, w_value_hbm,
    cotangent, tokens, w_own, w_query, w_key, w_value, grad_out, projected, *refs,
):
    *states, w_out, sems = refs
    places = len(states) + 1
    width = w_own.shape[0]
    count = [0]

    def bring(source, target):
        count[0] += 1
        return arrive(source, target, sems.at[count[0] - 1])

    parts = halves(tokens.shape[1])
    first = []
    for lanes in parts:
        here = [bring(cotangent_hbm.at[:, lanes], cotangent.at[:, lanes])]
        for k in range(1, places):
            here.append(bring(w_out_hbm.at[home_of(k, width), lanes], w_out.at[pl.ds((k - 1) * width, width), lanes]))
        first.append(here)
    tokens_copy = bring(tokens_hbm, tokens)
    weights = w_query, w_key, w_value
    copies = [bring(*pair) for pair in zip((w_query_hbm, w_key_hbm, w_value_hbm), weights)]
    own_copy = bring(w_out_hbm.at[home_of(0, width)], w_own)
    total = None
    for lanes, here in zip(parts, first):
        for copy in here:
            copy.wait()
        term = mul(cotangent[:, lanes], w_out[:, lanes], LAST_LAST)
        total = term if total is None else total + term
    grad_out[...] = total.astype(jnp.bfloat16)
    tokens_copy.wait()
    for kind, (copy, weight) in enumerate(zip(copies, weights)):
        copy.wait()
        for k in range(1, places):
            product = mul(tokens[...], weight[:, home_of(k, width)])
            kinds_of(projected, k - 1, width)[kind][...] = product.astype(jnp.bfloat16)
    for k in range(1, places):
        states_of(*kinds_of(projected, k - 1, width), grad_out.at[:, pl.ds((k - 1) * width, width)], states[k - 1])
    own_copy.wait()


def own_kernel(cotangent, tokens, w_own, w_query, w_key, w_value, w_all, grad_out, projected, state):
    width = w_own.shape[0]
    weights = w_query, w_key, w_value
    for k in range(w_query.shape[1] // width):
        for source, target in zip(weights, kinds_of(w_all, k, width)):
            target[...] = source[:, home_of(k, width)]
    grad_out[...] = mul(cotangent[...], w_own[...], LAST_LAST).astype(jnp.bfloat16)
    projected[...] = mul(tokens[...], w_all[:, pl.ds(0, 3 * width)]).astype(jnp.bfloat16)
    states_of(*kinds_of(projected, 0, width), grad_out, state)


def operands_of(piece, own, others, own_grad, others_grad):
    width = own_grad.shape[1]
    if piece == 0:
        return (*kinds_of(own, 0, width), own_grad)
    return (*kinds_of(others, piece - 1, width), others_grad.at[:, pl.ds((piece - 1) * width, width)])


def intra_kernel(own, others, own_grad, others_grad, _, parts):
    rows, width = own_grad.shape
    step = min(rows, 256)
    blocks = [pl.ds(at * step, step) for at in range(rows // step)]
    below = lax.broadcasted_iota(jnp.int32, (step, step), 0) >= lax.broadcasted_iota(jnp.int32, (step, step), 1)

    def score(left, right, masked):
        found = mul(left, right, LAST_LAST)
        return (jnp.where(below, found, 0.0) if masked else found).astype(jnp.bfloat16)

    for piece in range(parts.shape[1] // (3 * width)):
        query_ref, keys_ref, values_ref, grad_out_ref = operands_of(piece, own, others, own_grad, others_grad)
        grad_query_ref, grad_key_ref, grad_value_ref = kinds_of(parts, piece, width)
        for head in range(width // DH):
            lanes = pl.ds(head * DH, DH)
            query_t = query_ref[:, lanes].T
            grad_out_t = grad_out_ref[:, lanes].T
            key_sums, value_sums = [None] * len(blocks), [None] * len(blocks)
            for t, mine in enumerate(blocks):
                span = slice(t * step, (t + 1) * step)
                query_sum = None
                for s, theirs in enumerate(blocks[: t + 1]):
                    probe = score(grad_out_ref[mine, lanes], values_ref[theirs, lanes], s == t)
                    attend = score(query_ref[mine, lanes], keys_ref[theirs, lanes], s == t)
                    term = mul(probe, keys_ref[theirs, lanes])
                    query_sum = term if query_sum is None else query_sum + term
                    term = mul(query_t[:, span], probe)
                    key_sums[s] = term if key_sums[s] is None else key_sums[s] + term
                    term = mul(grad_out_t[:, span], attend)
                    value_sums[s] = term if value_sums[s] is None else value_sums[s] + term
                grad_query_ref[mine, lanes] = query_sum.astype(jnp.bfloat16)
            for s, theirs in enumerate(blocks):
                grad_key_ref[theirs, lanes] = key_sums[s].T.astype(jnp.bfloat16)
                grad_value_ref[theirs, lanes] = value_sums[s].T.astype(jnp.bfloat16)


def finish_kernel(factor, piece, last, *refs):
    if piece:
        total, *refs = refs
    parts, own, others, own_grad, others_grad, weight, sums, *refs = refs
    width = own_grad.shape[1]
    if last:
        out_hbm, grads, out, sems = refs
    else:
        out, grads = refs
    _, keys, values, grad_out = operands_of(piece, own, others, own_grad, others_grad)
    for head in range(width // DH):
        lanes = pl.ds(head * DH, DH)
        prior, later = sums[0, lanes], sums[1, lanes]
        inters = (
            mul(grad_out[:, lanes], prior, LAST_LAST),
            mul(values[:, lanes], later, LAST_LAST),
            mul(keys[:, lanes], later),
        )
        for inter, part, grad in zip(inters, kinds_of(parts, piece, width), kinds_of(grads, 0, width)):
            grad[:, lanes] = (factor * (inter + part[:, lanes].astype(jnp.float32))).astype(jnp.bfloat16)
    columns = pl.ds(3 * piece * width, 3 * width)
    if not last:
        term = mul(grads[...], weight[:, columns], LAST_LAST)
        out[...] = total[...] + term if piece else term
        return
    sent = []
    for half, rows in enumerate(halves(weight.shape[0])):
        term = mul(grads[...], weight[rows, columns], LAST_LAST)
        out[:, rows] = (total[:, rows] + term).astype(jnp.bfloat16)
        sent.append(arrive(out.at[:, rows], out_hbm.at[:, rows], sems.at[half]))
    for copy in sent:
        copy.wait()


def shards(tokens, cotangent, w_query, w_key, w_value, w_out):
    rows, wide = tokens.shape
    columns = w_query.shape[1]
    places = lax.axis_size("rest")
    width = columns // places
    factor = 1.0 / math.sqrt(DH * rows * lax.axis_size(AXES))

    def vmem(*shape):
        return pltpu.VMEM(shape, jnp.bfloat16)

    def cost(flops, bytes_accessed):
        return pl.CostEstimate(flops=flops, bytes_accessed=bytes_accessed, transcendentals=0)

    piece = vmem(2, width, DH)
    weight = vmem(wide, columns)
    found = pl.pallas_call(
        others_kernel,
        in_specs=[FAR] * 6,
        out_specs=[HELD] * (7 + places),
        out_shape=[
            vmem(rows, wide), vmem(rows, wide), vmem(width, wide), weight, weight, weight,
            vmem(rows, columns - width), vmem(rows, 3 * (columns - width)),
        ] + [piece] * (places - 1),
        scratch_shapes=[vmem(columns - width, wide), pltpu.SemaphoreType.DMA((2 * places + 5,))],
        compiler_params=params(16),
        cost_estimate=cost(8 * rows * wide * (columns - width), 4 * (rows + 2 * columns) * wide),
        name="project_others",
    )(*map(far, (cotangent, w_out, tokens, w_query, w_key, w_value)))
    near, (others_grad, others), pieces = found[:6], found[6:8], found[8:]
    w_all, own_grad, own, own_piece = pl.pallas_call(
        own_kernel,
        in_specs=[HELD] * 6,
        out_specs=[HELD] * 4,
        out_shape=[vmem(wide, 3 * columns), vmem(rows, width), vmem(rows, 3 * width), piece],
        compiler_params=params(12),
        cost_estimate=cost(8 * rows * wide * width, 12 * wide * columns),
        name="project_own",
    )(*map(held, near))
    operands = own, others, own_grad, others_grad

    def intra(after):
        return pl.pallas_call(
            intra_kernel,
            in_specs=[HELD] * 5,
            out_specs=HELD,
            out_shape=vmem(rows, 3 * columns),
            compiler_params=params(16),
            cost_estimate=cost(10 * rows * rows * columns, 14 * rows * columns),
            name="intra",
        )(*map(held, (*operands, after)))

    pieces, parts = exclusive_scan([own_piece, *pieces], intra)

    total = []
    for k in range(places):
        last = k == places - 1
        total = [pl.pallas_call(
            functools.partial(finish_kernel, factor, k, last),
            in_specs=[HELD] * (7 + len(total)),
            out_specs=FAR if last else HELD,
            out_shape=jax.ShapeDtypeStruct((rows, wide), jnp.bfloat16) if last else pltpu.VMEM((rows, wide), jnp.float32),
            scratch_shapes=[vmem(rows, 3 * width)] + ([vmem(rows, wide), pltpu.SemaphoreType.DMA((2,))] if last else []),
            compiler_params=params(20),
            cost_estimate=cost(6 * rows * width * (wide + DH), 6 * (rows + wide) * width),
            name="finish",
        )(*map(held, (*total, parts, *operands, w_all, pieces[k])))]
    return total[0]


def solution(mesh):
    groups, places = mesh.devices.shape
    mesh = jax.sharding.Mesh(mesh.devices.reshape(groups // 2, 2, 2, places // 2), AXES)
    placed = (P(AXES, None), P(AXES, None), P(), P(), P(), P())
    return jax.shard_map(
        shards, mesh=mesh, in_specs=placed, out_specs=P(AXES, None), check_vma=False
    )
```

```python
import functools
import math

import jax
import jax.numpy as jnp
from jax import lax
from jax.experimental import pallas as pl
from jax.experimental.pallas import tpu as pltpu
from jax.sharding import PartitionSpec as P

DH = 128
AXES = ("x", "core", "half", "rest")
ROWS_ROWS = (((0,), (0,)), ((), ()))
LAST_LAST = (((1,), (1,)), ((), ()))
PLAIN = (((1,), (0,)), ((), ()))


def mul(left, right, dims=PLAIN):
    return lax.dot_general(left, right, dims, preferred_element_type=jnp.float32)


HELD = pl.BlockSpec(memory_space=pltpu.VMEM)
FAR = pl.BlockSpec(memory_space=pl.ANY)


def held(array):
    return pltpu.with_memory_space_constraint(array, pltpu.VMEM)


def far(array):
    return pltpu.with_memory_space_constraint(array, pltpu.HBM)


def params(mebibytes):
    return pltpu.CompilerParams(vmem_limit_bytes=mebibytes << 20)


def swap(pieces, axis):
    places = len(pieces)
    swapped = list(pieces)
    for k in reversed(range(1, places)):
        swapped[k] = lax.ppermute(pieces[k], axis, [(place, place ^ k) for place in range(places)])
    return swapped


def group_kernel(places, *refs):
    slices, (slices_ref, sum_ref) = refs[:places], refs[-2:]
    me = lax.axis_index("rest")
    total = None
    for k, piece in enumerate(reversed(slices)):
        slices_ref[me ^ k] = piece[...]
        term = piece[...].astype(jnp.float32)
        total = term if total is None else total + term
    sum_ref[...] = total.astype(jnp.bfloat16)


def cross_of(kind, total, sum_ref, before_ref, cross_ref):
    before_ref[...] = total.astype(jnp.bfloat16)
    added = jnp.where(lax.axis_index("half") == kind, sum_ref[kind].astype(jnp.float32), 0.0)
    cross_ref[...] = (total + added).astype(jnp.bfloat16)


def core_before(kind, other_ref):
    return jnp.where(lax.axis_index("core") != kind, other_ref[kind].astype(jnp.float32), 0.0)


def chip_kernel(split, sum_ref, other_ref, *refs):
    chip = lax.axis_index("x")
    sends = refs[:-2] if split else refs
    for k, send in enumerate(sends):
        kind = jnp.where(chip < (chip ^ (k + 1)), 0, 1)
        send[...] = (sum_ref[kind].astype(jnp.float32) + other_ref[kind].astype(jnp.float32)).astype(jnp.bfloat16)
    if split:
        cross_of(chip, core_before(chip, other_ref), sum_ref, *refs[-2:])


def half_kernel(split, chips, sum_ref, other_ref, *refs):
    chip, outs = lax.axis_index("x"), refs[-2:]
    if split:
        total = core_before(1 - chip, other_ref) + refs[0][...].astype(jnp.float32)
        cross_of(1 - chip, total, sum_ref, *outs)
        return
    for kind in range(2):
        total = core_before(kind, other_ref)
        for k in range(1, chips):
            ahead = (chip ^ k) > chip if kind else (chip ^ k) < chip
            total = total + jnp.where(ahead, refs[k - 1][...].astype(jnp.float32), 0.0)
        cross_of(kind, total, sum_ref, *[out.at[kind] for out in outs])


def scan_kernel(split, slices_ref, *refs):
    places = slices_ref.shape[0]
    pieces, out_ref = refs[-1 - places : -1], refs[-1]
    chip = lax.axis_index("x")

    def base(kind):
        if split:
            first, first_cross, second, second_cross = [ref[...].astype(jnp.float32) for ref in refs[:4]]
            return jnp.where(chip == kind, first + first_cross, second + second_cross)
        return refs[0][kind].astype(jnp.float32) + refs[1][kind].astype(jnp.float32)

    for kind in range(2):
        total = base(kind)
        for step in range(places):
            place = places - 1 - step if kind else step
            out_ref[place, kind] = total.astype(jnp.bfloat16)
            total = total + slices_ref[place, kind].astype(jnp.float32)
    me = lax.axis_index("rest")
    for k, piece in enumerate(pieces):
        piece[...] = out_ref[me ^ k]


def small_call(kernel, name, operands, outs, scratch=()):
    return pl.pallas_call(
        kernel,
        in_specs=[HELD] * len(operands),
        out_specs=[HELD] * len(outs),
        out_shape=[pltpu.VMEM(shape, jnp.bfloat16) for shape in outs],
        scratch_shapes=[pltpu.VMEM(shape, jnp.bfloat16) for shape in scratch],
        compiler_params=params(8),
        name=name,
    )(*map(held, operands))


def exclusive_scan(pieces, work):
    places, chips = len(pieces), lax.axis_size("x")
    split = chips == 2
    piece = pieces[0].shape
    part, several = piece[1:], (places,) + piece
    halves_swap = [(0, 1), (1, 0)]
    done = [work(0, pieces[1])]
    slices, total = small_call(
        functools.partial(group_kernel, places), "group", [*reversed(swap(pieces, "rest")), *done], [several, piece]
    )
    other = lax.ppermute(total, "core", halves_swap)
    found = small_call(
        functools.partial(chip_kernel, split), "chip", [total, other], [part] * (chips + 1 if split else chips - 1)
    )
    sends, first = found[: chips - 1], found[chips - 1 :]
    done.append(work(1, sends[0]))
    near = swap([None, *sends], "x")[1:]
    crossed = [first[0], lax.ppermute(first[1], "half", halves_swap)] if split else []
    before, cross = small_call(
        functools.partial(half_kernel, split, chips), "half", [total, other, *near, done[1]], [part if split else piece] * 2
    )
    done.append(work(2, before))
    crossed += [before, lax.ppermute(cross, "half", halves_swap)]
    pieces = small_call(
        functools.partial(scan_kernel, split), "scan", [slices, *crossed, done[2]], [piece] * places, [several]
    )
    return swap(pieces, "rest"), done


def arrive(source, target, sem):
    copy = pltpu.make_async_copy(source, target, sem)
    copy.start()
    return copy


def halves(extent):
    return [pl.ds(half * (extent // 2), extent // 2) for half in range(2)]


def states_of(queries, keys, values, grads, state_ref):
    for head in range(state_ref.shape[1] // DH):
        lanes = pl.ds(head * DH, DH)
        for kind, (left, right) in enumerate(((keys, values), (queries, grads))):
            state_ref[kind, lanes] = mul(left[:, lanes], right[:, lanes], ROWS_ROWS).astype(jnp.bfloat16)


def kinds_of(ref, piece, width):
    return [ref.at[:, pl.ds((3 * piece + kind) * width, width)] for kind in range(3)]


def home_of(k, width):
    return pl.ds(pl.multiple_of((lax.axis_index("rest") ^ k) * width, width), width)


def others_kernel(
    cotangent_hbm, w_out_hbm, tokens_hbm, w_query_hbm, w_key_hbm, w_value_hbm,
    cotangent, tokens, w_own, w_query, w_key, w_value, grad_out, projected, *refs,
):
    *states, w_out, sems = refs
    places = len(states) + 1
    width = w_own.shape[0]
    count = [0]

    def bring(source, target):
        count[0] += 1
        return arrive(source, target, sems.at[count[0] - 1])

    parts = halves(tokens.shape[1])
    first = []
    for lanes in parts:
        here = [bring(cotangent_hbm.at[:, lanes], cotangent.at[:, lanes])]
        for k in range(1, places):
            here.append(bring(w_out_hbm.at[home_of(k, width), lanes], w_out.at[pl.ds((k - 1) * width, width), lanes]))
        first.append(here)
    tokens_copy = bring(tokens_hbm, tokens)
    weights = w_query, w_key, w_value
    copies = [bring(*pair) for pair in zip((w_query_hbm, w_key_hbm, w_value_hbm), weights)]
    own_copy = bring(w_out_hbm.at[home_of(0, width)], w_own)
    total = None
    for lanes, here in zip(parts, first):
        for copy in here:
            copy.wait()
        term = mul(cotangent[:, lanes], w_out[:, lanes], LAST_LAST)
        total = term if total is None else total + term
    grad_out[...] = total.astype(jnp.bfloat16)
    tokens_copy.wait()
    for kind, (copy, weight) in enumerate(zip(copies, weights)):
        copy.wait()
        for k in range(1, places):
            product = mul(tokens[...], weight[:, home_of(k, width)])
            kinds_of(projected, k - 1, width)[kind][...] = product.astype(jnp.bfloat16)
    for k in range(1, places):
        states_of(*kinds_of(projected, k - 1, width), grad_out.at[:, pl.ds((k - 1) * width, width)], states[k - 1])
    own_copy.wait()


def own_kernel(cotangent, tokens, w_own, w_query, w_key, w_value, w_all, grad_out, projected, state):
    width = w_own.shape[0]
    weights = w_query, w_key, w_value
    for k in range(w_query.shape[1] // width):
        for source, target in zip(weights, kinds_of(w_all, k, width)):
            target[...] = source[:, home_of(k, width)]
    grad_out[...] = mul(cotangent[...], w_own[...], LAST_LAST).astype(jnp.bfloat16)
    projected[...] = mul(tokens[...], w_all[:, pl.ds(0, 3 * width)]).astype(jnp.bfloat16)
    states_of(*kinds_of(projected, 0, width), grad_out, state)


def operands_of(piece, width, own, others, own_grad, others_grad):
    if piece == 0:
        return (*kinds_of(own, 0, width), own_grad)
    return (*kinds_of(others, piece - 1, width), others_grad.at[:, pl.ds((piece - 1) * width, width)])


def intra_kernel(pieces, own, others, own_grad, others_grad, _, parts):
    rows, width = parts.shape[0], parts.shape[1] // (3 * len(pieces))
    step = min(rows, 256)
    blocks = [pl.ds(at * step, step) for at in range(rows // step)]
    below = lax.broadcasted_iota(jnp.int32, (step, step), 0) >= lax.broadcasted_iota(jnp.int32, (step, step), 1)

    def score(left, right, masked):
        found = mul(left, right, LAST_LAST)
        return (jnp.where(below, found, 0.0) if masked else found).astype(jnp.bfloat16)

    for at, piece in enumerate(pieces):
        query_ref, keys_ref, values_ref, grad_out_ref = operands_of(piece, width, own, others, own_grad, others_grad)
        grad_query_ref, grad_key_ref, grad_value_ref = kinds_of(parts, at, width)
        for head in range(width // DH):
            lanes = pl.ds(head * DH, DH)
            query_t = query_ref[:, lanes].T
            grad_out_t = grad_out_ref[:, lanes].T
            key_sums, value_sums = [None] * len(blocks), [None] * len(blocks)
            for t, mine in enumerate(blocks):
                span = slice(t * step, (t + 1) * step)
                query_sum = None
                for s, theirs in enumerate(blocks[: t + 1]):
                    probe = score(grad_out_ref[mine, lanes], values_ref[theirs, lanes], s == t)
                    attend = score(query_ref[mine, lanes], keys_ref[theirs, lanes], s == t)
                    term = mul(probe, keys_ref[theirs, lanes])
                    query_sum = term if query_sum is None else query_sum + term
                    term = mul(query_t[:, span], probe)
                    key_sums[s] = term if key_sums[s] is None else key_sums[s] + term
                    term = mul(grad_out_t[:, span], attend)
                    value_sums[s] = term if value_sums[s] is None else value_sums[s] + term
                grad_query_ref[mine, lanes] = query_sum.astype(jnp.bfloat16)
            for s, theirs in enumerate(blocks):
                grad_key_ref[theirs, lanes] = key_sums[s].T.astype(jnp.bfloat16)
                grad_value_ref[theirs, lanes] = value_sums[s].T.astype(jnp.bfloat16)


def finish_kernel(factor, piece, at, last, *refs):
    if piece:
        total, *refs = refs
    parts, own, others, own_grad, others_grad, weight, sums, *refs = refs
    width = own_grad.shape[1]
    if last:
        out_hbm, grads, out, sems = refs
    else:
        out, grads = refs
    _, keys, values, grad_out = operands_of(piece, width, own, others, own_grad, others_grad)
    for head in range(width // DH):
        lanes = pl.ds(head * DH, DH)
        prior, later = sums[0, lanes], sums[1, lanes]
        inters = (
            mul(grad_out[:, lanes], prior, LAST_LAST),
            mul(values[:, lanes], later, LAST_LAST),
            mul(keys[:, lanes], later),
        )
        for inter, part, grad in zip(inters, kinds_of(parts, at, width), kinds_of(grads, 0, width)):
            grad[:, lanes] = (factor * (inter + part[:, lanes].astype(jnp.float32))).astype(jnp.bfloat16)
    columns = pl.ds(3 * piece * width, 3 * width)
    if not last:
        term = mul(grads[...], weight[:, columns], LAST_LAST)
        out[...] = total[...] + term if piece else term
        return
    sent = []
    for half, rows in enumerate(halves(weight.shape[0])):
        term = mul(grads[...], weight[rows, columns], LAST_LAST)
        out[:, rows] = (total[:, rows] + term).astype(jnp.bfloat16)
        sent.append(arrive(out.at[:, rows], out_hbm.at[:, rows], sems.at[half]))
    for copy in sent:
        copy.wait()


def shards(tokens, cotangent, w_query, w_key, w_value, w_out):
    rows, wide = tokens.shape
    columns = w_query.shape[1]
    places = lax.axis_size("rest")
    width = columns // places
    factor = 1.0 / math.sqrt(DH * rows * lax.axis_size(AXES))

    def vmem(*shape):
        return pltpu.VMEM(shape, jnp.bfloat16)

    def cost(flops, bytes_accessed):
        return pl.CostEstimate(flops=flops, bytes_accessed=bytes_accessed, transcendentals=0)

    piece = vmem(2, width, DH)
    weight = vmem(wide, columns)
    found = pl.pallas_call(
        others_kernel,
        in_specs=[FAR] * 6,
        out_specs=[HELD] * (7 + places),
        out_shape=[
            vmem(rows, wide), vmem(rows, wide), vmem(width, wide), weight, weight, weight,
            vmem(rows, columns - width), vmem(rows, 3 * (columns - width)),
        ] + [piece] * (places - 1),
        scratch_shapes=[vmem(columns - width, wide), pltpu.SemaphoreType.DMA((2 * places + 5,))],
        compiler_params=params(16),
        cost_estimate=cost(8 * rows * wide * (columns - width), 4 * (rows + 2 * columns) * wide),
        name="project_others",
    )(*map(far, (cotangent, w_out, tokens, w_query, w_key, w_value)))
    near, (others_grad, others), pieces = found[:6], found[6:8], found[8:]
    w_all, own_grad, own, own_piece = pl.pallas_call(
        own_kernel,
        in_specs=[HELD] * 6,
        out_specs=[HELD] * 4,
        out_shape=[vmem(wide, 3 * columns), vmem(rows, width), vmem(rows, 3 * width), piece],
        compiler_params=params(12),
        cost_estimate=cost(8 * rows * wide * width, 12 * wide * columns),
        name="project_own",
    )(*map(held, near))
    operands = own, others, own_grad, others_grad
    turns = [(places - 1,), (1,), (0, *range(2, places - 1))]

    def intra(step, after):
        share = len(turns[step])
        views = operands if step == 2 else (others, others, others_grad, others_grad)
        return pl.pallas_call(
            functools.partial(intra_kernel, turns[step]),
            in_specs=[HELD] * 5,
            out_specs=HELD,
            out_shape=vmem(rows, 3 * width * share),
            compiler_params=params(12),
            cost_estimate=cost(10 * rows * rows * width * share, 14 * rows * width * share),
            name="intra",
        )(*map(held, (*views, after)))

    pieces, parts = exclusive_scan([own_piece, *pieces], intra)
    part_of = {piece: (step, at) for step, turn in enumerate(turns) for at, piece in enumerate(turn)}
    total = []
    for k in range(places):
        last = k == places - 1
        total = [pl.pallas_call(
            functools.partial(finish_kernel, factor, k, part_of[k][1], last),
            in_specs=[HELD] * (7 + len(total)),
            out_specs=FAR if last else HELD,
            out_shape=jax.ShapeDtypeStruct((rows, wide), jnp.bfloat16) if last else pltpu.VMEM((rows, wide), jnp.float32),
            scratch_shapes=[vmem(rows, 3 * width)] + ([vmem(rows, wide), pltpu.SemaphoreType.DMA((2,))] if last else []),
            compiler_params=params(20),
            cost_estimate=cost(6 * rows * width * (wide + DH), 6 * (rows + wide) * width),
            name="finish",
        )(*map(held, (*total, parts[part_of[k][0]], *operands, w_all, pieces[k])))]
    return total[0]


def solution(mesh):
    groups, places = mesh.devices.shape
    mesh = jax.sharding.Mesh(mesh.devices.reshape(groups // 2, 2, 2, places // 2), AXES)
    placed = (P(AXES, None), P(AXES, None), P(), P(), P(), P())
    return jax.shard_map(
        shards, mesh=mesh, in_specs=placed, out_specs=P(AXES, None), check_vma=False
    )
```

```python
import functools
import math

import jax
import jax.numpy as jnp
from jax import lax
from jax.experimental import pallas as pl
from jax.experimental.pallas import tpu as pltpu
from jax.sharding import PartitionSpec as P

DH = 128
AXES = ("x", "core", "half", "rest")
ROWS_ROWS = (((0,), (0,)), ((), ()))
LAST_LAST = (((1,), (1,)), ((), ()))
PLAIN = (((1,), (0,)), ((), ()))


def mul(left, right, dims=PLAIN):
    return lax.dot_general(left, right, dims, preferred_element_type=jnp.float32)


HELD = pl.BlockSpec(memory_space=pltpu.VMEM)
FAR = pl.BlockSpec(memory_space=pl.ANY)


def held(array):
    return pltpu.with_memory_space_constraint(array, pltpu.VMEM)


def far(array):
    return pltpu.with_memory_space_constraint(array, pltpu.HBM)


def params(mebibytes):
    return pltpu.CompilerParams(vmem_limit_bytes=mebibytes << 20)


def swap(pieces, axis):
    places = len(pieces)
    swapped = list(pieces)
    for k in reversed(range(1, places)):
        swapped[k] = lax.ppermute(pieces[k], axis, [(place, place ^ k) for place in range(places)])
    return swapped


def group_kernel(places, *refs):
    slices, (slices_ref, sum_ref) = refs[:places], refs[-2:]
    me = lax.axis_index("rest")
    total = None
    for k, piece in enumerate(reversed(slices)):
        slices_ref[me ^ k] = piece[...]
        term = piece[...].astype(jnp.float32)
        total = term if total is None else total + term
    sum_ref[...] = total.astype(jnp.bfloat16)


def cross_of(kind, total, sum_ref, before_ref, cross_ref):
    before_ref[...] = total.astype(jnp.bfloat16)
    added = jnp.where(lax.axis_index("half") == kind, sum_ref[kind].astype(jnp.float32), 0.0)
    cross_ref[...] = (total + added).astype(jnp.bfloat16)


def core_before(kind, other_ref):
    return jnp.where(lax.axis_index("core") != kind, other_ref[kind].astype(jnp.float32), 0.0)


def chip_kernel(split, sum_ref, other_ref, *refs):
    chip = lax.axis_index("x")
    sends = refs[:-2] if split else refs
    for k, send in enumerate(sends):
        kind = jnp.where(chip < (chip ^ (k + 1)), 0, 1)
        send[...] = (sum_ref[kind].astype(jnp.float32) + other_ref[kind].astype(jnp.float32)).astype(jnp.bfloat16)
    if split:
        cross_of(chip, core_before(chip, other_ref), sum_ref, *refs[-2:])


def half_kernel(split, chips, sum_ref, other_ref, *refs):
    chip, outs = lax.axis_index("x"), refs[-2:]
    if split:
        total = core_before(1 - chip, other_ref) + refs[0][...].astype(jnp.float32)
        cross_of(1 - chip, total, sum_ref, *outs)
        return
    for kind in range(2):
        total = core_before(kind, other_ref)
        for k in range(1, chips):
            ahead = (chip ^ k) > chip if kind else (chip ^ k) < chip
            total = total + jnp.where(ahead, refs[k - 1][...].astype(jnp.float32), 0.0)
        cross_of(kind, total, sum_ref, *[out.at[kind] for out in outs])


def scan_kernel(split, slices_ref, *refs):
    places = slices_ref.shape[0]
    pieces, out_ref = refs[-1 - places : -1], refs[-1]
    chip = lax.axis_index("x")

    def base(kind):
        if split:
            first, first_cross, second, second_cross = [ref[...].astype(jnp.float32) for ref in refs[:4]]
            return jnp.where(chip == kind, first + first_cross, second + second_cross)
        return refs[0][kind].astype(jnp.float32) + refs[1][kind].astype(jnp.float32)

    for kind in range(2):
        total = base(kind)
        for step in range(places):
            place = places - 1 - step if kind else step
            out_ref[place, kind] = total.astype(jnp.bfloat16)
            total = total + slices_ref[place, kind].astype(jnp.float32)
    me = lax.axis_index("rest")
    for k, piece in enumerate(pieces):
        piece[...] = out_ref[me ^ k]


def small_call(kernel, name, operands, outs, scratch=()):
    return pl.pallas_call(
        kernel,
        in_specs=[HELD] * len(operands),
        out_specs=[HELD] * len(outs),
        out_shape=[pltpu.VMEM(shape, jnp.bfloat16) for shape in outs],
        scratch_shapes=[pltpu.VMEM(shape, jnp.bfloat16) for shape in scratch],
        compiler_params=params(8),
        name=name,
    )(*map(held, operands))


def exclusive_scan(pieces, work):
    places, chips = len(pieces), lax.axis_size("x")
    split = chips == 2
    piece = pieces[0].shape
    part, several = piece[1:], (places,) + piece
    halves_swap = [(0, 1), (1, 0)]
    done = [work(0, pieces[1])]
    slices, total = small_call(
        functools.partial(group_kernel, places), "group", [*reversed(swap(pieces, "rest")), *done], [several, piece]
    )
    other = lax.ppermute(total, "core", halves_swap)
    found = small_call(
        functools.partial(chip_kernel, split), "chip", [total, other], [part] * (chips + 1 if split else chips - 1)
    )
    sends, first = found[: chips - 1], found[chips - 1 :]
    done.append(work(1, sends[0]))
    near = swap([None, *sends], "x")[1:]
    crossed = [first[0], lax.ppermute(first[1], "half", halves_swap)] if split else []
    before, cross = small_call(
        functools.partial(half_kernel, split, chips), "half", [total, other, *near, done[1]], [part if split else piece] * 2
    )
    done.append(work(2, before))
    crossed += [before, lax.ppermute(cross, "half", halves_swap)]
    pieces = small_call(
        functools.partial(scan_kernel, split), "scan", [slices, *crossed, done[2]], [piece] * places, [several]
    )
    return swap(pieces, "rest"), done


def arrive(source, target, sem):
    copy = pltpu.make_async_copy(source, target, sem)
    copy.start()
    return copy


def halves(extent):
    return [pl.ds(half * (extent // 2), extent // 2) for half in range(2)]


def states_of(queries, keys, values, grads, state_ref):
    for head in range(state_ref.shape[1] // DH):
        lanes = pl.ds(head * DH, DH)
        for kind, (left, right) in enumerate(((keys, values), (queries, grads))):
            state_ref[kind, lanes] = mul(left[:, lanes], right[:, lanes], ROWS_ROWS).astype(jnp.bfloat16)


def kinds_of(ref, piece, width):
    return [ref.at[:, pl.ds((3 * piece + kind) * width, width)] for kind in range(3)]


def home_of(k, width):
    return pl.ds(pl.multiple_of((lax.axis_index("rest") ^ k) * width, width), width)


def joined(refs):
    return jnp.concatenate([ref[...] for ref in refs], axis=1)


def others_kernel(
    cotangent_hbm, w_out_hbm, tokens_hbm, w_query_hbm, w_key_hbm, w_value_hbm,
    cotangent, tokens, w_own, w_query, w_key, w_value, grad_out, projected, *refs,
):
    *states, w_out, sems = refs
    places = len(states) + 1
    width = w_own.shape[0]
    count = [0]

    def bring(source, target):
        count[0] += 1
        return arrive(source, target, sems.at[count[0] - 1])

    parts = halves(tokens.shape[1])
    first = []
    for lanes in parts:
        here = [bring(cotangent_hbm.at[:, lanes], cotangent.at[:, lanes])]
        for k in range(1, places):
            here.append(bring(w_out_hbm.at[home_of(k, width), lanes], w_out.at[pl.ds((k - 1) * width, width), lanes]))
        first.append(here)
    tokens_copy = bring(tokens_hbm, tokens)
    weights = w_query, w_key, w_value
    copies = [bring(*pair) for pair in zip((w_query_hbm, w_key_hbm, w_value_hbm), weights)]
    own_copy = bring(w_out_hbm.at[home_of(0, width)], w_own)
    total = None
    for lanes, here in zip(parts, first):
        for copy in here:
            copy.wait()
        term = mul(cotangent[:, lanes], w_out[:, lanes], LAST_LAST)
        total = term if total is None else total + term
    grad_out[...] = total.astype(jnp.bfloat16)
    tokens_copy.wait()
    for kind, (copy, weight) in enumerate(zip(copies, weights)):
        copy.wait()
        product = mul(tokens[...], joined([weight.at[:, home_of(k, width)] for k in range(1, places)]))
        for k in range(1, places):
            kinds_of(projected, k - 1, width)[kind][...] = product[:, (k - 1) * width : k * width].astype(jnp.bfloat16)
    for k in range(1, places):
        states_of(*kinds_of(projected, k - 1, width), grad_out.at[:, pl.ds((k - 1) * width, width)], states[k - 1])
    own_copy.wait()


def own_kernel(cotangent, tokens, w_own, w_query, w_key, w_value, grad_out, projected, state):
    width = w_own.shape[0]
    grad_out[...] = mul(cotangent[...], w_own[...], LAST_LAST).astype(jnp.bfloat16)
    weights = [weight.at[:, home_of(0, width)] for weight in (w_query, w_key, w_value)]
    projected[...] = mul(tokens[...], joined(weights)).astype(jnp.bfloat16)
    states_of(*kinds_of(projected, 0, width), grad_out, state)


def operands_of(piece, width, own, others, own_grad, others_grad):
    if piece == 0:
        return (*kinds_of(own, 0, width), own_grad)
    return (*kinds_of(others, piece - 1, width), others_grad.at[:, pl.ds((piece - 1) * width, width)])


def intra_kernel(pieces, own, others, own_grad, others_grad, _, parts):
    rows, width = parts.shape[0], parts.shape[1] // (3 * len(pieces))
    step = min(rows, 256)
    blocks = [pl.ds(at * step, step) for at in range(rows // step)]
    below = lax.broadcasted_iota(jnp.int32, (step, step), 0) >= lax.broadcasted_iota(jnp.int32, (step, step), 1)

    def score(left, right, masked):
        found = mul(left, right, LAST_LAST)
        return (jnp.where(below, found, 0.0) if masked else found).astype(jnp.bfloat16)

    for at, piece in enumerate(pieces):
        query_ref, keys_ref, values_ref, grad_out_ref = operands_of(piece, width, own, others, own_grad, others_grad)
        grad_query_ref, grad_key_ref, grad_value_ref = kinds_of(parts, at, width)
        for head in range(width // DH):
            lanes = pl.ds(head * DH, DH)
            query_t = query_ref[:, lanes].T
            grad_out_t = grad_out_ref[:, lanes].T
            key_sums, value_sums = [None] * len(blocks), [None] * len(blocks)
            for t, mine in enumerate(blocks):
                span = slice(t * step, (t + 1) * step)
                query_sum = None
                for s, theirs in enumerate(blocks[: t + 1]):
                    probe = score(grad_out_ref[mine, lanes], values_ref[theirs, lanes], s == t)
                    attend = score(query_ref[mine, lanes], keys_ref[theirs, lanes], s == t)
                    term = mul(probe, keys_ref[theirs, lanes])
                    query_sum = term if query_sum is None else query_sum + term
                    term = mul(query_t[:, span], probe)
                    key_sums[s] = term if key_sums[s] is None else key_sums[s] + term
                    term = mul(grad_out_t[:, span], attend)
                    value_sums[s] = term if value_sums[s] is None else value_sums[s] + term
                grad_query_ref[mine, lanes] = query_sum.astype(jnp.bfloat16)
            for s, theirs in enumerate(blocks):
                grad_key_ref[theirs, lanes] = key_sums[s].T.astype(jnp.bfloat16)
                grad_value_ref[theirs, lanes] = value_sums[s].T.astype(jnp.bfloat16)


def finish_kernel(factor, piece, at, last, *refs):
    if piece:
        total, *refs = refs
    parts, own, others, own_grad, others_grad, w_query, w_key, w_value, sums, *refs = refs
    width = own_grad.shape[1]
    if last:
        out_hbm, grads, out, sems = refs
    else:
        out, grads = refs
    _, keys, values, grad_out = operands_of(piece, width, own, others, own_grad, others_grad)
    for head in range(width // DH):
        lanes = pl.ds(head * DH, DH)
        prior, later = sums[0, lanes], sums[1, lanes]
        inters = (
            mul(grad_out[:, lanes], prior, LAST_LAST),
            mul(values[:, lanes], later, LAST_LAST),
            mul(keys[:, lanes], later),
        )
        for inter, part, grad in zip(inters, kinds_of(parts, at, width), kinds_of(grads, 0, width)):
            grad[:, lanes] = (factor * (inter + part[:, lanes].astype(jnp.float32))).astype(jnp.bfloat16)
    columns = home_of(piece, width)
    weights = w_query, w_key, w_value
    if not last:
        term = mul(grads[...], joined([weight.at[:, columns] for weight in weights]), LAST_LAST)
        out[...] = total[...] + term if piece else term
        return
    sent = []
    for half, rows in enumerate(halves(w_query.shape[0])):
        term = mul(grads[...], joined([weight.at[rows, columns] for weight in weights]), LAST_LAST)
        out[:, rows] = (total[:, rows] + term).astype(jnp.bfloat16)
        sent.append(arrive(out.at[:, rows], out_hbm.at[:, rows], sems.at[half]))
    for copy in sent:
        copy.wait()


def shards(tokens, cotangent, w_query, w_key, w_value, w_out):
    rows, wide = tokens.shape
    columns = w_query.shape[1]
    places = lax.axis_size("rest")
    width = columns // places
    factor = 1.0 / math.sqrt(DH * rows * lax.axis_size(AXES))

    def vmem(*shape):
        return pltpu.VMEM(shape, jnp.bfloat16)

    def cost(flops, bytes_accessed):
        return pl.CostEstimate(flops=flops, bytes_accessed=bytes_accessed, transcendentals=0)

    piece = vmem(2, width, DH)
    weight = vmem(wide, columns)
    found = pl.pallas_call(
        others_kernel,
        in_specs=[FAR] * 6,
        out_specs=[HELD] * (7 + places),
        out_shape=[
            vmem(rows, wide), vmem(rows, wide), vmem(width, wide), weight, weight, weight,
            vmem(rows, columns - width), vmem(rows, 3 * (columns - width)),
        ] + [piece] * (places - 1),
        scratch_shapes=[vmem(columns - width, wide), pltpu.SemaphoreType.DMA((2 * places + 5,))],
        compiler_params=params(16),
        cost_estimate=cost(8 * rows * wide * (columns - width), 4 * (rows + 2 * columns) * wide),
        name="project_others",
    )(*map(far, (cotangent, w_out, tokens, w_query, w_key, w_value)))
    near, (others_grad, others), pieces = found[:6], found[6:8], found[8:]
    own_grad, own, own_piece = pl.pallas_call(
        own_kernel,
        in_specs=[HELD] * 6,
        out_specs=[HELD] * 3,
        out_shape=[vmem(rows, width), vmem(rows, 3 * width), piece],
        compiler_params=params(16),
        cost_estimate=cost(8 * rows * wide * width, 8 * wide * width),
        name="project_own",
    )(*map(held, near))
    operands = own, others, own_grad, others_grad
    turns = [(places - 1,), (1,), (0, *range(2, places - 1))]

    def intra(step, after):
        share = len(turns[step])
        views = operands if step == 2 else (others, others, others_grad, others_grad)
        return pl.pallas_call(
            functools.partial(intra_kernel, turns[step]),
            in_specs=[HELD] * 5,
            out_specs=HELD,
            out_shape=vmem(rows, 3 * width * share),
            compiler_params=params(12),
            cost_estimate=cost(10 * rows * rows * width * share, 14 * rows * width * share),
            name="intra",
        )(*map(held, (*views, after)))

    pieces, parts = exclusive_scan([own_piece, *pieces], intra)
    part_of = {piece: (step, at) for step, turn in enumerate(turns) for at, piece in enumerate(turn)}
    total = []
    for k in range(places):
        last = k == places - 1
        total = [pl.pallas_call(
            functools.partial(finish_kernel, factor, k, part_of[k][1], last),
            in_specs=[HELD] * (9 + len(total)),
            out_specs=FAR if last else HELD,
            out_shape=jax.ShapeDtypeStruct((rows, wide), jnp.bfloat16) if last else pltpu.VMEM((rows, wide), jnp.float32),
            scratch_shapes=[vmem(rows, 3 * width)] + ([vmem(rows, wide), pltpu.SemaphoreType.DMA((2,))] if last else []),
            compiler_params=params(20),
            cost_estimate=cost(6 * rows * width * (wide + DH), 6 * (rows + wide) * width),
            name="finish",
        )(*map(held, (*total, parts[part_of[k][0]], *operands, *near[3:], pieces[k])))]
    return total[0]


def solution(mesh):
    groups, places = mesh.devices.shape
    mesh = jax.sharding.Mesh(mesh.devices.reshape(groups // 2, 2, 2, places // 2), AXES)
    placed = (P(AXES, None), P(AXES, None), P(), P(), P(), P())
    return jax.shard_map(
        shards, mesh=mesh, in_specs=placed, out_specs=P(AXES, None), check_vma=False
    )
```

```python
import functools
import math

import jax
import jax.numpy as jnp
from jax import lax
from jax.experimental import pallas as pl
from jax.experimental.pallas import tpu as pltpu
from jax.sharding import PartitionSpec as P

DH = 128
AXES = ("x", "core", "half", "rest")
ROWS_ROWS = (((0,), (0,)), ((), ()))
LAST_LAST = (((1,), (1,)), ((), ()))
PLAIN = (((1,), (0,)), ((), ()))


def mul(left, right, dims=PLAIN):
    return lax.dot_general(left, right, dims, preferred_element_type=jnp.float32)


HELD = pl.BlockSpec(memory_space=pltpu.VMEM)
FAR = pl.BlockSpec(memory_space=pl.ANY)


def held(array):
    return pltpu.with_memory_space_constraint(array, pltpu.VMEM)


def far(array):
    return pltpu.with_memory_space_constraint(array, pltpu.HBM)


def params(mebibytes):
    return pltpu.CompilerParams(vmem_limit_bytes=mebibytes << 20)


def swap(pieces, axis):
    places = len(pieces)
    swapped = list(pieces)
    for k in reversed(range(1, places)):
        swapped[k] = lax.ppermute(pieces[k], axis, [(place, place ^ k) for place in range(places)])
    return swapped


def group_kernel(places, *refs):
    slices, (slices_ref, sum_ref) = refs[:places], refs[-2:]
    me = lax.axis_index("rest")
    total = None
    for k, piece in enumerate(reversed(slices)):
        slices_ref[me ^ k] = piece[...]
        term = piece[...].astype(jnp.float32)
        total = term if total is None else total + term
    sum_ref[...] = total.astype(jnp.bfloat16)


def cross_of(kind, total, sum_ref, before_ref, cross_ref):
    before_ref[...] = total.astype(jnp.bfloat16)
    added = jnp.where(lax.axis_index("half") == kind, sum_ref[kind].astype(jnp.float32), 0.0)
    cross_ref[...] = (total + added).astype(jnp.bfloat16)


def core_before(kind, other_ref):
    return jnp.where(lax.axis_index("core") != kind, other_ref[kind].astype(jnp.float32), 0.0)


def chip_kernel(split, sum_ref, other_ref, *refs):
    chip = lax.axis_index("x")
    sends = refs[:-2] if split else refs
    for k, send in enumerate(sends):
        kind = jnp.where(chip < (chip ^ (k + 1)), 0, 1)
        send[...] = (sum_ref[kind].astype(jnp.float32) + other_ref[kind].astype(jnp.float32)).astype(jnp.bfloat16)
    if split:
        cross_of(chip, core_before(chip, other_ref), sum_ref, *refs[-2:])


def half_kernel(split, chips, sum_ref, other_ref, *refs):
    chip, outs = lax.axis_index("x"), refs[-2:]
    if split:
        total = core_before(1 - chip, other_ref) + refs[0][...].astype(jnp.float32)
        cross_of(1 - chip, total, sum_ref, *outs)
        return
    for kind in range(2):
        total = core_before(kind, other_ref)
        for k in range(1, chips):
            ahead = (chip ^ k) > chip if kind else (chip ^ k) < chip
            total = total + jnp.where(ahead, refs[k - 1][...].astype(jnp.float32), 0.0)
        cross_of(kind, total, sum_ref, *[out.at[kind] for out in outs])


def scan_kernel(split, slices_ref, *refs):
    places = slices_ref.shape[0]
    pieces, out_ref = refs[-1 - places : -1], refs[-1]
    chip = lax.axis_index("x")

    def base(kind):
        if split:
            first, first_cross, second, second_cross = [ref[...].astype(jnp.float32) for ref in refs[:4]]
            return jnp.where(chip == kind, first + first_cross, second + second_cross)
        return refs[0][kind].astype(jnp.float32) + refs[1][kind].astype(jnp.float32)

    for kind in range(2):
        total = base(kind)
        for step in range(places):
            place = places - 1 - step if kind else step
            out_ref[place, kind] = total.astype(jnp.bfloat16)
            total = total + slices_ref[place, kind].astype(jnp.float32)
    me = lax.axis_index("rest")
    for k, piece in enumerate(pieces):
        piece[...] = out_ref[me ^ k]


def small_call(kernel, name, operands, outs, scratch=()):
    return pl.pallas_call(
        kernel,
        in_specs=[HELD] * len(operands),
        out_specs=[HELD] * len(outs),
        out_shape=[pltpu.VMEM(shape, jnp.bfloat16) for shape in outs],
        scratch_shapes=[pltpu.VMEM(shape, jnp.bfloat16) for shape in scratch],
        compiler_params=params(8),
        name=name,
    )(*map(held, operands))


def exclusive_scan(pieces, work):
    places, chips = len(pieces), lax.axis_size("x")
    split = chips == 2
    piece = pieces[0].shape
    part, several = piece[1:], (places,) + piece
    halves_swap = [(0, 1), (1, 0)]
    done = [work(0, pieces[1])]
    slices, total = small_call(
        functools.partial(group_kernel, places), "group", [*reversed(swap(pieces, "rest")), *done], [several, piece]
    )
    other = lax.ppermute(total, "core", halves_swap)
    found = small_call(
        functools.partial(chip_kernel, split), "chip", [total, other], [part] * (chips + 1 if split else chips - 1)
    )
    sends, first = found[: chips - 1], found[chips - 1 :]
    done.append(work(1, sends[0]))
    near = swap([None, *sends], "x")[1:]
    crossed = [first[0], lax.ppermute(first[1], "half", halves_swap)] if split else []
    before, cross = small_call(
        functools.partial(half_kernel, split, chips), "half", [total, other, *near, done[1]], [part if split else piece] * 2
    )
    done.append(work(2, before))
    crossed += [before, lax.ppermute(cross, "half", halves_swap)]
    pieces = small_call(
        functools.partial(scan_kernel, split), "scan", [slices, *crossed, done[2]], [piece] * places, [several]
    )
    return swap(pieces, "rest"), done


def arrive(source, target, sem):
    copy = pltpu.make_async_copy(source, target, sem)
    copy.start()
    return copy


def halves(extent):
    return [pl.ds(half * (extent // 2), extent // 2) for half in range(2)]


def states_of(queries, keys, values, grads, state_ref):
    for head in range(state_ref.shape[1] // DH):
        lanes = pl.ds(head * DH, DH)
        for kind, (left, right) in enumerate(((keys, values), (queries, grads))):
            state_ref[kind, lanes] = mul(left[:, lanes], right[:, lanes], ROWS_ROWS).astype(jnp.bfloat16)


def kinds_of(ref, piece, width):
    return [ref.at[:, pl.ds((3 * piece + kind) * width, width)] for kind in range(3)]


def home_of(k, width):
    return pl.ds(pl.multiple_of((lax.axis_index("rest") ^ k) * width, width), width)


def joined(refs):
    return jnp.concatenate([ref[...] for ref in refs], axis=1)


def others_kernel(
    cotangent_hbm, w_out_hbm, tokens_hbm, w_query_hbm, w_key_hbm, w_value_hbm,
    cotangent, tokens, w_query, w_key, w_value, grad_out, projected, *refs,
):
    *states, w_out, sems = refs
    places = len(states) + 1
    width = grad_out.shape[1] // (places - 1)
    count = [0]

    def bring(source, target):
        count[0] += 1
        return arrive(source, target, sems.at[count[0] - 1])

    parts = halves(tokens.shape[1])
    first = []
    for lanes in parts:
        here = [bring(cotangent_hbm.at[:, lanes], cotangent.at[:, lanes])]
        for k in range(1, places):
            here.append(bring(w_out_hbm.at[home_of(k, width), lanes], w_out.at[pl.ds((k - 1) * width, width), lanes]))
        first.append(here)
    weights = w_query, w_key, w_value
    copies = []
    total = None
    for half, (lanes, here) in enumerate(zip(parts, first)):
        for copy in here:
            copy.wait()
        if half == 0:
            copies.append([bring(tokens_hbm, tokens), bring(w_query_hbm, w_query)])
        else:
            copies.append([bring(w_key_hbm, w_key)])
        term = mul(cotangent[:, lanes], w_out[:, lanes], LAST_LAST)
        total = term if total is None else total + term
    grad_out[...] = total.astype(jnp.bfloat16)
    for kind, weight in enumerate(weights):
        for copy in copies[kind]:
            copy.wait()
        if kind == 0:
            copies.append([bring(w_value_hbm, w_value)])
        product = mul(tokens[...], joined([weight.at[:, home_of(k, width)] for k in range(1, places)]))
        for k in range(1, places):
            kinds_of(projected, k - 1, width)[kind][...] = product[:, (k - 1) * width : k * width].astype(jnp.bfloat16)
    for k in range(1, places):
        states_of(*kinds_of(projected, k - 1, width), grad_out.at[:, pl.ds((k - 1) * width, width)], states[k - 1])


def own_kernel(cotangent, tokens, w_query, w_key, w_value, w_out_hbm, grad_out, projected, state, w_out, sems):
    width = w_out.shape[0]
    copy = arrive(w_out_hbm.at[home_of(0, width)], w_out, sems.at[0])
    weights = [weight.at[:, home_of(0, width)] for weight in (w_query, w_key, w_value)]
    projected[...] = mul(tokens[...], joined(weights)).astype(jnp.bfloat16)
    copy.wait()
    grad_out[...] = mul(cotangent[...], w_out[...], LAST_LAST).astype(jnp.bfloat16)
    states_of(*kinds_of(projected, 0, width), grad_out, state)


def operands_of(piece, width, own, others, own_grad, others_grad):
    if piece == 0:
        return (*kinds_of(own, 0, width), own_grad)
    return (*kinds_of(others, piece - 1, width), others_grad.at[:, pl.ds((piece - 1) * width, width)])


def intra_kernel(pieces, own, others, own_grad, others_grad, _, parts):
    rows, width = parts.shape[0], parts.shape[1] // (3 * len(pieces))
    step = min(rows, 256)
    blocks = [pl.ds(at * step, step) for at in range(rows // step)]
    below = lax.broadcasted_iota(jnp.int32, (step, step), 0) >= lax.broadcasted_iota(jnp.int32, (step, step), 1)

    def score(left, right, masked):
        found = mul(left, right, LAST_LAST)
        return (jnp.where(below, found, 0.0) if masked else found).astype(jnp.bfloat16)

    for at, piece in enumerate(pieces):
        query_ref, keys_ref, values_ref, grad_out_ref = operands_of(piece, width, own, others, own_grad, others_grad)
        grad_query_ref, grad_key_ref, grad_value_ref = kinds_of(parts, at, width)
        for head in range(width // DH):
            lanes = pl.ds(head * DH, DH)
            query_t = query_ref[:, lanes].T
            grad_out_t = grad_out_ref[:, lanes].T
            key_sums, value_sums = [None] * len(blocks), [None] * len(blocks)
            for t, mine in enumerate(blocks):
                span = slice(t * step, (t + 1) * step)
                query_sum = None
                for s, theirs in enumerate(blocks[: t + 1]):
                    probe = score(grad_out_ref[mine, lanes], values_ref[theirs, lanes], s == t)
                    attend = score(query_ref[mine, lanes], keys_ref[theirs, lanes], s == t)
                    term = mul(probe, keys_ref[theirs, lanes])
                    query_sum = term if query_sum is None else query_sum + term
                    term = mul(query_t[:, span], probe)
                    key_sums[s] = term if key_sums[s] is None else key_sums[s] + term
                    term = mul(grad_out_t[:, span], attend)
                    value_sums[s] = term if value_sums[s] is None else value_sums[s] + term
                grad_query_ref[mine, lanes] = query_sum.astype(jnp.bfloat16)
            for s, theirs in enumerate(blocks):
                grad_key_ref[theirs, lanes] = key_sums[s].T.astype(jnp.bfloat16)
                grad_value_ref[theirs, lanes] = value_sums[s].T.astype(jnp.bfloat16)


def finish_kernel(factor, piece, at, last, *refs):
    if piece:
        total, *refs = refs
    parts, own, others, own_grad, others_grad, w_query, w_key, w_value, sums, *refs = refs
    width = own_grad.shape[1]
    if last:
        out_hbm, grads, out, sems = refs
    else:
        out, grads = refs
    _, keys, values, grad_out = operands_of(piece, width, own, others, own_grad, others_grad)
    for head in range(width // DH):
        lanes = pl.ds(head * DH, DH)
        prior, later = sums[0, lanes], sums[1, lanes]
        inters = (
            mul(grad_out[:, lanes], prior, LAST_LAST),
            mul(values[:, lanes], later, LAST_LAST),
            mul(keys[:, lanes], later),
        )
        for inter, part, grad in zip(inters, kinds_of(parts, at, width), kinds_of(grads, 0, width)):
            grad[:, lanes] = (factor * (inter + part[:, lanes].astype(jnp.float32))).astype(jnp.bfloat16)
    columns = home_of(piece, width)
    weights = w_query, w_key, w_value
    if not last:
        term = mul(grads[...], joined([weight.at[:, columns] for weight in weights]), LAST_LAST)
        out[...] = total[...] + term if piece else term
        return
    sent = []
    for half, rows in enumerate(halves(w_query.shape[0])):
        term = mul(grads[...], joined([weight.at[rows, columns] for weight in weights]), LAST_LAST)
        out[:, rows] = (total[:, rows] + term).astype(jnp.bfloat16)
        sent.append(arrive(out.at[:, rows], out_hbm.at[:, rows], sems.at[half]))
    for copy in sent:
        copy.wait()


def shards(tokens, cotangent, w_query, w_key, w_value, w_out):
    rows, wide = tokens.shape
    columns = w_query.shape[1]
    places = lax.axis_size("rest")
    width = columns // places
    factor = 1.0 / math.sqrt(DH * rows * lax.axis_size(AXES))

    def vmem(*shape):
        return pltpu.VMEM(shape, jnp.bfloat16)

    def cost(flops, bytes_accessed):
        return pl.CostEstimate(flops=flops, bytes_accessed=bytes_accessed, transcendentals=0)

    piece = vmem(2, width, DH)
    weight = vmem(wide, columns)
    found = pl.pallas_call(
        others_kernel,
        in_specs=[FAR] * 6,
        out_specs=[HELD] * (6 + places),
        out_shape=[
            vmem(rows, wide), vmem(rows, wide), weight, weight, weight,
            vmem(rows, columns - width), vmem(rows, 3 * (columns - width)),
        ] + [piece] * (places - 1),
        scratch_shapes=[vmem(columns - width, wide), pltpu.SemaphoreType.DMA((2 * places + 4,))],
        compiler_params=params(16),
        cost_estimate=cost(8 * rows * wide * (columns - width), 4 * (rows + 2 * columns) * wide),
        name="project_others",
    )(*map(far, (cotangent, w_out, tokens, w_query, w_key, w_value)))
    near, (others_grad, others), pieces = found[:5], found[5:7], found[7:]
    own_grad, own, own_piece = pl.pallas_call(
        own_kernel,
        in_specs=[HELD] * 5 + [FAR],
        out_specs=[HELD] * 3,
        out_shape=[vmem(rows, width), vmem(rows, 3 * width), piece],
        scratch_shapes=[vmem(width, wide), pltpu.SemaphoreType.DMA((1,))],
        compiler_params=params(16),
        cost_estimate=cost(8 * rows * wide * width, 8 * wide * width),
        name="project_own",
    )(*map(held, near), far(w_out))
    operands = own, others, own_grad, others_grad
    turns = [(places - 1,), (1,), (0, *range(2, places - 1))]

    def intra(step, after):
        share = len(turns[step])
        views = operands if step == 2 else (others, others, others_grad, others_grad)
        return pl.pallas_call(
            functools.partial(intra_kernel, turns[step]),
            in_specs=[HELD] * 5,
            out_specs=HELD,
            out_shape=vmem(rows, 3 * width * share),
            compiler_params=params(12),
            cost_estimate=cost(10 * rows * rows * width * share, 14 * rows * width * share),
            name="intra",
        )(*map(held, (*views, after)))

    pieces, parts = exclusive_scan([own_piece, *pieces], intra)
    part_of = {piece: (step, at) for step, turn in enumerate(turns) for at, piece in enumerate(turn)}
    total = []
    for k in range(places):
        last = k == places - 1
        total = [pl.pallas_call(
            functools.partial(finish_kernel, factor, k, part_of[k][1], last),
            in_specs=[HELD] * (9 + len(total)),
            out_specs=FAR if last else HELD,
            out_shape=jax.ShapeDtypeStruct((rows, wide), jnp.bfloat16) if last else pltpu.VMEM((rows, wide), jnp.float32),
            scratch_shapes=[vmem(rows, 3 * width)] + ([vmem(rows, wide), pltpu.SemaphoreType.DMA((2,))] if last else []),
            compiler_params=params(20),
            cost_estimate=cost(6 * rows * width * (wide + DH), 6 * (rows + wide) * width),
            name="finish",
        )(*map(held, (*total, parts[part_of[k][0]], *operands, *near[2:], pieces[k])))]
    return total[0]


def solution(mesh):
    groups, places = mesh.devices.shape
    mesh = jax.sharding.Mesh(mesh.devices.reshape(groups // 2, 2, 2, places // 2), AXES)
    placed = (P(AXES, None), P(AXES, None), P(), P(), P(), P())
    return jax.shard_map(
        shards, mesh=mesh, in_specs=placed, out_specs=P(AXES, None), check_vma=False
    )
```

```python
import functools
import math

import jax
import jax.numpy as jnp
from jax import lax
from jax.experimental import pallas as pl
from jax.experimental.pallas import tpu as pltpu
from jax.sharding import PartitionSpec as P

DH = 128
AXES = ("x", "core", "half", "rest")
ROWS_ROWS = (((0,), (0,)), ((), ()))
LAST_LAST = (((1,), (1,)), ((), ()))
PLAIN = (((1,), (0,)), ((), ()))


def mul(left, right, dims=PLAIN):
    return lax.dot_general(left, right, dims, preferred_element_type=jnp.float32)


HELD = pl.BlockSpec(memory_space=pltpu.VMEM)
FAR = pl.BlockSpec(memory_space=pl.ANY)


def held(array):
    return pltpu.with_memory_space_constraint(array, pltpu.VMEM)


def far(array):
    return pltpu.with_memory_space_constraint(array, pltpu.HBM)


def params(mebibytes):
    return pltpu.CompilerParams(vmem_limit_bytes=mebibytes << 20)


def swap(pieces, axis):
    places = len(pieces)
    swapped = list(pieces)
    for k in reversed(range(1, places)):
        swapped[k] = lax.ppermute(pieces[k], axis, [(place, place ^ k) for place in range(places)])
    return swapped


def group_kernel(places, *refs):
    slices, (slices_ref, sum_ref) = refs[:places], refs[-2:]
    me = lax.axis_index("rest")
    total = None
    for k, piece in enumerate(reversed(slices)):
        slices_ref[me ^ k] = piece[...]
        term = piece[...].astype(jnp.float32)
        total = term if total is None else total + term
    sum_ref[...] = total.astype(jnp.bfloat16)


def cross_of(kind, total, sum_ref, before_ref, cross_ref):
    before_ref[...] = total.astype(jnp.bfloat16)
    added = jnp.where(lax.axis_index("half") == kind, sum_ref[kind].astype(jnp.float32), 0.0)
    cross_ref[...] = (total + added).astype(jnp.bfloat16)


def core_before(kind, other_ref):
    return jnp.where(lax.axis_index("core") != kind, other_ref[kind].astype(jnp.float32), 0.0)


def chip_kernel(split, sum_ref, other_ref, *refs):
    chip = lax.axis_index("x")
    sends = refs[:-2] if split else refs
    for k, send in enumerate(sends):
        kind = jnp.where(chip < (chip ^ (k + 1)), 0, 1)
        send[...] = (sum_ref[kind].astype(jnp.float32) + other_ref[kind].astype(jnp.float32)).astype(jnp.bfloat16)
    if split:
        cross_of(chip, core_before(chip, other_ref), sum_ref, *refs[-2:])


def half_kernel(split, chips, sum_ref, other_ref, *refs):
    chip, outs = lax.axis_index("x"), refs[-2:]
    if split:
        total = core_before(1 - chip, other_ref) + refs[0][...].astype(jnp.float32)
        cross_of(1 - chip, total, sum_ref, *outs)
        return
    for kind in range(2):
        total = core_before(kind, other_ref)
        for k in range(1, chips):
            ahead = (chip ^ k) > chip if kind else (chip ^ k) < chip
            total = total + jnp.where(ahead, refs[k - 1][...].astype(jnp.float32), 0.0)
        cross_of(kind, total, sum_ref, *[out.at[kind] for out in outs])


def scan_kernel(split, slices_ref, *refs):
    places = slices_ref.shape[0]
    pieces, out_ref = refs[-1 - places : -1], refs[-1]
    chip = lax.axis_index("x")

    def base(kind):
        if split:
            first, first_cross, second, second_cross = [ref[...].astype(jnp.float32) for ref in refs[:4]]
            return jnp.where(chip == kind, first + first_cross, second + second_cross)
        return refs[0][kind].astype(jnp.float32) + refs[1][kind].astype(jnp.float32)

    for kind in range(2):
        total = base(kind)
        for step in range(places):
            place = places - 1 - step if kind else step
            out_ref[place, kind] = total.astype(jnp.bfloat16)
            total = total + slices_ref[place, kind].astype(jnp.float32)
    me = lax.axis_index("rest")
    for k, piece in enumerate(pieces):
        piece[...] = out_ref[me ^ k]


def small_call(kernel, name, operands, outs, scratch=()):
    return pl.pallas_call(
        kernel,
        in_specs=[HELD] * len(operands),
        out_specs=[HELD] * len(outs),
        out_shape=[pltpu.VMEM(shape, jnp.bfloat16) for shape in outs],
        scratch_shapes=[pltpu.VMEM(shape, jnp.bfloat16) for shape in scratch],
        compiler_params=params(8),
        name=name,
    )(*map(held, operands))


def exclusive_scan(pieces, work):
    places, chips = len(pieces), lax.axis_size("x")
    split = chips == 2
    piece = pieces[0].shape
    part, several = piece[1:], (places,) + piece
    halves_swap = [(0, 1), (1, 0)]
    done = [work(0, pieces[1])]
    slices, total = small_call(
        functools.partial(group_kernel, places), "group", [*reversed(swap(pieces, "rest")), *done], [several, piece]
    )
    other = lax.ppermute(total, "core", halves_swap)
    found = small_call(
        functools.partial(chip_kernel, split), "chip", [total, other], [part] * (chips + 1 if split else chips - 1)
    )
    sends, first = found[: chips - 1], found[chips - 1 :]
    done.append(work(1, sends[0]))
    near = swap([None, *sends], "x")[1:]
    crossed = [first[0], lax.ppermute(first[1], "half", halves_swap)] if split else []
    before, cross = small_call(
        functools.partial(half_kernel, split, chips), "half", [total, other, *near, done[1]], [part if split else piece] * 2
    )
    done.append(work(2, before))
    crossed += [before, lax.ppermute(cross, "half", halves_swap)]
    pieces = small_call(
        functools.partial(scan_kernel, split), "scan", [slices, *crossed, done[2]], [piece] * places, [several]
    )
    return swap(pieces, "rest"), done


def arrive(source, target, sem):
    copy = pltpu.make_async_copy(source, target, sem)
    copy.start()
    return copy


def halves(extent):
    return [pl.ds(half * (extent // 2), extent // 2) for half in range(2)]


def states_of(queries, keys, values, grads, state_ref):
    for head in range(state_ref.shape[1] // DH):
        lanes = pl.ds(head * DH, DH)
        for kind, (left, right) in enumerate(((keys, values), (queries, grads))):
            state_ref[kind, lanes] = mul(left[:, lanes], right[:, lanes], ROWS_ROWS).astype(jnp.bfloat16)


def kinds_of(ref, piece, width):
    return [ref.at[:, pl.ds((3 * piece + kind) * width, width)] for kind in range(3)]


def home_of(k, width):
    return pl.ds(pl.multiple_of((lax.axis_index("rest") ^ k) * width, width), width)


def joined(refs):
    return jnp.concatenate([ref[...] for ref in refs], axis=1)


def others_kernel(
    cotangent_hbm, w_out_hbm, tokens_hbm, w_query_hbm, w_key_hbm, w_value_hbm,
    cotangent, tokens, w_query, w_key, w_value, grad_out, projected, *refs,
):
    *states, w_out, total, sems = refs
    places = len(states) + 1
    width = grad_out.shape[1] // (places - 1)
    count = [0]

    def bring(source, target):
        count[0] += 1
        return arrive(source, target, sems.at[count[0] - 1])

    parts = halves(tokens.shape[1])
    first = []
    for lanes in parts:
        here = [bring(cotangent_hbm.at[:, lanes], cotangent.at[:, lanes])]
        for k in range(1, places):
            here.append(bring(w_out_hbm.at[home_of(k, width), lanes], w_out.at[pl.ds((k - 1) * width, width), lanes]))
        first.append(here)
    weights = w_query, w_key, w_value
    copies = []
    stage = pl.when(lax.axis_index("rest") >= 0)
    for half, (lanes, here) in enumerate(zip(parts, first)):
        for copy in here:
            copy.wait()
        if half == 0:
            copies.append([bring(tokens_hbm, tokens), bring(w_query_hbm, w_query)])
        else:
            copies.append([bring(w_key_hbm, w_key)])

        @stage
        def _(half=half, lanes=lanes):
            term = mul(cotangent[:, lanes], w_out[:, lanes], LAST_LAST)
            if half == 0:
                total[...] = term
            else:
                grad_out[...] = (total[...] + term).astype(jnp.bfloat16)

    for kind, weight in enumerate(weights):
        for copy in copies[kind]:
            copy.wait()
        if kind == 0:
            copies.append([bring(w_value_hbm, w_value)])

        @stage
        def _(kind=kind, weight=weight):
            product = mul(tokens[...], joined([weight.at[:, home_of(k, width)] for k in range(1, places)]))
            for k in range(1, places):
                kinds_of(projected, k - 1, width)[kind][...] = product[:, (k - 1) * width : k * width].astype(jnp.bfloat16)

    for k in range(1, places):
        states_of(*kinds_of(projected, k - 1, width), grad_out.at[:, pl.ds((k - 1) * width, width)], states[k - 1])


def own_kernel(cotangent, tokens, w_query, w_key, w_value, w_out_hbm, grad_out, projected, state, w_out, sems):
    width = w_out.shape[0]
    copy = arrive(w_out_hbm.at[home_of(0, width)], w_out, sems.at[0])
    weights = [weight.at[:, home_of(0, width)] for weight in (w_query, w_key, w_value)]

    @pl.when(lax.axis_index("rest") >= 0)
    def _():
        projected[...] = mul(tokens[...], joined(weights)).astype(jnp.bfloat16)

    copy.wait()
    grad_out[...] = mul(cotangent[...], w_out[...], LAST_LAST).astype(jnp.bfloat16)
    states_of(*kinds_of(projected, 0, width), grad_out, state)


def operands_of(piece, width, own, others, own_grad, others_grad):
    if piece == 0:
        return (*kinds_of(own, 0, width), own_grad)
    return (*kinds_of(others, piece - 1, width), others_grad.at[:, pl.ds((piece - 1) * width, width)])


def intra_kernel(pieces, own, others, own_grad, others_grad, _, parts):
    rows, width = parts.shape[0], parts.shape[1] // (3 * len(pieces))
    step = min(rows, 256)
    blocks = [pl.ds(at * step, step) for at in range(rows // step)]
    below = lax.broadcasted_iota(jnp.int32, (step, step), 0) >= lax.broadcasted_iota(jnp.int32, (step, step), 1)

    def score(left, right, masked):
        found = mul(left, right, LAST_LAST)
        return (jnp.where(below, found, 0.0) if masked else found).astype(jnp.bfloat16)

    for at, piece in enumerate(pieces):
        query_ref, keys_ref, values_ref, grad_out_ref = operands_of(piece, width, own, others, own_grad, others_grad)
        grad_query_ref, grad_key_ref, grad_value_ref = kinds_of(parts, at, width)
        for head in range(width // DH):
            lanes = pl.ds(head * DH, DH)
            query_t = query_ref[:, lanes].T
            grad_out_t = grad_out_ref[:, lanes].T
            key_sums, value_sums = [None] * len(blocks), [None] * len(blocks)
            for t, mine in enumerate(blocks):
                span = slice(t * step, (t + 1) * step)
                query_sum = None
                for s, theirs in enumerate(blocks[: t + 1]):
                    probe = score(grad_out_ref[mine, lanes], values_ref[theirs, lanes], s == t)
                    attend = score(query_ref[mine, lanes], keys_ref[theirs, lanes], s == t)
                    term = mul(probe, keys_ref[theirs, lanes])
                    query_sum = term if query_sum is None else query_sum + term
                    term = mul(query_t[:, span], probe)
                    key_sums[s] = term if key_sums[s] is None else key_sums[s] + term
                    term = mul(grad_out_t[:, span], attend)
                    value_sums[s] = term if value_sums[s] is None else value_sums[s] + term
                grad_query_ref[mine, lanes] = query_sum.astype(jnp.bfloat16)
            for s, theirs in enumerate(blocks):
                grad_key_ref[theirs, lanes] = key_sums[s].T.astype(jnp.bfloat16)
                grad_value_ref[theirs, lanes] = value_sums[s].T.astype(jnp.bfloat16)


def finish_kernel(factor, piece, at, last, *refs):
    if piece:
        total, *refs = refs
    parts, own, others, own_grad, others_grad, w_query, w_key, w_value, sums, *refs = refs
    width = own_grad.shape[1]
    if last:
        out_hbm, grads, out, sems = refs
    else:
        out, grads = refs
    _, keys, values, grad_out = operands_of(piece, width, own, others, own_grad, others_grad)
    for head in range(width // DH):
        lanes = pl.ds(head * DH, DH)
        prior, later = sums[0, lanes], sums[1, lanes]
        inters = (
            mul(grad_out[:, lanes], prior, LAST_LAST),
            mul(values[:, lanes], later, LAST_LAST),
            mul(keys[:, lanes], later),
        )
        for inter, part, grad in zip(inters, kinds_of(parts, at, width), kinds_of(grads, 0, width)):
            grad[:, lanes] = (factor * (inter + part[:, lanes].astype(jnp.float32))).astype(jnp.bfloat16)
    columns = home_of(piece, width)
    weights = w_query, w_key, w_value
    if not last:
        term = mul(grads[...], joined([weight.at[:, columns] for weight in weights]), LAST_LAST)
        out[...] = total[...] + term if piece else term
        return
    sent = []
    for half, rows in enumerate(halves(w_query.shape[0])):
        term = mul(grads[...], joined([weight.at[rows, columns] for weight in weights]), LAST_LAST)
        out[:, rows] = (total[:, rows] + term).astype(jnp.bfloat16)
        sent.append(arrive(out.at[:, rows], out_hbm.at[:, rows], sems.at[half]))
    for copy in sent:
        copy.wait()


def shards(tokens, cotangent, w_query, w_key, w_value, w_out):
    rows, wide = tokens.shape
    columns = w_query.shape[1]
    places = lax.axis_size("rest")
    width = columns // places
    factor = 1.0 / math.sqrt(DH * rows * lax.axis_size(AXES))

    def vmem(*shape):
        return pltpu.VMEM(shape, jnp.bfloat16)

    def cost(flops, bytes_accessed):
        return pl.CostEstimate(flops=flops, bytes_accessed=bytes_accessed, transcendentals=0)

    piece = vmem(2, width, DH)
    weight = vmem(wide, columns)
    found = pl.pallas_call(
        others_kernel,
        in_specs=[FAR] * 6,
        out_specs=[HELD] * (6 + places),
        out_shape=[
            vmem(rows, wide), vmem(rows, wide), weight, weight, weight,
            vmem(rows, columns - width), vmem(rows, 3 * (columns - width)),
        ] + [piece] * (places - 1),
        scratch_shapes=[
            vmem(columns - width, wide), pltpu.VMEM((rows, columns - width), jnp.float32),
            pltpu.SemaphoreType.DMA((2 * places + 4,)),
        ],
        compiler_params=params(16),
        cost_estimate=cost(8 * rows * wide * (columns - width), 4 * (rows + 2 * columns) * wide),
        name="project_others",
    )(*map(far, (cotangent, w_out, tokens, w_query, w_key, w_value)))
    near, (others_grad, others), pieces = found[:5], found[5:7], found[7:]
    own_grad, own, own_piece = pl.pallas_call(
        own_kernel,
        in_specs=[HELD] * 5 + [FAR],
        out_specs=[HELD] * 3,
        out_shape=[vmem(rows, width), vmem(rows, 3 * width), piece],
        scratch_shapes=[vmem(width, wide), pltpu.SemaphoreType.DMA((1,))],
        compiler_params=params(16),
        cost_estimate=cost(8 * rows * wide * width, 8 * wide * width),
        name="project_own",
    )(*map(held, near), far(w_out))
    operands = own, others, own_grad, others_grad
    turns = [(places - 1,), (1,), (0, *range(2, places - 1))]

    def intra(step, after):
        share = len(turns[step])
        views = operands if step == 2 else (others, others, others_grad, others_grad)
        return pl.pallas_call(
            functools.partial(intra_kernel, turns[step]),
            in_specs=[HELD] * 5,
            out_specs=HELD,
            out_shape=vmem(rows, 3 * width * share),
            compiler_params=params(12),
            cost_estimate=cost(10 * rows * rows * width * share, 14 * rows * width * share),
            name="intra",
        )(*map(held, (*views, after)))

    pieces, parts = exclusive_scan([own_piece, *pieces], intra)
    part_of = {piece: (step, at) for step, turn in enumerate(turns) for at, piece in enumerate(turn)}
    total = []
    for k in range(places):
        last = k == places - 1
        total = [pl.pallas_call(
            functools.partial(finish_kernel, factor, k, part_of[k][1], last),
            in_specs=[HELD] * (9 + len(total)),
            out_specs=FAR if last else HELD,
            out_shape=jax.ShapeDtypeStruct((rows, wide), jnp.bfloat16) if last else pltpu.VMEM((rows, wide), jnp.float32),
            scratch_shapes=[vmem(rows, 3 * width)] + ([vmem(rows, wide), pltpu.SemaphoreType.DMA((2,))] if last else []),
            compiler_params=params(20),
            cost_estimate=cost(6 * rows * width * (wide + DH), 6 * (rows + wide) * width),
            name="finish",
        )(*map(held, (*total, parts[part_of[k][0]], *operands, *near[2:], pieces[k])))]
    return total[0]


def solution(mesh):
    groups, places = mesh.devices.shape
    mesh = jax.sharding.Mesh(mesh.devices.reshape(groups // 2, 2, 2, places // 2), AXES)
    placed = (P(AXES, None), P(AXES, None), P(), P(), P(), P())
    return jax.shard_map(
        shards, mesh=mesh, in_specs=placed, out_specs=P(AXES, None), check_vma=False
    )
```

```python
import functools
import math

import jax
import jax.numpy as jnp
from jax import lax
from jax.experimental import pallas as pl
from jax.experimental.pallas import tpu as pltpu
from jax.sharding import PartitionSpec as P

DH = 128
AXES = ("x", "core", "half", "rest")
ROWS_ROWS = (((0,), (0,)), ((), ()))
LAST_LAST = (((1,), (1,)), ((), ()))
PLAIN = (((1,), (0,)), ((), ()))


def mul(left, right, dims=PLAIN):
    return lax.dot_general(left, right, dims, preferred_element_type=jnp.float32)


HELD = pl.BlockSpec(memory_space=pltpu.VMEM)
FAR = pl.BlockSpec(memory_space=pl.ANY)


def held(array):
    return pltpu.with_memory_space_constraint(array, pltpu.VMEM)


def far(array):
    return pltpu.with_memory_space_constraint(array, pltpu.HBM)


def params(mebibytes):
    return pltpu.CompilerParams(vmem_limit_bytes=mebibytes << 20)


def swap(pieces, axis):
    places = len(pieces)
    swapped = list(pieces)
    for k in reversed(range(1, places)):
        swapped[k] = lax.ppermute(pieces[k], axis, [(place, place ^ k) for place in range(places)])
    return swapped


def group_kernel(places, *refs):
    slices, (slices_ref, sum_ref) = refs[:places], refs[-2:]
    me = lax.axis_index("rest")
    total = None
    for k, piece in enumerate(reversed(slices)):
        slices_ref[me ^ k] = piece[...]
        term = piece[...].astype(jnp.float32)
        total = term if total is None else total + term
    sum_ref[...] = total.astype(jnp.bfloat16)


def cross_of(kind, total, sum_ref, before_ref, cross_ref):
    before_ref[...] = total.astype(jnp.bfloat16)
    added = jnp.where(lax.axis_index("half") == kind, sum_ref[kind].astype(jnp.float32), 0.0)
    cross_ref[...] = (total + added).astype(jnp.bfloat16)


def core_before(kind, other_ref):
    return jnp.where(lax.axis_index("core") != kind, other_ref[kind].astype(jnp.float32), 0.0)


def chip_kernel(split, sum_ref, other_ref, *refs):
    chip = lax.axis_index("x")
    sends = refs[:-2] if split else refs
    for k, send in enumerate(sends):
        kind = jnp.where(chip < (chip ^ (k + 1)), 0, 1)
        send[...] = (sum_ref[kind].astype(jnp.float32) + other_ref[kind].astype(jnp.float32)).astype(jnp.bfloat16)
    if split:
        cross_of(chip, core_before(chip, other_ref), sum_ref, *refs[-2:])


def half_kernel(split, chips, sum_ref, other_ref, *refs):
    chip, outs = lax.axis_index("x"), refs[-2:]
    if split:
        total = core_before(1 - chip, other_ref) + refs[0][...].astype(jnp.float32)
        cross_of(1 - chip, total, sum_ref, *outs)
        return
    for kind in range(2):
        total = core_before(kind, other_ref)
        for k in range(1, chips):
            ahead = (chip ^ k) > chip if kind else (chip ^ k) < chip
            total = total + jnp.where(ahead, refs[k - 1][...].astype(jnp.float32), 0.0)
        cross_of(kind, total, sum_ref, *[out.at[kind] for out in outs])


def scan_kernel(split, slices_ref, *refs):
    places = slices_ref.shape[0]
    pieces, out_ref = refs[-1 - places : -1], refs[-1]
    chip = lax.axis_index("x")

    def base(kind):
        if split:
            first, first_cross, second, second_cross = [ref[...].astype(jnp.float32) for ref in refs[:4]]
            return jnp.where(chip == kind, first + first_cross, second + second_cross)
        return refs[0][kind].astype(jnp.float32) + refs[1][kind].astype(jnp.float32)

    for kind in range(2):
        total = base(kind)
        for step in range(places):
            place = places - 1 - step if kind else step
            out_ref[place, kind] = total.astype(jnp.bfloat16)
            total = total + slices_ref[place, kind].astype(jnp.float32)
    me = lax.axis_index("rest")
    for k, piece in enumerate(pieces):
        piece[...] = out_ref[me ^ k]


def small_call(kernel, name, operands, outs, scratch=()):
    return pl.pallas_call(
        kernel,
        in_specs=[HELD] * len(operands),
        out_specs=[HELD] * len(outs),
        out_shape=[pltpu.VMEM(shape, jnp.bfloat16) for shape in outs],
        scratch_shapes=[pltpu.VMEM(shape, jnp.bfloat16) for shape in scratch],
        compiler_params=params(8),
        name=name,
    )(*map(held, operands))


def exclusive_scan(pieces, work):
    places, chips = len(pieces), lax.axis_size("x")
    split = chips == 2
    piece = pieces[0].shape
    part, several = piece[1:], (places,) + piece
    halves_swap = [(0, 1), (1, 0)]
    done = [work(0, pieces[1])]
    slices, total = small_call(
        functools.partial(group_kernel, places), "group", [*reversed(swap(pieces, "rest")), *done], [several, piece]
    )
    other = lax.ppermute(total, "core", halves_swap)
    found = small_call(
        functools.partial(chip_kernel, split), "chip", [total, other], [part] * (chips + 1 if split else chips - 1)
    )
    sends, first = found[: chips - 1], found[chips - 1 :]
    done.append(work(1, sends[0]))
    near = swap([None, *sends], "x")[1:]
    crossed = [first[0], lax.ppermute(first[1], "half", halves_swap)] if split else []
    before, cross = small_call(
        functools.partial(half_kernel, split, chips), "half", [total, other, *near, done[1]], [part if split else piece] * 2
    )
    done.append(work(2, before))
    crossed += [before, lax.ppermute(cross, "half", halves_swap)]
    pieces = small_call(
        functools.partial(scan_kernel, split), "scan", [slices, *crossed, done[2]], [piece] * places, [several]
    )
    return swap(pieces, "rest"), done


def arrive(source, target, sem):
    copy = pltpu.make_async_copy(source, target, sem)
    copy.start()
    return copy


def halves(extent):
    return [pl.ds(half * (extent // 2), extent // 2) for half in range(2)]


def states_of(queries, keys, values, grads, state_ref):
    for head in range(state_ref.shape[1] // DH):
        lanes = pl.ds(head * DH, DH)
        for kind, (left, right) in enumerate(((keys, values), (queries, grads))):
            state_ref[kind, lanes] = mul(left[:, lanes], right[:, lanes], ROWS_ROWS).astype(jnp.bfloat16)


def kinds_of(ref, piece, width):
    return [ref.at[:, pl.ds((3 * piece + kind) * width, width)] for kind in range(3)]


def home_of(k, width):
    return pl.ds(pl.multiple_of((lax.axis_index("rest") ^ k) * width, width), width)


def joined(refs):
    return jnp.concatenate([ref[...] for ref in refs], axis=1)


def others_kernel(
    cotangent_hbm, w_out_hbm, tokens_hbm, w_query_hbm, w_key_hbm, w_value_hbm,
    cotangent, tokens, w_query, w_key, w_value, grad_out, projected, *refs,
):
    *states, w_out, total, sems = refs
    places = len(states) + 1
    width = grad_out.shape[1] // (places - 1)
    count = [0]

    def bring(source, target):
        count[0] += 1
        return arrive(source, target, sems.at[count[0] - 1])

    parts = halves(tokens.shape[1])
    first = []
    for lanes in parts:
        here = [bring(cotangent_hbm.at[:, lanes], cotangent.at[:, lanes])]
        for k in range(1, places):
            here.append(bring(w_out_hbm.at[home_of(k, width), lanes], w_out.at[pl.ds((k - 1) * width, width), lanes]))
        first.append(here)
    weights = w_query, w_key, w_value
    copies = [[bring(tokens_hbm, tokens), bring(w_query_hbm, w_query)]]
    stage = pl.when(lax.axis_index("rest") >= 0)
    for half, (lanes, here) in enumerate(zip(parts, first)):
        for copy in here:
            copy.wait()
        copies.append([bring((w_key_hbm, w_value_hbm)[half], weights[half + 1])])

        @stage
        def _(half=half, lanes=lanes):
            term = mul(cotangent[:, lanes], w_out[:, lanes], LAST_LAST)
            if half == 0:
                total[...] = term
            else:
                grad_out[...] = (total[...] + term).astype(jnp.bfloat16)

    for kind, weight in enumerate(weights):
        for copy in copies[kind]:
            copy.wait()

        @stage
        def _(kind=kind, weight=weight):
            product = mul(tokens[...], joined([weight.at[:, home_of(k, width)] for k in range(1, places)]))
            for k in range(1, places):
                kinds_of(projected, k - 1, width)[kind][...] = product[:, (k - 1) * width : k * width].astype(jnp.bfloat16)

    for k in range(1, places):
        states_of(*kinds_of(projected, k - 1, width), grad_out.at[:, pl.ds((k - 1) * width, width)], states[k - 1])


def own_kernel(cotangent, tokens, w_query, w_key, w_value, w_out_hbm, grad_out, projected, state, w_out, sems):
    width = w_out.shape[0]
    copy = arrive(w_out_hbm.at[home_of(0, width)], w_out, sems.at[0])
    weights = [weight.at[:, home_of(0, width)] for weight in (w_query, w_key, w_value)]

    @pl.when(lax.axis_index("rest") >= 0)
    def _():
        projected[...] = mul(tokens[...], joined(weights)).astype(jnp.bfloat16)

    copy.wait()
    grad_out[...] = mul(cotangent[...], w_out[...], LAST_LAST).astype(jnp.bfloat16)
    states_of(*kinds_of(projected, 0, width), grad_out, state)


def operands_of(piece, width, own, others, own_grad, others_grad):
    if piece == 0:
        return (*kinds_of(own, 0, width), own_grad)
    return (*kinds_of(others, piece - 1, width), others_grad.at[:, pl.ds((piece - 1) * width, width)])


def intra_kernel(pieces, own, others, own_grad, others_grad, _, parts):
    rows, width = parts.shape[0], parts.shape[1] // (3 * len(pieces))
    step = min(rows, 256)
    blocks = [pl.ds(at * step, step) for at in range(rows // step)]
    below = lax.broadcasted_iota(jnp.int32, (step, step), 0) >= lax.broadcasted_iota(jnp.int32, (step, step), 1)

    def score(left, right, masked):
        found = mul(left, right, LAST_LAST)
        return (jnp.where(below, found, 0.0) if masked else found).astype(jnp.bfloat16)

    for at, piece in enumerate(pieces):
        query_ref, keys_ref, values_ref, grad_out_ref = operands_of(piece, width, own, others, own_grad, others_grad)
        grad_query_ref, grad_key_ref, grad_value_ref = kinds_of(parts, at, width)
        for head in range(width // DH):
            lanes = pl.ds(head * DH, DH)
            query_t = query_ref[:, lanes].T
            grad_out_t = grad_out_ref[:, lanes].T
            key_sums, value_sums = [None] * len(blocks), [None] * len(blocks)
            for t, mine in enumerate(blocks):
                span = slice(t * step, (t + 1) * step)
                query_sum = None
                for s, theirs in enumerate(blocks[: t + 1]):
                    probe = score(grad_out_ref[mine, lanes], values_ref[theirs, lanes], s == t)
                    attend = score(query_ref[mine, lanes], keys_ref[theirs, lanes], s == t)
                    term = mul(probe, keys_ref[theirs, lanes])
                    query_sum = term if query_sum is None else query_sum + term
                    term = mul(query_t[:, span], probe)
                    key_sums[s] = term if key_sums[s] is None else key_sums[s] + term
                    term = mul(grad_out_t[:, span], attend)
                    value_sums[s] = term if value_sums[s] is None else value_sums[s] + term
                grad_query_ref[mine, lanes] = query_sum.astype(jnp.bfloat16)
            for s, theirs in enumerate(blocks):
                grad_key_ref[theirs, lanes] = key_sums[s].T.astype(jnp.bfloat16)
                grad_value_ref[theirs, lanes] = value_sums[s].T.astype(jnp.bfloat16)


def finish_kernel(factor, piece, at, last, *refs):
    if piece:
        total, *refs = refs
    parts, own, others, own_grad, others_grad, w_query, w_key, w_value, sums, *refs = refs
    width = own_grad.shape[1]
    if last:
        out_hbm, grads, out, sems = refs
    else:
        out, grads = refs
    _, keys, values, grad_out = operands_of(piece, width, own, others, own_grad, others_grad)
    for head in range(width // DH):
        lanes = pl.ds(head * DH, DH)
        prior, later = sums[0, lanes], sums[1, lanes]
        inters = (
            mul(grad_out[:, lanes], prior, LAST_LAST),
            mul(values[:, lanes], later, LAST_LAST),
            mul(keys[:, lanes], later),
        )
        for inter, part, grad in zip(inters, kinds_of(parts, at, width), kinds_of(grads, 0, width)):
            grad[:, lanes] = (factor * (inter + part[:, lanes].astype(jnp.float32))).astype(jnp.bfloat16)
    columns = home_of(piece, width)
    weights = w_query, w_key, w_value
    if not last:
        term = mul(grads[...], joined([weight.at[:, columns] for weight in weights]), LAST_LAST)
        out[...] = total[...] + term if piece else term
        return
    sent = []
    for half, rows in enumerate(halves(w_query.shape[0])):
        @pl.when(lax.axis_index("rest") >= 0)
        def _(rows=rows):
            term = mul(grads[...], joined([weight.at[rows, columns] for weight in weights]), LAST_LAST)
            out[:, rows] = (total[:, rows] + term).astype(jnp.bfloat16)

        sent.append(arrive(out.at[:, rows], out_hbm.at[:, rows], sems.at[half]))
    for copy in sent:
        copy.wait()


def shards(tokens, cotangent, w_query, w_key, w_value, w_out):
    rows, wide = tokens.shape
    columns = w_query.shape[1]
    places = lax.axis_size("rest")
    width = columns // places
    factor = 1.0 / math.sqrt(DH * rows * lax.axis_size(AXES))

    def vmem(*shape):
        return pltpu.VMEM(shape, jnp.bfloat16)

    def cost(flops, bytes_accessed):
        return pl.CostEstimate(flops=flops, bytes_accessed=bytes_accessed, transcendentals=0)

    piece = vmem(2, width, DH)
    weight = vmem(wide, columns)
    found = pl.pallas_call(
        others_kernel,
        in_specs=[FAR] * 6,
        out_specs=[HELD] * (6 + places),
        out_shape=[
            vmem(rows, wide), vmem(rows, wide), weight, weight, weight,
            vmem(rows, columns - width), vmem(rows, 3 * (columns - width)),
        ] + [piece] * (places - 1),
        scratch_shapes=[
            vmem(columns - width, wide), pltpu.VMEM((rows, columns - width), jnp.float32),
            pltpu.SemaphoreType.DMA((2 * places + 4,)),
        ],
        compiler_params=params(16),
        cost_estimate=cost(8 * rows * wide * (columns - width), 4 * (rows + 2 * columns) * wide),
        name="project_others",
    )(*map(far, (cotangent, w_out, tokens, w_query, w_key, w_value)))
    near, (others_grad, others), pieces = found[:5], found[5:7], found[7:]
    own_grad, own, own_piece = pl.pallas_call(
        own_kernel,
        in_specs=[HELD] * 5 + [FAR],
        out_specs=[HELD] * 3,
        out_shape=[vmem(rows, width), vmem(rows, 3 * width), piece],
        scratch_shapes=[vmem(width, wide), pltpu.SemaphoreType.DMA((1,))],
        compiler_params=params(16),
        cost_estimate=cost(8 * rows * wide * width, 8 * wide * width),
        name="project_own",
    )(*map(held, near), far(w_out))
    operands = own, others, own_grad, others_grad
    turns = [(places - 1,), (1,), (0, *range(2, places - 1))]

    def intra(step, after):
        share = len(turns[step])
        views = operands if step == 2 else (others, others, others_grad, others_grad)
        return pl.pallas_call(
            functools.partial(intra_kernel, turns[step]),
            in_specs=[HELD] * 5,
            out_specs=HELD,
            out_shape=vmem(rows, 3 * width * share),
            compiler_params=params(12),
            cost_estimate=cost(10 * rows * rows * width * share, 14 * rows * width * share),
            name="intra",
        )(*map(held, (*views, after)))

    pieces, parts = exclusive_scan([own_piece, *pieces], intra)
    part_of = {piece: (step, at) for step, turn in enumerate(turns) for at, piece in enumerate(turn)}
    total = []
    for k in range(places):
        last = k == places - 1
        total = [pl.pallas_call(
            functools.partial(finish_kernel, factor, k, part_of[k][1], last),
            in_specs=[HELD] * (9 + len(total)),
            out_specs=FAR if last else HELD,
            out_shape=jax.ShapeDtypeStruct((rows, wide), jnp.bfloat16) if last else pltpu.VMEM((rows, wide), jnp.float32),
            scratch_shapes=[vmem(rows, 3 * width)] + ([vmem(rows, wide), pltpu.SemaphoreType.DMA((2,))] if last else []),
            compiler_params=params(20),
            cost_estimate=cost(6 * rows * width * (wide + DH), 6 * (rows + wide) * width),
            name="finish",
        )(*map(held, (*total, parts[part_of[k][0]], *operands, *near[2:], pieces[k])))]
    return total[0]


def solution(mesh):
    groups, places = mesh.devices.shape
    mesh = jax.sharding.Mesh(mesh.devices.reshape(groups // 2, 2, 2, places // 2), AXES)
    placed = (P(AXES, None), P(AXES, None), P(), P(), P(), P())
    return jax.shard_map(
        shards, mesh=mesh, in_specs=placed, out_specs=P(AXES, None), check_vma=False
    )
```

```python
import functools
import math

import jax
import jax.numpy as jnp
from jax import lax
from jax.experimental import pallas as pl
from jax.experimental.pallas import tpu as pltpu
from jax.sharding import PartitionSpec as P

DH = 128
AXES = ("x", "core", "half", "rest")
ROWS_ROWS = (((0,), (0,)), ((), ()))
LAST_LAST = (((1,), (1,)), ((), ()))
PLAIN = (((1,), (0,)), ((), ()))


def mul(left, right, dims=PLAIN):
    return lax.dot_general(left, right, dims, preferred_element_type=jnp.float32)


HELD = pl.BlockSpec(memory_space=pltpu.VMEM)
FAR = pl.BlockSpec(memory_space=pl.ANY)


def held(array):
    return pltpu.with_memory_space_constraint(array, pltpu.VMEM)


def far(array):
    return pltpu.with_memory_space_constraint(array, pltpu.HBM)


def params(mebibytes):
    return pltpu.CompilerParams(vmem_limit_bytes=mebibytes << 20)


def swap(pieces, axis):
    places = len(pieces)
    swapped = list(pieces)
    for k in reversed(range(1, places)):
        swapped[k] = lax.ppermute(pieces[k], axis, [(place, place ^ k) for place in range(places)])
    return swapped


def group_kernel(places, *refs):
    slices, (slices_ref, sum_ref) = refs[:places], refs[-2:]
    me = lax.axis_index("rest")
    total = None
    for k, piece in enumerate(reversed(slices)):
        slices_ref[me ^ k] = piece[...]
        term = piece[...].astype(jnp.float32)
        total = term if total is None else total + term
    sum_ref[...] = total.astype(jnp.bfloat16)


def cross_of(kind, total, sum_ref, before_ref, cross_ref):
    before_ref[...] = total.astype(jnp.bfloat16)
    added = jnp.where(lax.axis_index("half") == kind, sum_ref[kind].astype(jnp.float32), 0.0)
    cross_ref[...] = (total + added).astype(jnp.bfloat16)


def core_before(kind, other_ref):
    return jnp.where(lax.axis_index("core") != kind, other_ref[kind].astype(jnp.float32), 0.0)


def chip_kernel(split, sum_ref, other_ref, *refs):
    chip = lax.axis_index("x")
    sends = refs[:-2] if split else refs
    for k, send in enumerate(sends):
        kind = jnp.where(chip < (chip ^ (k + 1)), 0, 1)
        send[...] = (sum_ref[kind].astype(jnp.float32) + other_ref[kind].astype(jnp.float32)).astype(jnp.bfloat16)
    if split:
        cross_of(chip, core_before(chip, other_ref), sum_ref, *refs[-2:])


def half_kernel(split, chips, sum_ref, other_ref, *refs):
    chip, outs = lax.axis_index("x"), refs[-2:]
    if split:
        total = core_before(1 - chip, other_ref) + refs[0][...].astype(jnp.float32)
        cross_of(1 - chip, total, sum_ref, *outs)
        return
    for kind in range(2):
        total = core_before(kind, other_ref)
        for k in range(1, chips):
            ahead = (chip ^ k) > chip if kind else (chip ^ k) < chip
            total = total + jnp.where(ahead, refs[k - 1][...].astype(jnp.float32), 0.0)
        cross_of(kind, total, sum_ref, *[out.at[kind] for out in outs])


def scan_kernel(split, slices_ref, *refs):
    places = slices_ref.shape[0]
    pieces, out_ref = refs[-1 - places : -1], refs[-1]
    chip = lax.axis_index("x")

    def base(kind):
        if split:
            first, first_cross, second, second_cross = [ref[...].astype(jnp.float32) for ref in refs[:4]]
            return jnp.where(chip == kind, first + first_cross, second + second_cross)
        return refs[0][kind].astype(jnp.float32) + refs[1][kind].astype(jnp.float32)

    for kind in range(2):
        total = base(kind)
        for step in range(places):
            place = places - 1 - step if kind else step
            out_ref[place, kind] = total.astype(jnp.bfloat16)
            total = total + slices_ref[place, kind].astype(jnp.float32)
    me = lax.axis_index("rest")
    for k, piece in enumerate(pieces):
        piece[...] = out_ref[me ^ k]


def small_call(kernel, name, operands, outs, scratch=()):
    return pl.pallas_call(
        kernel,
        in_specs=[HELD] * len(operands),
        out_specs=[HELD] * len(outs),
        out_shape=[pltpu.VMEM(shape, jnp.bfloat16) for shape in outs],
        scratch_shapes=[pltpu.VMEM(shape, jnp.bfloat16) for shape in scratch],
        compiler_params=params(8),
        name=name,
    )(*map(held, operands))


def exclusive_scan(pieces, work):
    places, chips = len(pieces), lax.axis_size("x")
    split = chips == 2
    piece = pieces[0].shape
    part, several = piece[1:], (places,) + piece
    halves_swap = [(0, 1), (1, 0)]
    done = [work(0, pieces[1])]
    slices, total = small_call(
        functools.partial(group_kernel, places), "group", [*reversed(swap(pieces, "rest")), *done], [several, piece]
    )
    other = lax.ppermute(total, "core", halves_swap)
    found = small_call(
        functools.partial(chip_kernel, split), "chip", [total, other], [part] * (chips + 1 if split else chips - 1)
    )
    sends, first = found[: chips - 1], found[chips - 1 :]
    done.append(work(1, sends[0]))
    near = swap([None, *sends], "x")[1:]
    crossed = [first[0], lax.ppermute(first[1], "half", halves_swap)] if split else []
    before, cross = small_call(
        functools.partial(half_kernel, split, chips), "half", [total, other, *near, done[1]], [part if split else piece] * 2
    )
    done.append(work(2, before))
    crossed += [before, lax.ppermute(cross, "half", halves_swap)]
    pieces = small_call(
        functools.partial(scan_kernel, split), "scan", [slices, *crossed, done[2]], [piece] * places, [several]
    )
    return swap(pieces, "rest"), done


def arrive(source, target, sem):
    copy = pltpu.make_async_copy(source, target, sem)
    copy.start()
    return copy


def halves(extent):
    return [pl.ds(half * (extent // 2), extent // 2) for half in range(2)]


def states_of(queries, keys, values, grads, state_ref):
    for head in range(state_ref.shape[1] // DH):
        lanes = pl.ds(head * DH, DH)
        for kind, (left, right) in enumerate(((keys, values), (queries, grads))):
            state_ref[kind, lanes] = mul(left[:, lanes], right[:, lanes], ROWS_ROWS).astype(jnp.bfloat16)


def kinds_of(ref, piece, width):
    return [ref.at[:, pl.ds((3 * piece + kind) * width, width)] for kind in range(3)]


def home_of(k, width):
    return pl.ds(pl.multiple_of((lax.axis_index("rest") ^ k) * width, width), width)


def joined(refs):
    return jnp.concatenate([ref[...] for ref in refs], axis=1)


def others_kernel(
    cotangent_hbm, w_out_hbm, tokens_hbm, w_query_hbm, w_key_hbm, w_value_hbm,
    cotangent, tokens, w_query, w_key, w_value, grad_out, projected, *refs,
):
    *states, w_out, total, sems = refs
    places = len(states) + 1
    width = grad_out.shape[1] // (places - 1)
    count = [0]

    def bring(source, target):
        count[0] += 1
        return arrive(source, target, sems.at[count[0] - 1])

    parts = halves(tokens.shape[1])
    first = []
    for lanes in parts:
        here = [bring(cotangent_hbm.at[:, lanes], cotangent.at[:, lanes])]
        for k in range(1, places):
            here.append(bring(w_out_hbm.at[home_of(k, width), lanes], w_out.at[pl.ds((k - 1) * width, width), lanes]))
        first.append(here)
    weights = w_query, w_key, w_value
    copies = [[bring(tokens_hbm, tokens), bring(w_query_hbm, w_query)]]
    stage = pl.when(lax.axis_index("rest") >= 0)
    for half, (lanes, here) in enumerate(zip(parts, first)):
        for copy in here:
            copy.wait()
        copies.append([bring((w_key_hbm, w_value_hbm)[half], weights[half + 1])])

        @stage
        def _(half=half, lanes=lanes):
            term = mul(cotangent[:, lanes], w_out[:, lanes], LAST_LAST)
            if half == 0:
                total[...] = term
            else:
                grad_out[...] = (total[...] + term).astype(jnp.bfloat16)

    for kind, weight in enumerate(weights):
        for copy in copies[kind]:
            copy.wait()

        @stage
        def _(kind=kind, weight=weight):
            product = mul(tokens[...], joined([weight.at[:, home_of(k, width)] for k in range(1, places)]))
            for k in range(1, places):
                kinds_of(projected, k - 1, width)[kind][...] = product[:, (k - 1) * width : k * width].astype(jnp.bfloat16)

    for k in range(1, places):
        states_of(*kinds_of(projected, k - 1, width), grad_out.at[:, pl.ds((k - 1) * width, width)], states[k - 1])


def own_kernel(cotangent, tokens, w_query, w_key, w_value, w_out_hbm, grad_out, projected, state, w_out, sems):
    width = w_out.shape[0]
    copy = arrive(w_out_hbm.at[home_of(0, width)], w_out, sems.at[0])
    weights = [weight.at[:, home_of(0, width)] for weight in (w_query, w_key, w_value)]

    @pl.when(lax.axis_index("rest") >= 0)
    def _():
        projected[...] = mul(tokens[...], joined(weights)).astype(jnp.bfloat16)

    copy.wait()
    grad_out[...] = mul(cotangent[...], w_out[...], LAST_LAST).astype(jnp.bfloat16)
    states_of(*kinds_of(projected, 0, width), grad_out, state)


def operands_of(piece, width, own, others, own_grad, others_grad):
    if piece == 0:
        return (*kinds_of(own, 0, width), own_grad)
    return (*kinds_of(others, piece - 1, width), others_grad.at[:, pl.ds((piece - 1) * width, width)])


def intra_kernel(pieces, own, others, own_grad, others_grad, _, parts):
    rows, width = parts.shape[0], parts.shape[1] // (3 * len(pieces))
    step = min(rows, 256)
    blocks = [pl.ds(at * step, step) for at in range(rows // step)]
    below = lax.broadcasted_iota(jnp.int32, (step, step), 0) >= lax.broadcasted_iota(jnp.int32, (step, step), 1)

    def score(left, right, masked):
        found = mul(left, right, LAST_LAST)
        return (jnp.where(below, found, 0.0) if masked else found).astype(jnp.bfloat16)

    for at, piece in enumerate(pieces):
        query_ref, keys_ref, values_ref, grad_out_ref = operands_of(piece, width, own, others, own_grad, others_grad)
        grad_query_ref, grad_key_ref, grad_value_ref = kinds_of(parts, at, width)
        for head in range(width // DH):
            lanes = pl.ds(head * DH, DH)
            query_t = query_ref[:, lanes].T
            grad_out_t = grad_out_ref[:, lanes].T
            key_sums, value_sums = [None] * len(blocks), [None] * len(blocks)
            for t, mine in enumerate(blocks):
                span = slice(t * step, (t + 1) * step)
                query_sum = None
                for s, theirs in enumerate(blocks[: t + 1]):
                    probe = score(grad_out_ref[mine, lanes], values_ref[theirs, lanes], s == t)
                    attend = score(query_ref[mine, lanes], keys_ref[theirs, lanes], s == t)
                    term = mul(probe, keys_ref[theirs, lanes])
                    query_sum = term if query_sum is None else query_sum + term
                    term = mul(query_t[:, span], probe)
                    key_sums[s] = term if key_sums[s] is None else key_sums[s] + term
                    term = mul(grad_out_t[:, span], attend)
                    value_sums[s] = term if value_sums[s] is None else value_sums[s] + term
                grad_query_ref[mine, lanes] = query_sum.astype(jnp.bfloat16)
            for s, theirs in enumerate(blocks):
                grad_key_ref[theirs, lanes] = key_sums[s].T.astype(jnp.bfloat16)
                grad_value_ref[theirs, lanes] = value_sums[s].T.astype(jnp.bfloat16)


def finish_kernel(factor, piece, at, last, *refs):
    if piece:
        total, *refs = refs
    parts, own, others, own_grad, others_grad, w_query, w_key, w_value, sums, *refs = refs
    width = own_grad.shape[1]
    if last:
        out_hbm, grads, out, sems = refs
    else:
        out, grads = refs
    _, keys, values, grad_out = operands_of(piece, width, own, others, own_grad, others_grad)
    for head in range(width // DH):
        lanes = pl.ds(head * DH, DH)
        prior, later = sums[0, lanes], sums[1, lanes]
        inters = (
            mul(grad_out[:, lanes], prior, LAST_LAST),
            mul(values[:, lanes], later, LAST_LAST),
            mul(keys[:, lanes], later),
        )
        for inter, part, grad in zip(inters, kinds_of(parts, at, width), kinds_of(grads, 0, width)):
            grad[:, lanes] = (factor * (inter + part[:, lanes].astype(jnp.float32))).astype(jnp.bfloat16)
    columns = home_of(piece, width)
    weights = w_query, w_key, w_value
    if not last:
        term = mul(grads[...], joined([weight.at[:, columns] for weight in weights]), LAST_LAST)
        out[...] = total[...] + term if piece else term
        return
    sent = []
    for half, rows in enumerate(halves(w_query.shape[0])):
        term = mul(grads[...], joined([weight.at[rows, columns] for weight in weights]), LAST_LAST)
        out[:, rows] = (total[:, rows] + term).astype(jnp.bfloat16)
        sent.append(arrive(out.at[:, rows], out_hbm.at[:, rows], sems.at[half]))
    for copy in sent:
        copy.wait()


def shards(tokens, cotangent, w_query, w_key, w_value, w_out):
    rows, wide = tokens.shape
    columns = w_query.shape[1]
    places = lax.axis_size("rest")
    width = columns // places
    factor = 1.0 / math.sqrt(DH * rows * lax.axis_size(AXES))

    def vmem(*shape):
        return pltpu.VMEM(shape, jnp.bfloat16)

    def cost(flops, bytes_accessed):
        return pl.CostEstimate(flops=flops, bytes_accessed=bytes_accessed, transcendentals=0)

    piece = vmem(2, width, DH)
    weight = vmem(wide, columns)
    found = pl.pallas_call(
        others_kernel,
        in_specs=[FAR] * 6,
        out_specs=[HELD] * (6 + places),
        out_shape=[
            vmem(rows, wide), vmem(rows, wide), weight, weight, weight,
            vmem(rows, columns - width), vmem(rows, 3 * (columns - width)),
        ] + [piece] * (places - 1),
        scratch_shapes=[
            vmem(columns - width, wide), pltpu.VMEM((rows, columns - width), jnp.float32),
            pltpu.SemaphoreType.DMA((2 * places + 4,)),
        ],
        compiler_params=params(16),
        cost_estimate=cost(8 * rows * wide * (columns - width), 4 * (rows + 2 * columns) * wide),
        name="project_others",
    )(*map(far, (cotangent, w_out, tokens, w_query, w_key, w_value)))
    near, (others_grad, others), pieces = found[:5], found[5:7], found[7:]
    own_grad, own, own_piece = pl.pallas_call(
        own_kernel,
        in_specs=[HELD] * 5 + [FAR],
        out_specs=[HELD] * 3,
        out_shape=[vmem(rows, width), vmem(rows, 3 * width), piece],
        scratch_shapes=[vmem(width, wide), pltpu.SemaphoreType.DMA((1,))],
        compiler_params=params(16),
        cost_estimate=cost(8 * rows * wide * width, 8 * wide * width),
        name="project_own",
    )(*map(held, near), far(w_out))
    operands = own, others, own_grad, others_grad
    turns = [(places - 1,), (1,), (0, *range(2, places - 1))]

    def intra(step, after):
        share = len(turns[step])
        views = operands if step == 2 else (others, others, others_grad, others_grad)
        return pl.pallas_call(
            functools.partial(intra_kernel, turns[step]),
            in_specs=[HELD] * 5,
            out_specs=HELD,
            out_shape=vmem(rows, 3 * width * share),
            compiler_params=params(12),
            cost_estimate=cost(10 * rows * rows * width * share, 14 * rows * width * share),
            name="intra",
        )(*map(held, (*views, after)))

    pieces, parts = exclusive_scan([own_piece, *pieces], intra)
    part_of = {piece: (step, at) for step, turn in enumerate(turns) for at, piece in enumerate(turn)}
    total = []
    for k in range(places):
        last = k == places - 1
        total = [pl.pallas_call(
            functools.partial(finish_kernel, factor, k, part_of[k][1], last),
            in_specs=[HELD] * (9 + len(total)),
            out_specs=FAR if last else HELD,
            out_shape=jax.ShapeDtypeStruct((rows, wide), jnp.bfloat16) if last else pltpu.VMEM((rows, wide), jnp.float32),
            scratch_shapes=[vmem(rows, 3 * width)] + ([vmem(rows, wide), pltpu.SemaphoreType.DMA((2,))] if last else []),
            compiler_params=params(20),
            cost_estimate=cost(6 * rows * width * (wide + DH), 6 * (rows + wide) * width),
            name="finish",
        )(*map(held, (*total, parts[part_of[k][0]], *operands, *near[2:], pieces[k])))]
    return total[0]


def solution(mesh):
    groups, places = mesh.devices.shape
    mesh = jax.sharding.Mesh(mesh.devices.reshape(groups // 2, 2, 2, places // 2), AXES)
    placed = (P(AXES, None), P(AXES, None), P(), P(), P(), P())
    return jax.shard_map(
        shards, mesh=mesh, in_specs=placed, out_specs=P(AXES, None), check_vma=False
    )
```

```python
import functools
import math

import jax
import jax.numpy as jnp
from jax import lax
from jax.experimental import pallas as pl
from jax.experimental.pallas import tpu as pltpu
from jax.sharding import PartitionSpec as P

DH = 128
AXES = ("x", "core", "half", "rest")
ROWS_ROWS = (((0,), (0,)), ((), ()))
LAST_LAST = (((1,), (1,)), ((), ()))
PLAIN = (((1,), (0,)), ((), ()))


def mul(left, right, dims=PLAIN):
    return lax.dot_general(left, right, dims, preferred_element_type=jnp.float32)


HELD = pl.BlockSpec(memory_space=pltpu.VMEM)
FAR = pl.BlockSpec(memory_space=pl.ANY)


def held(array):
    return pltpu.with_memory_space_constraint(array, pltpu.VMEM)


def far(array):
    return pltpu.with_memory_space_constraint(array, pltpu.HBM)


def params(mebibytes):
    return pltpu.CompilerParams(vmem_limit_bytes=mebibytes << 20)


def swap(pieces, axis):
    places = len(pieces)
    swapped = list(pieces)
    for k in reversed(range(1, places)):
        swapped[k] = lax.ppermute(pieces[k], axis, [(place, place ^ k) for place in range(places)])
    return swapped


def group_kernel(places, *refs):
    slices, (slices_ref, sum_ref) = refs[:places], refs[-2:]
    me = lax.axis_index("rest")
    total = None
    for k, piece in enumerate(reversed(slices)):
        slices_ref[me ^ k] = piece[...]
        term = piece[...].astype(jnp.float32)
        total = term if total is None else total + term
    sum_ref[...] = total.astype(jnp.bfloat16)


def cross_of(kind, total, sum_ref, before_ref, cross_ref):
    before_ref[...] = total.astype(jnp.bfloat16)
    added = jnp.where(lax.axis_index("half") == kind, sum_ref[kind].astype(jnp.float32), 0.0)
    cross_ref[...] = (total + added).astype(jnp.bfloat16)


def core_before(kind, other_ref):
    return jnp.where(lax.axis_index("core") != kind, other_ref[kind].astype(jnp.float32), 0.0)


def chip_kernel(split, sum_ref, other_ref, *refs):
    chip = lax.axis_index("x")
    sends = refs[:-2] if split else refs
    for k, send in enumerate(sends):
        kind = jnp.where(chip < (chip ^ (k + 1)), 0, 1)
        send[...] = (sum_ref[kind].astype(jnp.float32) + other_ref[kind].astype(jnp.float32)).astype(jnp.bfloat16)
    if split:
        cross_of(chip, core_before(chip, other_ref), sum_ref, *refs[-2:])


def half_kernel(split, chips, sum_ref, other_ref, *refs):
    chip, outs = lax.axis_index("x"), refs[-2:]
    if split:
        total = core_before(1 - chip, other_ref) + refs[0][...].astype(jnp.float32)
        cross_of(1 - chip, total, sum_ref, *outs)
        return
    for kind in range(2):
        total = core_before(kind, other_ref)
        for k in range(1, chips):
            ahead = (chip ^ k) > chip if kind else (chip ^ k) < chip
            total = total + jnp.where(ahead, refs[k - 1][...].astype(jnp.float32), 0.0)
        cross_of(kind, total, sum_ref, *[out.at[kind] for out in outs])


def scan_kernel(split, slices_ref, *refs):
    places = slices_ref.shape[0]
    pieces, out_ref = refs[-1 - places : -1], refs[-1]
    chip = lax.axis_index("x")

    def base(kind):
        if split:
            first, first_cross, second, second_cross = [ref[...].astype(jnp.float32) for ref in refs[:4]]
            return jnp.where(chip == kind, first + first_cross, second + second_cross)
        return refs[0][kind].astype(jnp.float32) + refs[1][kind].astype(jnp.float32)

    for kind in range(2):
        total = base(kind)
        for step in range(places):
            place = places - 1 - step if kind else step
            out_ref[place, kind] = total.astype(jnp.bfloat16)
            total = total + slices_ref[place, kind].astype(jnp.float32)
    me = lax.axis_index("rest")
    for k, piece in enumerate(pieces):
        piece[...] = out_ref[me ^ k]


def small_call(kernel, name, operands, outs, scratch=()):
    return pl.pallas_call(
        kernel,
        in_specs=[HELD] * len(operands),
        out_specs=[HELD] * len(outs),
        out_shape=[pltpu.VMEM(shape, jnp.bfloat16) for shape in outs],
        scratch_shapes=[pltpu.VMEM(shape, jnp.bfloat16) for shape in scratch],
        compiler_params=params(8),
        name=name,
    )(*map(held, operands))


def exclusive_scan(pieces, work):
    places, chips = len(pieces), lax.axis_size("x")
    split = chips == 2
    piece = pieces[0].shape
    part, several = piece[1:], (places,) + piece
    halves_swap = [(0, 1), (1, 0)]
    done = [work(0, pieces[1])]
    slices, total = small_call(
        functools.partial(group_kernel, places), "group", [*reversed(swap(pieces, "rest")), *done], [several, piece]
    )
    other = lax.ppermute(total, "core", halves_swap)
    found = small_call(
        functools.partial(chip_kernel, split), "chip", [total, other], [part] * (chips + 1 if split else chips - 1)
    )
    sends, first = found[: chips - 1], found[chips - 1 :]
    done.append(work(1, sends[0]))
    near = swap([None, *sends], "x")[1:]
    crossed = [first[0], lax.ppermute(first[1], "half", halves_swap)] if split else []
    before, cross = small_call(
        functools.partial(half_kernel, split, chips), "half", [total, other, *near, done[1]], [part if split else piece] * 2
    )
    done.append(work(2, before))
    crossed += [before, lax.ppermute(cross, "half", halves_swap)]
    pieces = small_call(
        functools.partial(scan_kernel, split), "scan", [slices, *crossed, done[2]], [piece] * places, [several]
    )
    return swap(pieces, "rest"), done


def arrive(source, target, sem):
    copy = pltpu.make_async_copy(source, target, sem)
    copy.start()
    return copy


def halves(extent):
    return [pl.ds(half * (extent // 2), extent // 2) for half in range(2)]


def states_of(queries, keys, values, grads, state_ref):
    for head in range(state_ref.shape[1] // DH):
        lanes = pl.ds(head * DH, DH)
        for kind, (left, right) in enumerate(((keys, values), (queries, grads))):
            state_ref[kind, lanes] = mul(left[:, lanes], right[:, lanes], ROWS_ROWS).astype(jnp.bfloat16)


def kinds_of(ref, piece, width):
    return [ref.at[:, pl.ds((3 * piece + kind) * width, width)] for kind in range(3)]


def home_of(k, width):
    return pl.ds(pl.multiple_of((lax.axis_index("rest") ^ k) * width, width), width)


def joined(refs):
    return jnp.concatenate([ref[...] for ref in refs], axis=1)


def others_kernel(
    cotangent_hbm, w_out_hbm, tokens_hbm, w_query_hbm, w_key_hbm, w_value_hbm,
    cotangent, tokens, w_query, w_key, w_value, grad_out, projected, *refs,
):
    *states, w_out, total, sems = refs
    places = len(states) + 1
    width = grad_out.shape[1] // (places - 1)
    count = [0]

    def bring(source, target):
        count[0] += 1
        return arrive(source, target, sems.at[count[0] - 1])

    quarter = tokens.shape[1] // 4
    parts = [pl.ds(0, quarter), pl.ds(quarter, quarter), pl.ds(2 * quarter, 2 * quarter)]
    first = []
    for lanes in parts:
        here = [bring(cotangent_hbm.at[:, lanes], cotangent.at[:, lanes])]
        for k in range(1, places):
            here.append(bring(w_out_hbm.at[home_of(k, width), lanes], w_out.at[pl.ds((k - 1) * width, width), lanes]))
        first.append(here)
    weights = w_query, w_key, w_value
    copies = [[bring(tokens_hbm, tokens), bring(w_query_hbm, w_query)]]
    stage = pl.when(lax.axis_index("rest") >= 0)
    for at, (lanes, here) in enumerate(zip(parts, first)):
        for copy in here:
            copy.wait()
        if at:
            copies.append([bring((w_key_hbm, w_value_hbm)[at - 1], weights[at])])

        @stage
        def _(at=at, lanes=lanes):
            term = mul(cotangent[:, lanes], w_out[:, lanes], LAST_LAST)
            if at == 0:
                total[...] = term
            elif at == 1:
                total[...] += term
            else:
                grad_out[...] = (total[...] + term).astype(jnp.bfloat16)

    for kind, weight in enumerate(weights):
        for copy in copies[kind]:
            copy.wait()

        @stage
        def _(kind=kind, weight=weight):
            product = mul(tokens[...], joined([weight.at[:, home_of(k, width)] for k in range(1, places)]))
            for k in range(1, places):
                kinds_of(projected, k - 1, width)[kind][...] = product[:, (k - 1) * width : k * width].astype(jnp.bfloat16)

    for k in range(1, places):
        states_of(*kinds_of(projected, k - 1, width), grad_out.at[:, pl.ds((k - 1) * width, width)], states[k - 1])


def own_kernel(cotangent, tokens, w_query, w_key, w_value, w_out_hbm, grad_out, projected, state, w_out, sems):
    width = w_out.shape[0]
    copy = arrive(w_out_hbm.at[home_of(0, width)], w_out, sems.at[0])
    weights = [weight.at[:, home_of(0, width)] for weight in (w_query, w_key, w_value)]

    @pl.when(lax.axis_index("rest") >= 0)
    def _():
        projected[...] = mul(tokens[...], joined(weights)).astype(jnp.bfloat16)

    copy.wait()
    grad_out[...] = mul(cotangent[...], w_out[...], LAST_LAST).astype(jnp.bfloat16)
    states_of(*kinds_of(projected, 0, width), grad_out, state)


def operands_of(piece, width, own, others, own_grad, others_grad):
    if piece == 0:
        return (*kinds_of(own, 0, width), own_grad)
    return (*kinds_of(others, piece - 1, width), others_grad.at[:, pl.ds((piece - 1) * width, width)])


def intra_kernel(pieces, own, others, own_grad, others_grad, _, parts):
    rows, width = parts.shape[0], parts.shape[1] // (3 * len(pieces))
    step = min(rows, 256)
    blocks = [pl.ds(at * step, step) for at in range(rows // step)]
    below = lax.broadcasted_iota(jnp.int32, (step, step), 0) >= lax.broadcasted_iota(jnp.int32, (step, step), 1)

    def score(left, right, masked):
        found = mul(left, right, LAST_LAST)
        return (jnp.where(below, found, 0.0) if masked else found).astype(jnp.bfloat16)

    for at, piece in enumerate(pieces):
        query_ref, keys_ref, values_ref, grad_out_ref = operands_of(piece, width, own, others, own_grad, others_grad)
        grad_query_ref, grad_key_ref, grad_value_ref = kinds_of(parts, at, width)
        for head in range(width // DH):
            lanes = pl.ds(head * DH, DH)
            query_t = query_ref[:, lanes].T
            grad_out_t = grad_out_ref[:, lanes].T
            key_sums, value_sums = [None] * len(blocks), [None] * len(blocks)
            for t, mine in enumerate(blocks):
                span = slice(t * step, (t + 1) * step)
                query_sum = None
                for s, theirs in enumerate(blocks[: t + 1]):
                    probe = score(grad_out_ref[mine, lanes], values_ref[theirs, lanes], s == t)
                    attend = score(query_ref[mine, lanes], keys_ref[theirs, lanes], s == t)
                    term = mul(probe, keys_ref[theirs, lanes])
                    query_sum = term if query_sum is None else query_sum + term
                    term = mul(query_t[:, span], probe)
                    key_sums[s] = term if key_sums[s] is None else key_sums[s] + term
                    term = mul(grad_out_t[:, span], attend)
                    value_sums[s] = term if value_sums[s] is None else value_sums[s] + term
                grad_query_ref[mine, lanes] = query_sum.astype(jnp.bfloat16)
            for s, theirs in enumerate(blocks):
                grad_key_ref[theirs, lanes] = key_sums[s].T.astype(jnp.bfloat16)
                grad_value_ref[theirs, lanes] = value_sums[s].T.astype(jnp.bfloat16)


def finish_kernel(factor, piece, at, last, *refs):
    if piece:
        total, *refs = refs
    parts, own, others, own_grad, others_grad, w_query, w_key, w_value, sums, *refs = refs
    width = own_grad.shape[1]
    if last:
        out_hbm, grads, out, sems = refs
    else:
        out, grads = refs
    _, keys, values, grad_out = operands_of(piece, width, own, others, own_grad, others_grad)
    for head in range(width // DH):
        lanes = pl.ds(head * DH, DH)
        prior, later = sums[0, lanes], sums[1, lanes]
        inters = (
            mul(grad_out[:, lanes], prior, LAST_LAST),
            mul(values[:, lanes], later, LAST_LAST),
            mul(keys[:, lanes], later),
        )
        for inter, part, grad in zip(inters, kinds_of(parts, at, width), kinds_of(grads, 0, width)):
            grad[:, lanes] = (factor * (inter + part[:, lanes].astype(jnp.float32))).astype(jnp.bfloat16)
    columns = home_of(piece, width)
    weights = w_query, w_key, w_value
    if not last:
        term = mul(grads[...], joined([weight.at[:, columns] for weight in weights]), LAST_LAST)
        out[...] = total[...] + term if piece else term
        return
    sent = []
    for half, rows in enumerate(halves(w_query.shape[0])):
        term = mul(grads[...], joined([weight.at[rows, columns] for weight in weights]), LAST_LAST)
        out[:, rows] = (total[:, rows] + term).astype(jnp.bfloat16)
        sent.append(arrive(out.at[:, rows], out_hbm.at[:, rows], sems.at[half]))
    for copy in sent:
        copy.wait()


def shards(tokens, cotangent, w_query, w_key, w_value, w_out):
    rows, wide = tokens.shape
    columns = w_query.shape[1]
    places = lax.axis_size("rest")
    width = columns // places
    factor = 1.0 / math.sqrt(DH * rows * lax.axis_size(AXES))

    def vmem(*shape):
        return pltpu.VMEM(shape, jnp.bfloat16)

    def cost(flops, bytes_accessed):
        return pl.CostEstimate(flops=flops, bytes_accessed=bytes_accessed, transcendentals=0)

    piece = vmem(2, width, DH)
    weight = vmem(wide, columns)
    found = pl.pallas_call(
        others_kernel,
        in_specs=[FAR] * 6,
        out_specs=[HELD] * (6 + places),
        out_shape=[
            vmem(rows, wide), vmem(rows, wide), weight, weight, weight,
            vmem(rows, columns - width), vmem(rows, 3 * (columns - width)),
        ] + [piece] * (places - 1),
        scratch_shapes=[
            vmem(columns - width, wide), pltpu.VMEM((rows, columns - width), jnp.float32),
            pltpu.SemaphoreType.DMA((3 * places + 4,)),
        ],
        compiler_params=params(16),
        cost_estimate=cost(8 * rows * wide * (columns - width), 4 * (rows + 2 * columns) * wide),
        name="project_others",
    )(*map(far, (cotangent, w_out, tokens, w_query, w_key, w_value)))
    near, (others_grad, others), pieces = found[:5], found[5:7], found[7:]
    own_grad, own, own_piece = pl.pallas_call(
        own_kernel,
        in_specs=[HELD] * 5 + [FAR],
        out_specs=[HELD] * 3,
        out_shape=[vmem(rows, width), vmem(rows, 3 * width), piece],
        scratch_shapes=[vmem(width, wide), pltpu.SemaphoreType.DMA((1,))],
        compiler_params=params(16),
        cost_estimate=cost(8 * rows * wide * width, 8 * wide * width),
        name="project_own",
    )(*map(held, near), far(w_out))
    operands = own, others, own_grad, others_grad
    turns = [(places - 1,), (1,), (0, *range(2, places - 1))]

    def intra(step, after):
        share = len(turns[step])
        views = operands if step == 2 else (others, others, others_grad, others_grad)
        return pl.pallas_call(
            functools.partial(intra_kernel, turns[step]),
            in_specs=[HELD] * 5,
            out_specs=HELD,
            out_shape=vmem(rows, 3 * width * share),
            compiler_params=params(12),
            cost_estimate=cost(10 * rows * rows * width * share, 14 * rows * width * share),
            name="intra",
        )(*map(held, (*views, after)))

    pieces, parts = exclusive_scan([own_piece, *pieces], intra)
    part_of = {piece: (step, at) for step, turn in enumerate(turns) for at, piece in enumerate(turn)}
    total = []
    for k in range(places):
        last = k == places - 1
        total = [pl.pallas_call(
            functools.partial(finish_kernel, factor, k, part_of[k][1], last),
            in_specs=[HELD] * (9 + len(total)),
            out_specs=FAR if last else HELD,
            out_shape=jax.ShapeDtypeStruct((rows, wide), jnp.bfloat16) if last else pltpu.VMEM((rows, wide), jnp.float32),
            scratch_shapes=[vmem(rows, 3 * width)] + ([vmem(rows, wide), pltpu.SemaphoreType.DMA((2,))] if last else []),
            compiler_params=params(20),
            cost_estimate=cost(6 * rows * width * (wide + DH), 6 * (rows + wide) * width),
            name="finish",
        )(*map(held, (*total, parts[part_of[k][0]], *operands, *near[2:], pieces[k])))]
    return total[0]


def solution(mesh):
    groups, places = mesh.devices.shape
    mesh = jax.sharding.Mesh(mesh.devices.reshape(groups // 2, 2, 2, places // 2), AXES)
    placed = (P(AXES, None), P(AXES, None), P(), P(), P(), P())
    return jax.shard_map(
        shards, mesh=mesh, in_specs=placed, out_specs=P(AXES, None), check_vma=False
    )
```

```python
import functools
import math

import jax
import jax.numpy as jnp
from jax import lax
from jax.experimental import pallas as pl
from jax.experimental.pallas import tpu as pltpu
from jax.sharding import PartitionSpec as P

DH = 128
AXES = ("x", "core", "half", "rest")
ROWS_ROWS = (((0,), (0,)), ((), ()))
LAST_LAST = (((1,), (1,)), ((), ()))
PLAIN = (((1,), (0,)), ((), ()))


def mul(left, right, dims=PLAIN):
    return lax.dot_general(left, right, dims, preferred_element_type=jnp.float32)


HELD = pl.BlockSpec(memory_space=pltpu.VMEM)
FAR = pl.BlockSpec(memory_space=pl.ANY)


def held(array):
    return pltpu.with_memory_space_constraint(array, pltpu.VMEM)


def far(array):
    return pltpu.with_memory_space_constraint(array, pltpu.HBM)


def params(mebibytes):
    return pltpu.CompilerParams(vmem_limit_bytes=mebibytes << 20)


def swap(pieces, axis):
    places = len(pieces)
    swapped = list(pieces)
    for k in reversed(range(1, places)):
        swapped[k] = lax.ppermute(pieces[k], axis, [(place, place ^ k) for place in range(places)])
    return swapped


def group_kernel(places, *refs):
    slices, (slices_ref, sum_ref) = refs[:places], refs[-2:]
    me = lax.axis_index("rest")
    total = None
    for k, piece in enumerate(reversed(slices)):
        slices_ref[me ^ k] = piece[...]
        term = piece[...].astype(jnp.float32)
        total = term if total is None else total + term
    sum_ref[...] = total.astype(jnp.bfloat16)


def cross_of(kind, total, sum_ref, before_ref, cross_ref):
    before_ref[...] = total.astype(jnp.bfloat16)
    added = jnp.where(lax.axis_index("half") == kind, sum_ref[kind].astype(jnp.float32), 0.0)
    cross_ref[...] = (total + added).astype(jnp.bfloat16)


def core_before(kind, other_ref):
    return jnp.where(lax.axis_index("core") != kind, other_ref[kind].astype(jnp.float32), 0.0)


def chip_kernel(split, sum_ref, other_ref, *refs):
    chip = lax.axis_index("x")
    sends = refs[:-2] if split else refs
    for k, send in enumerate(sends):
        kind = jnp.where(chip < (chip ^ (k + 1)), 0, 1)
        send[...] = (sum_ref[kind].astype(jnp.float32) + other_ref[kind].astype(jnp.float32)).astype(jnp.bfloat16)
    if split:
        cross_of(chip, core_before(chip, other_ref), sum_ref, *refs[-2:])


def half_kernel(split, chips, sum_ref, other_ref, *refs):
    chip, outs = lax.axis_index("x"), refs[-2:]
    if split:
        total = core_before(1 - chip, other_ref) + refs[0][...].astype(jnp.float32)
        cross_of(1 - chip, total, sum_ref, *outs)
        return
    for kind in range(2):
        total = core_before(kind, other_ref)
        for k in range(1, chips):
            ahead = (chip ^ k) > chip if kind else (chip ^ k) < chip
            total = total + jnp.where(ahead, refs[k - 1][...].astype(jnp.float32), 0.0)
        cross_of(kind, total, sum_ref, *[out.at[kind] for out in outs])


def scan_kernel(split, slices_ref, *refs):
    places = slices_ref.shape[0]
    pieces, out_ref = refs[-1 - places : -1], refs[-1]
    chip = lax.axis_index("x")

    def base(kind):
        if split:
            first, first_cross, second, second_cross = [ref[...].astype(jnp.float32) for ref in refs[:4]]
            return jnp.where(chip == kind, first + first_cross, second + second_cross)
        return refs[0][kind].astype(jnp.float32) + refs[1][kind].astype(jnp.float32)

    for kind in range(2):
        total = base(kind)
        for step in range(places):
            place = places - 1 - step if kind else step
            out_ref[place, kind] = total.astype(jnp.bfloat16)
            total = total + slices_ref[place, kind].astype(jnp.float32)
    me = lax.axis_index("rest")
    for k, piece in enumerate(pieces):
        piece[...] = out_ref[me ^ k]


def small_call(kernel, name, operands, outs, scratch=()):
    return pl.pallas_call(
        kernel,
        in_specs=[HELD] * len(operands),
        out_specs=[HELD] * len(outs),
        out_shape=[pltpu.VMEM(shape, jnp.bfloat16) for shape in outs],
        scratch_shapes=[pltpu.VMEM(shape, jnp.bfloat16) for shape in scratch],
        compiler_params=params(8),
        name=name,
    )(*map(held, operands))


def exclusive_scan(pieces, work):
    places, chips = len(pieces), lax.axis_size("x")
    split = chips == 2
    piece = pieces[0].shape
    part, several = piece[1:], (places,) + piece
    halves_swap = [(0, 1), (1, 0)]
    done = [work(0, pieces[1])]
    slices, total = small_call(
        functools.partial(group_kernel, places), "group", [*reversed(swap(pieces, "rest")), *done], [several, piece]
    )
    other = lax.ppermute(total, "core", halves_swap)
    found = small_call(
        functools.partial(chip_kernel, split), "chip", [total, other], [part] * (chips + 1 if split else chips - 1)
    )
    sends, first = found[: chips - 1], found[chips - 1 :]
    done.append(work(1, sends[0]))
    near = swap([None, *sends], "x")[1:]
    crossed = [first[0], lax.ppermute(first[1], "half", halves_swap)] if split else []
    before, cross = small_call(
        functools.partial(half_kernel, split, chips), "half", [total, other, *near, done[1]], [part if split else piece] * 2
    )
    done.append(work(2, before))
    crossed += [before, lax.ppermute(cross, "half", halves_swap)]
    pieces = small_call(
        functools.partial(scan_kernel, split), "scan", [slices, *crossed, done[2]], [piece] * places, [several]
    )
    return swap(pieces, "rest"), done


def arrive(source, target, sem):
    copy = pltpu.make_async_copy(source, target, sem)
    copy.start()
    return copy


def halves(extent):
    return [pl.ds(half * (extent // 2), extent // 2) for half in range(2)]


def states_of(queries, keys, values, grads, state_ref):
    width = state_ref.shape[1]
    step = min(width, 2 * DH)
    for at in range(0, width, step):
        lanes = pl.ds(at, step)
        for kind, (left, right) in enumerate(((keys, values), (queries, grads))):
            found = mul(left[:, lanes], right[:, lanes], ROWS_ROWS).astype(jnp.bfloat16)
            for head in range(0, step, DH):
                state_ref[kind, pl.ds(at + head, DH)] = found[head : head + DH, head : head + DH]


def kinds_of(ref, piece, width):
    return [ref.at[:, pl.ds((3 * piece + kind) * width, width)] for kind in range(3)]


def home_of(k, width):
    return pl.ds(pl.multiple_of((lax.axis_index("rest") ^ k) * width, width), width)


def joined(refs):
    return jnp.concatenate([ref[...] for ref in refs], axis=1)


def others_kernel(
    cotangent_hbm, w_out_hbm, tokens_hbm, w_query_hbm, w_key_hbm, w_value_hbm,
    cotangent, tokens, w_query, w_key, w_value, grad_out, projected, *refs,
):
    *states, w_out, total, sems = refs
    places = len(states) + 1
    width = grad_out.shape[1] // (places - 1)
    count = [0]

    def bring(source, target):
        count[0] += 1
        return arrive(source, target, sems.at[count[0] - 1])

    parts = halves(tokens.shape[1])
    first = []
    for lanes in parts:
        here = [bring(cotangent_hbm.at[:, lanes], cotangent.at[:, lanes])]
        for k in range(1, places):
            here.append(bring(w_out_hbm.at[home_of(k, width), lanes], w_out.at[pl.ds((k - 1) * width, width), lanes]))
        first.append(here)
    weights = w_query, w_key, w_value
    copies = [[bring(tokens_hbm, tokens), bring(w_query_hbm, w_query)]]
    stage = pl.when(lax.axis_index("rest") >= 0)
    for half, (lanes, here) in enumerate(zip(parts, first)):
        for copy in here:
            copy.wait()
        copies.append([bring((w_key_hbm, w_value_hbm)[half], weights[half + 1])])

        @stage
        def _(half=half, lanes=lanes):
            term = mul(cotangent[:, lanes], w_out[:, lanes], LAST_LAST)
            if half == 0:
                total[...] = term
            else:
                grad_out[...] = (total[...] + term).astype(jnp.bfloat16)

    for kind, weight in enumerate(weights):
        for copy in copies[kind]:
            copy.wait()

        @stage
        def _(kind=kind, weight=weight):
            product = mul(tokens[...], joined([weight.at[:, home_of(k, width)] for k in range(1, places)]))
            for k in range(1, places):
                kinds_of(projected, k - 1, width)[kind][...] = product[:, (k - 1) * width : k * width].astype(jnp.bfloat16)

    for k in range(1, places):
        states_of(*kinds_of(projected, k - 1, width), grad_out.at[:, pl.ds((k - 1) * width, width)], states[k - 1])


def own_kernel(cotangent, tokens, w_query, w_key, w_value, w_out_hbm, grad_out, projected, state, w_out, sems):
    width = w_out.shape[0]
    copy = arrive(w_out_hbm.at[home_of(0, width)], w_out, sems.at[0])
    weights = [weight.at[:, home_of(0, width)] for weight in (w_query, w_key, w_value)]

    @pl.when(lax.axis_index("rest") >= 0)
    def _():
        projected[...] = mul(tokens[...], joined(weights)).astype(jnp.bfloat16)

    copy.wait()
    grad_out[...] = mul(cotangent[...], w_out[...], LAST_LAST).astype(jnp.bfloat16)
    states_of(*kinds_of(projected, 0, width), grad_out, state)


def operands_of(piece, width, own, others, own_grad, others_grad):
    if piece == 0:
        return (*kinds_of(own, 0, width), own_grad)
    return (*kinds_of(others, piece - 1, width), others_grad.at[:, pl.ds((piece - 1) * width, width)])


def intra_kernel(pieces, own, others, own_grad, others_grad, _, parts):
    rows, width = parts.shape[0], parts.shape[1] // (3 * len(pieces))
    step = min(rows, 256)
    blocks = [pl.ds(at * step, step) for at in range(rows // step)]
    below = lax.broadcasted_iota(jnp.int32, (step, step), 0) >= lax.broadcasted_iota(jnp.int32, (step, step), 1)

    def score(left, right, masked):
        found = mul(left, right, LAST_LAST)
        return (jnp.where(below, found, 0.0) if masked else found).astype(jnp.bfloat16)

    for at, piece in enumerate(pieces):
        query_ref, keys_ref, values_ref, grad_out_ref = operands_of(piece, width, own, others, own_grad, others_grad)
        grad_query_ref, grad_key_ref, grad_value_ref = kinds_of(parts, at, width)
        for head in range(width // DH):
            lanes = pl.ds(head * DH, DH)
            query_t = query_ref[:, lanes].T
            grad_out_t = grad_out_ref[:, lanes].T
            key_sums, value_sums = [None] * len(blocks), [None] * len(blocks)
            for t, mine in enumerate(blocks):
                span = slice(t * step, (t + 1) * step)
                query_sum = None
                for s, theirs in enumerate(blocks[: t + 1]):
                    probe = score(grad_out_ref[mine, lanes], values_ref[theirs, lanes], s == t)
                    attend = score(query_ref[mine, lanes], keys_ref[theirs, lanes], s == t)
                    term = mul(probe, keys_ref[theirs, lanes])
                    query_sum = term if query_sum is None else query_sum + term
                    term = mul(query_t[:, span], probe)
                    key_sums[s] = term if key_sums[s] is None else key_sums[s] + term
                    term = mul(grad_out_t[:, span], attend)
                    value_sums[s] = term if value_sums[s] is None else value_sums[s] + term
                grad_query_ref[mine, lanes] = query_sum.astype(jnp.bfloat16)
            for s, theirs in enumerate(blocks):
                grad_key_ref[theirs, lanes] = key_sums[s].T.astype(jnp.bfloat16)
                grad_value_ref[theirs, lanes] = value_sums[s].T.astype(jnp.bfloat16)


def finish_kernel(factor, piece, at, last, *refs):
    if piece:
        total, *refs = refs
    parts, own, others, own_grad, others_grad, w_query, w_key, w_value, sums, *refs = refs
    width = own_grad.shape[1]
    if last:
        out_hbm, grads, out, sems = refs
    else:
        out, grads = refs
    _, keys, values, grad_out = operands_of(piece, width, own, others, own_grad, others_grad)
    for head in range(width // DH):
        lanes = pl.ds(head * DH, DH)
        prior, later = sums[0, lanes], sums[1, lanes]
        inters = (
            mul(grad_out[:, lanes], prior, LAST_LAST),
            mul(values[:, lanes], later, LAST_LAST),
            mul(keys[:, lanes], later),
        )
        for inter, part, grad in zip(inters, kinds_of(parts, at, width), kinds_of(grads, 0, width)):
            grad[:, lanes] = (factor * (inter + part[:, lanes].astype(jnp.float32))).astype(jnp.bfloat16)
    columns = home_of(piece, width)
    weights = w_query, w_key, w_value
    if not last:
        term = mul(grads[...], joined([weight.at[:, columns] for weight in weights]), LAST_LAST)
        out[...] = total[...] + term if piece else term
        return
    sent = []
    for half, rows in enumerate(halves(w_query.shape[0])):
        term = mul(grads[...], joined([weight.at[rows, columns] for weight in weights]), LAST_LAST)
        out[:, rows] = (total[:, rows] + term).astype(jnp.bfloat16)
        sent.append(arrive(out.at[:, rows], out_hbm.at[:, rows], sems.at[half]))
    for copy in sent:
        copy.wait()


def shards(tokens, cotangent, w_query, w_key, w_value, w_out):
    rows, wide = tokens.shape
    columns = w_query.shape[1]
    places = lax.axis_size("rest")
    width = columns // places
    factor = 1.0 / math.sqrt(DH * rows * lax.axis_size(AXES))

    def vmem(*shape):
        return pltpu.VMEM(shape, jnp.bfloat16)

    def cost(flops, bytes_accessed):
        return pl.CostEstimate(flops=flops, bytes_accessed=bytes_accessed, transcendentals=0)

    piece = vmem(2, width, DH)
    weight = vmem(wide, columns)
    found = pl.pallas_call(
        others_kernel,
        in_specs=[FAR] * 6,
        out_specs=[HELD] * (6 + places),
        out_shape=[
            vmem(rows, wide), vmem(rows, wide), weight, weight, weight,
            vmem(rows, columns - width), vmem(rows, 3 * (columns - width)),
        ] + [piece] * (places - 1),
        scratch_shapes=[
            vmem(columns - width, wide), pltpu.VMEM((rows, columns - width), jnp.float32),
            pltpu.SemaphoreType.DMA((2 * places + 4,)),
        ],
        compiler_params=params(16),
        cost_estimate=cost(8 * rows * wide * (columns - width), 4 * (rows + 2 * columns) * wide),
        name="project_others",
    )(*map(far, (cotangent, w_out, tokens, w_query, w_key, w_value)))
    near, (others_grad, others), pieces = found[:5], found[5:7], found[7:]
    own_grad, own, own_piece = pl.pallas_call(
        own_kernel,
        in_specs=[HELD] * 5 + [FAR],
        out_specs=[HELD] * 3,
        out_shape=[vmem(rows, width), vmem(rows, 3 * width), piece],
        scratch_shapes=[vmem(width, wide), pltpu.SemaphoreType.DMA((1,))],
        compiler_params=params(16),
        cost_estimate=cost(8 * rows * wide * width, 8 * wide * width),
        name="project_own",
    )(*map(held, near), far(w_out))
    operands = own, others, own_grad, others_grad
    turns = [(places - 1,), (1,), (0, *range(2, places - 1))]

    def intra(step, after):
        share = len(turns[step])
        views = operands if step == 2 else (others, others, others_grad, others_grad)
        return pl.pallas_call(
            functools.partial(intra_kernel, turns[step]),
            in_specs=[HELD] * 5,
            out_specs=HELD,
            out_shape=vmem(rows, 3 * width * share),
            compiler_params=params(12),
            cost_estimate=cost(10 * rows * rows * width * share, 14 * rows * width * share),
            name="intra",
        )(*map(held, (*views, after)))

    pieces, parts = exclusive_scan([own_piece, *pieces], intra)
    part_of = {piece: (step, at) for step, turn in enumerate(turns) for at, piece in enumerate(turn)}
    total = []
    for k in range(places):
        last = k == places - 1
        total = [pl.pallas_call(
            functools.partial(finish_kernel, factor, k, part_of[k][1], last),
            in_specs=[HELD] * (9 + len(total)),
            out_specs=FAR if last else HELD,
            out_shape=jax.ShapeDtypeStruct((rows, wide), jnp.bfloat16) if last else pltpu.VMEM((rows, wide), jnp.float32),
            scratch_shapes=[vmem(rows, 3 * width)] + ([vmem(rows, wide), pltpu.SemaphoreType.DMA((2,))] if last else []),
            compiler_params=params(20),
            cost_estimate=cost(6 * rows * width * (wide + DH), 6 * (rows + wide) * width),
            name="finish",
        )(*map(held, (*total, parts[part_of[k][0]], *operands, *near[2:], pieces[k])))]
    return total[0]


def solution(mesh):
    groups, places = mesh.devices.shape
    mesh = jax.sharding.Mesh(mesh.devices.reshape(groups // 2, 2, 2, places // 2), AXES)
    placed = (P(AXES, None), P(AXES, None), P(), P(), P(), P())
    return jax.shard_map(
        shards, mesh=mesh, in_specs=placed, out_specs=P(AXES, None), check_vma=False
    )
```
